32 devices in a mesh: grp: 2 (over y), exp: 16 (over z, x, core).
Axes of the slice: x: 2, y: 2, z: 4, core: 2. Of those that a mesh axis runs over, the one named last changes fastest.
Arguments:
- tokens: bfloat16 [4096, 1024], P(('grp', 'exp')), may hold values from -6 to 6
- w_in: bfloat16 [32, 1024, 768], P('exp', 'grp'), may hold values from -0.1875 to 0.1875
- w_out: bfloat16 [32, 384, 1024], P('exp', 'grp'), may hold values from -0.3125 to 0.3125
- moments_in: bfloat16 [32, 2, 1024, 768], P('exp', None, 'grp'), may hold values from -6 to 6
- moments_out: bfloat16 [32, 2, 384, 1024], P('exp', None, 'grp'), may hold values from -6 to 6
- expert_ids: int32 [4096, 8], P(('grp', 'exp')), may hold values from 0 to 23, all different within a row; in each aligned block of 128 rows (0 to 127, 128 to 255, ...) at most 64 rows name the same one
- route_weights: float32 [4096, 8], P(('grp', 'exp')), may hold values from 0.1 to 1
- old_plan: int32 [32], replicated, may hold values from 0 to 23, as said below
- new_plan: int32 [32], replicated, may hold values from 0 to 23, as said below
Outputs:
- mixed: bfloat16 [4096, 1024], P(('grp', 'exp'))
- new_w_in: bfloat16 [32, 1024, 768], P('exp', 'grp')
- new_w_out: bfloat16 [32, 384, 1024], P('exp', 'grp')
- new_moments_in: bfloat16 [32, 2, 1024, 768], P('exp', None, 'grp')
- new_moments_out: bfloat16 [32, 2, 384, 1024], P('exp', None, 'grp')
The draws below stay inside these ranges and needn't reach their ends.
Inputs may be any that keep to these rules, and one draw needn't show every extreme that they name: `expert_ids`: each row names 8 different experts. Among the rows of one device no expert is named more than 64 times, and in every draw some device names some expert exactly 64 times. `old_plan`: every expert is held by one or two slots; exactly 8 experts are held by two. `new_plan`: every expert is held by one or two slots; exactly 8 experts are held by two.
All inputs are finite; a program needn't handle non-finite values.
Results may differ from the reference program's by a relative error of at most 0.0057.
Values may be sent and summed in bfloat16 or wider, within the bound.
No kernel may reach another device: no remote copies, remote signals or barrier semaphores. Data moves between devices by JAX's collectives and lax.ppermute only.
A program may use at most 64 MiB of HBM per device.

```python
import math
import jax
import jax.numpy as jnp
import numpy as np
from jax import lax

D = 1024
H = 384
TOP = 8
TOK_DEV = 128
EXPERTS = 24
SLOTS = 32
CAP = 64
TOKENS = 4096
N_GRP = 2
N_EXP = 16


def plan_draw(key, first, second):
    shuffled = jax.random.permutation(jax.random.fold_in(key, first), EXPERTS).astype(jnp.int32)
    doubled = jnp.concatenate([shuffled, shuffled[:SLOTS - EXPERTS]])
    placing = jax.random.permutation(jax.random.fold_in(key, second), SLOTS)
    return doubled[placing].astype(jnp.int32)


def draw_old_plan(key, part):
    return plan_draw(key, 11, 12)


def draw_new_plan(key, part):
    return plan_draw(key, 21, 22)


def level_of(rng, shape, cuts, low, high):
    factor_of = 1.0
    for axis_at, blocks in cuts:
        heights = jax.random.uniform(jax.random.fold_in(jax.random.fold_in(rng, 6), axis_at), (blocks,), jnp.float32, low / len(cuts), high / len(cuts))
        factor_of = factor_of * jnp.repeat(jnp.exp(heights), shape[axis_at] // blocks).reshape((-1,) + (1,) * (len(shape) - 1 - axis_at))
    return factor_of


def deal_out(rng, own, number, rows, amount, top, most, skew):
    ranking = jax.random.permutation(rng, amount)
    packed, common = shares(amount, rows * top, most, skew, True), shares(amount, rows * top, most, skew, False)
    places = jnp.arange(amount)

    def named(lengths, offset_by):
        used = int((lengths > 0).sum())
        fixed = max(1, used // 4)
        moved = fixed + (places - fixed + offset_by * (used - fixed)) % max(1, amount - fixed)
        return jnp.zeros((amount,), jnp.int32).at[ranking[jnp.where(places < fixed, places, moved)]].set(jnp.asarray(lengths, jnp.int32))

    lengths = jnp.where(number % 4 == 0, named(packed, number // 4), named(common, number - number // 4 - 1))
    mixed = jax.random.permutation(jax.random.fold_in(own, 3), amount)
    donor, taker = mixed[0:amount // 2 * 2:2], mixed[1:amount // 2 * 2:2]
    room = jnp.minimum(lengths[donor] - 1, most - lengths[taker]) // 2
    room = jnp.where((donor == ranking[0]) | (taker == ranking[0]) | (lengths[taker] == 0), 0, jnp.maximum(room, 0))
    moved = jax.random.randint(jax.random.fold_in(own, 4), (amount // 2,), 0, 1 << 20) % (room + 1)
    lengths = lengths.at[donor].add(-moved).at[taker].add(moved)
    labels = jnp.searchsorted(jnp.cumsum(lengths), jnp.arange(rows * top), side="right").astype(jnp.int32)
    listing = labels.reshape(top, rows).T
    listing = listing[jax.random.permutation(jax.random.fold_in(own, 1), rows)]
    offset_by = jax.random.randint(jax.random.fold_in(own, 2), (rows, 1), 0, top)
    return jnp.take_along_axis(listing, (jnp.arange(top)[None, :] + offset_by) % top, axis=1)


def shares(count, total, most, lean, full):
    weights = [(1 << 20) // math.isqrt(standing ** lean) + 1 for standing in range(1, count + 1)]
    largest = most if full else min(most, max(-(-total // count), total * weights[0] // sum(weights)))
    least = 1 if total - largest >= count - 1 else 0
    given, surplus = [largest] + [least] * (count - 1), total - largest - least * (count - 1)
    while surplus > 0:
        candidates = [i for i in range(1, count) if given[i] < largest] or [i for i in range(1, count) if given[i] < most]
        pool, left = sum([weights[i] for i in candidates]), surplus
        for i in candidates:
            extra = min(most - given[i], max(1, left * weights[i] // pool), surplus)
            given[i] = given[i] + extra
            surplus = surplus - extra
    return np.array(given)


def normal_values(rng, extent, spread, reach, pieces=(), kind=jnp.bfloat16):
    factor_of = level_of(rng, extent, pieces, -0.22, 0.18) if pieces else 1.0
    array = jax.random.normal(rng, extent, jnp.float32) * spread * factor_of
    return jnp.minimum(jnp.maximum(array, -reach), reach).astype(kind)


def setup_inputs(seed: int = 0) -> dict:
    seeds = jax.random.split(jax.random.key(seed), 10)
    tokens = normal_values(seeds[0], (TOKENS, D), 1.0, 6.0, ((0, 32),))
    w_in = normal_values(seeds[1], (SLOTS, D, 2 * H), D ** -0.5, 0.1875, ((0, 16), (1, 2)))
    w_out = normal_values(seeds[2], (SLOTS, H, D), H ** -0.5, 0.3125, ((0, 16), (1, 2)))
    moments_in = normal_values(seeds[3], (SLOTS, 2, D, 2 * H), 1.0, 6.0, ((0, 16), (2, 2)))
    moments_out = normal_values(seeds[4], (SLOTS, 2, H, D), 1.0, 6.0, ((0, 16), (2, 2)))
    expert_ids_keys = jax.random.split(jax.random.fold_in(seeds[5], 1), TOKENS // TOK_DEV)
    expert_ids_turns = jax.random.permutation(jax.random.fold_in(seeds[5], 3), TOKENS // TOK_DEV)
    expert_ids = jax.vmap(lambda own, number: deal_out(jax.random.fold_in(seeds[5], 2), own, number, TOK_DEV, EXPERTS, TOP, CAP, 2))(expert_ids_keys, expert_ids_turns).reshape((TOKENS, TOP))
    route_weights = jnp.clip(jnp.exp(math.log(1.0) - 2.3025851 * jax.random.uniform(seeds[6], (TOKENS, TOP), jnp.float32) ** level_of(seeds[6], (TOKENS, TOP), ((0, 32),), -0.2, 0.2)), 0.1, 1.0)
    old_plan = draw_old_plan(jax.random.fold_in(seeds[9], 71), 0)
    new_plan = draw_new_plan(jax.random.fold_in(seeds[9], 71), 0)
    return dict(tokens=tokens, w_in=w_in, w_out=w_out, moments_in=moments_in, moments_out=moments_out, expert_ids=expert_ids, route_weights=route_weights, old_plan=old_plan, new_plan=new_plan)


def reference(tokens, w_in, w_out, moments_in, moments_out, expert_ids, route_weights, old_plan, new_plan):
    slot_count = old_plan.shape[0]
    slot_index = jnp.arange(slot_count, dtype=jnp.int32)
    same_expert = new_plan[:, None] == old_plan[None, :]
    source = jnp.min(jnp.where(same_expert, slot_index[None, :], slot_count), axis=1).astype(jnp.int32)
    new_w_in = w_in[source]
    new_w_out = w_out[source]
    new_moments_in = moments_in[source]
    new_moments_out = moments_out[source]
    expert_index = jnp.arange(EXPERTS, dtype=jnp.int32)
    holders = new_plan[None, :] == expert_index[:, None]
    first_slot = jnp.min(jnp.where(holders, slot_index[None, :], slot_count), axis=1).astype(jnp.int32)
    expert_in = new_w_in[first_slot]
    expert_outw = new_w_out[first_slot]
    pair_expert = expert_ids.reshape(-1)
    order = jnp.argsort(pair_expert, stable=True).astype(jnp.int32)
    counts = jax.ops.segment_sum(jnp.ones_like(pair_expert), pair_expert, EXPERTS).astype(jnp.int32)
    starts = (jnp.cumsum(counts) - counts).astype(jnp.int32)
    most = N_GRP * N_EXP * CAP
    padded = jnp.concatenate([order, jnp.zeros((most,), jnp.int32)])
    share = route_weights / jnp.sum(route_weights, axis=1, keepdims=True)
    share_flat = share.reshape(-1)
    line = jnp.arange(most, dtype=jnp.int32)

    def one_expert(total, index):
        members = lax.dynamic_slice(padded, (starts[index],), (most,))
        valid = line < counts[index]
        token_index = members // TOP
        rows = tokens[token_index]
        both = jnp.dot(rows, expert_in[index], preferred_element_type=jnp.float32)
        hidden = (jax.nn.silu(both[:, :H]) * both[:, H:]).astype(jnp.bfloat16)
        result = jnp.dot(hidden, expert_outw[index], preferred_element_type=jnp.float32).astype(jnp.bfloat16)
        weight = jnp.where(valid, share_flat[members], jnp.zeros((), share_flat.dtype))
        total = total.at[token_index].add(weight[:, None] * result.astype(jnp.float32))
        return total, None

    total, _ = lax.scan(one_expert, jnp.zeros((tokens.shape[0], D), jnp.float32), expert_index)
    return (total.astype(jnp.bfloat16), new_w_in, new_w_out, new_moments_in, new_moments_out)
```

```python
import jax
import jax.numpy as jnp
from jax import lax
from jax.experimental import pallas as pl
from jax.experimental.pallas import tpu as pltpu
from jax.sharding import PartitionSpec as P

SUB = 8
LANE = 128
PARTIAL_BYTES = 8 * 1024 * 1024


def to_tiles(x):
    slots, columns = x.shape[0], x.shape[-1]
    x = x.reshape(slots, -1, SUB, columns // LANE, LANE)
    return x.swapaxes(2, 3).reshape(slots, -1, SUB, LANE)


def from_tiles(x, shape):
    columns = shape[-1]
    x = x.reshape(shape[0], -1, columns // LANE, SUB, LANE)
    return x.swapaxes(2, 3).reshape(shape)


def reshuffle(arrays, source, devices):
    tiles = [to_tiles(a) for a in arrays]
    counts = [t.shape[1] for t in tiles]
    total = sum(counts)
    extra = -total % devices
    if extra:
        tiles.append(jnp.zeros((tiles[0].shape[0], extra, SUB, LANE), tiles[0].dtype))
    packed = jnp.concatenate(tiles, axis=1) if len(tiles) > 1 else tiles[0]
    slots = packed.shape[0]
    part = packed.shape[1] // devices
    packed = packed.reshape(slots, devices, part, SUB, LANE).swapaxes(0, 1)
    spread = lax.all_to_all(packed, "exp", split_axis=0, concat_axis=0, tiled=True)
    spread = spread.reshape(devices * slots, part, SUB, LANE)
    picked = jnp.take(spread, source, axis=0, mode="clip")
    picked = picked.reshape(devices, slots, part, SUB, LANE)
    landed = lax.all_to_all(picked, "exp", split_axis=0, concat_axis=0, tiled=True)
    landed = landed.swapaxes(0, 1).reshape(slots, devices * part, SUB, LANE)
    outs, at = [], 0
    for a, count in zip(arrays, counts):
        outs.append(from_tiles(landed[:, at : at + count], a.shape))
        at += count
    return outs


def expert_kernel(first_ref, x_ref, w_in_ref, w_out_ref, out_ref):
    slots, width, _ = w_in_ref.shape
    hidden_size = w_out_ref.shape[1]
    half = (x_ref.shape[1] - width) // 2
    x = x_ref[:, :width]
    weights = x_ref[:, width:].astype(jnp.float32)
    lane = lax.broadcasted_iota(jnp.int32, weights.shape, 1)
    total = jnp.zeros(out_ref.shape, jnp.float32)
    for j in range(slots):
        both = jnp.dot(x, w_in_ref[j], preferred_element_type=jnp.float32)
        gate, up = both[:, :hidden_size], both[:, hidden_size:]
        hidden = (gate / (1.0 + jnp.exp(-gate)) * up).astype(jnp.bfloat16)
        result = jnp.dot(hidden, w_out_ref[j], preferred_element_type=jnp.float32)
        result = result.astype(jnp.bfloat16).astype(jnp.float32)
        at = first_ref[0] + j
        mine = (lane == at) | (lane == at + half)
        weight = jnp.sum(jnp.where(mine, weights, 0.0), axis=1, keepdims=True)
        total = total + weight * result
    out_ref[...] = total.astype(out_ref.dtype)


def experts(x, w_in, w_out, first):
    rows, columns = x.shape
    slots, width, hidden2 = w_in.shape
    block = 256 if rows % 256 == 0 else rows
    return pl.pallas_call(
        expert_kernel,
        grid=(rows // block,),
        in_specs=[
            pl.BlockSpec(memory_space=pltpu.SMEM),
            pl.BlockSpec((block, columns), lambda i: (i, 0)),
            pl.BlockSpec(w_in.shape, lambda i: (0, 0, 0)),
            pl.BlockSpec(w_out.shape, lambda i: (0, 0, 0)),
        ],
        out_specs=pl.BlockSpec((block, width), lambda i: (i, 0)),
        out_shape=jax.ShapeDtypeStruct((rows, width), jnp.float32),
        compiler_params=pltpu.CompilerParams(vmem_limit_bytes=40 * 1024 * 1024),
        cost_estimate=pl.CostEstimate(
            flops=3 * rows * slots * width * hidden2,
            bytes_accessed=rows * columns * 2 + rows * width * 4 + w_in.size * 3,
            transcendentals=rows * slots * hidden2 // 2,
        ),
    )(first, x, w_in, w_out)


def on_device(
    tokens, w_in, w_out, moments_in, moments_out, expert_ids, route_weights, old_plan, new_plan
):
    devices = lax.axis_size("exp")
    per_device = w_in.shape[0]
    slot_count = per_device * devices
    slot_index = jnp.arange(slot_count, dtype=jnp.int32)

    share = route_weights / jnp.sum(route_weights, axis=1, keepdims=True)
    earlier = (old_plan[None, :] == old_plan[:, None]) & (slot_index[None, :] < slot_index[:, None])
    is_first = ~jnp.any(earlier, axis=1)
    chosen = (expert_ids[:, :, None] == old_plan[None, None, :]) & is_first[None, None, :]
    weight = jnp.sum(jnp.where(chosen, share[:, :, None], 0.0), axis=1)
    high = lax.reduce_precision(weight, exponent_bits=8, mantissa_bits=7)
    half = -(-2 * slot_count // LANE) * LANE // 2
    pad = jnp.zeros((tokens.shape[0], half - slot_count), jnp.bfloat16)
    sent = jnp.concatenate(
        [tokens, high.astype(jnp.bfloat16), pad, (weight - high).astype(jnp.bfloat16), pad], axis=1
    )
    rows = lax.all_gather(sent, "exp", axis=0, tiled=True)
    full_in = lax.all_gather(w_in, "grp", axis=1, tiled=True)
    full_out = lax.all_gather(w_out, "grp", axis=1, tiled=True)

    same_expert = new_plan[:, None] == old_plan[None, :]
    source = jnp.min(jnp.where(same_expert, slot_index[None, :], slot_count), axis=1)
    (new_moments_in,) = reshuffle((moments_in,), source, devices)
    new_w_in, new_w_out, new_moments_out = reshuffle((w_in, w_out, moments_out), source, devices)

    first = (lax.axis_index("exp") * per_device).astype(jnp.int32).reshape(1)
    held = rows.reshape(devices, -1, rows.shape[1])

    def finished(part):
        size = part.shape[1]
        partial = experts(part.reshape(devices * size, -1), full_in, full_out, first)
        return lax.psum_scatter(partial, "exp", scatter_dimension=0, tiled=True)

    parts = -(-rows.shape[0] * tokens.shape[1] * 4 // PARTIAL_BYTES)
    if parts == 1:
        mixed = finished(held)
    else:
        size = held.shape[1] // parts
        mixed = lax.map(
            lambda p: finished(lax.dynamic_slice_in_dim(held, p * size, size, axis=1)),
            jnp.arange(parts, dtype=jnp.int32),
        ).reshape(tokens.shape)
    return (mixed.astype(jnp.bfloat16), new_w_in, new_w_out, new_moments_in, new_moments_out)


def solution(mesh):
    return jax.shard_map(
        on_device,
        mesh=mesh,
        in_specs=(
            P(("grp", "exp"), None),
            P("exp", "grp", None),
            P("exp", "grp", None),
            P("exp", None, "grp", None),
            P("exp", None, "grp", None),
            P(("grp", "exp"), None),
            P(("grp", "exp"), None),
            P(),
            P(),
        ),
        out_specs=(
            P(("grp", "exp"), None),
            P("exp", "grp", None),
            P("exp", "grp", None),
            P("exp", None, "grp", None),
            P("exp", None, "grp", None),
        ),
        check_vma=False,
    )
```

```python
import functools

import jax
import jax.numpy as jnp
from jax import lax
from jax.experimental import pallas as pl
from jax.experimental.pallas import tpu as pltpu
from jax.sharding import PartitionSpec as P

SUB = 8
LANE = 128
CLASSES = (7, 8, 9, 10, 16)


def to_tiles(x):
    slots, columns = x.shape[0], x.shape[-1]
    x = x.reshape(slots, -1, SUB, columns // LANE, LANE)
    return x.swapaxes(2, 3).reshape(slots, -1, SUB, LANE)


def from_tiles(x, shape):
    columns = shape[-1]
    x = x.reshape(shape[0], -1, columns // LANE, SUB, LANE)
    return x.swapaxes(2, 3).reshape(shape)


def pack(arrays, parts):
    tiles = [to_tiles(a) for a in arrays]
    slots = tiles[0].shape[0]
    extra = -sum(t.shape[1] for t in tiles) % parts
    if extra:
        tiles.append(jnp.zeros((slots, extra, SUB, LANE), tiles[0].dtype))
    packed = jnp.concatenate(tiles, axis=1) if len(tiles) > 1 else tiles[0]
    return packed.reshape(slots, parts, -1, SUB, LANE).swapaxes(0, 1)


def unpack(landed, arrays):
    slots = landed.shape[1]
    landed = landed.swapaxes(0, 1).reshape(slots, -1, SUB, LANE)
    outs, at = [], 0
    for a in arrays:
        count = a.size // (slots * SUB * LANE)
        outs.append(from_tiles(landed[:, at : at + count], a.shape))
        at += count
    return outs


def pick_kernel(index_ref, *refs):
    *tables, out_ref, sems = refs
    count = out_ref.shape[0]
    for d in range(count):
        i = index_ref[d]
        low = 0
        for table in tables:
            size = table.shape[0]

            @pl.when((i >= low) & (i < low + size))
            def _(table=table, low=low):
                pltpu.make_async_copy(table.at[i - low], out_ref.at[d], sems.at[d]).start()

            low += size
    for d in range(count):
        pltpu.make_async_copy(tables[0].at[0], out_ref.at[d], sems.at[d]).wait()


def pick(index, *tables):
    count = index.shape[0]
    shape = (count,) + tables[0].shape[1:]
    out = jax.ShapeDtypeStruct(shape, tables[0].dtype)
    return pl.pallas_call(
        pick_kernel,
        in_specs=[pl.BlockSpec(memory_space=pltpu.SMEM)]
        + [pl.BlockSpec(memory_space=pl.ANY)] * len(tables),
        out_specs=pl.BlockSpec(memory_space=pl.ANY),
        out_shape=out,
        scratch_shapes=[pltpu.SemaphoreType.DMA((count,))],
        cost_estimate=pl.CostEstimate(
            flops=0, bytes_accessed=4 * out.size, transcendentals=0
        ),
    )(index, *tables)


def expert_kernel(first_ref, x_ref, w_in_ref, w_out_ref, out_ref):
    slots, width, _ = w_in_ref.shape
    hidden_size = w_out_ref.shape[1]
    half = (x_ref.shape[1] - width) // 2
    x = x_ref[:, :width]
    weights = x_ref[:, width:].astype(jnp.float32)
    lane = lax.broadcasted_iota(jnp.int32, weights.shape, 1)
    total = jnp.zeros(out_ref.shape, jnp.float32)
    for j in range(slots):
        both = jnp.dot(x, w_in_ref[j], preferred_element_type=jnp.float32)
        gate, up = both[:, :hidden_size], both[:, hidden_size:]
        hidden = (gate / (1.0 + jnp.exp(-gate)) * up).astype(jnp.bfloat16)
        result = jnp.dot(hidden, w_out_ref[j], preferred_element_type=jnp.float32)
        result = result.astype(jnp.bfloat16).astype(jnp.float32)
        at = first_ref[0] + j
        mine = (lane == at) | (lane == at + half)
        weight = jnp.sum(jnp.where(mine, weights, 0.0), axis=1, keepdims=True)
        total = total + weight * result
    out_ref[...] = total.astype(out_ref.dtype)


def experts(x, w_in, w_out, first, dtype):
    rows, columns = x.shape
    slots, width, hidden2 = w_in.shape
    block = 256 if rows % 256 == 0 else rows
    return pl.pallas_call(
        expert_kernel,
        grid=(rows // block,),
        in_specs=[
            pl.BlockSpec(memory_space=pltpu.SMEM),
            pl.BlockSpec((block, columns), lambda i: (i, 0)),
            pl.BlockSpec(w_in.shape, lambda i: (0, 0, 0)),
            pl.BlockSpec(w_out.shape, lambda i: (0, 0, 0)),
        ],
        out_specs=pl.BlockSpec((block, width), lambda i: (i, 0)),
        out_shape=jax.ShapeDtypeStruct((rows, width), dtype),
        compiler_params=pltpu.CompilerParams(vmem_limit_bytes=40 * 1024 * 1024),
        cost_estimate=pl.CostEstimate(
            flops=3 * rows * slots * width * hidden2,
            bytes_accessed=rows * columns * 2 + rows * width * 4 + w_in.size * 3,
            transcendentals=rows * slots * hidden2 // 2,
        ),
    )(first, x, w_in, w_out)


def flip(x, bit, devices):
    return lax.ppermute(x, "exp", [(d, d ^ bit) for d in range(devices)])


def mixture(tokens, w_in, w_out, expert_ids, share, old_plan):
    devices = lax.axis_size("exp")
    per_device = w_in.shape[0]
    slot_count = per_device * devices
    slot_index = jnp.arange(slot_count, dtype=jnp.int32)
    full_in = lax.all_gather(w_in, "grp", axis=1, tiled=True)
    full_out = lax.all_gather(w_out, "grp", axis=1, tiled=True)

    earlier = (old_plan[None, :] == old_plan[:, None]) & (slot_index[None, :] < slot_index[:, None])
    is_first = ~jnp.any(earlier, axis=1)
    chosen = (expert_ids[:, :, None] == old_plan[None, None, :]) & is_first[None, None, :]
    weight = jnp.sum(jnp.where(chosen, share[:, :, None], 0.0), axis=1)
    high = lax.reduce_precision(weight, exponent_bits=8, mantissa_bits=7)
    half = -(-2 * slot_count // LANE) * LANE // 2
    pad = jnp.zeros((tokens.shape[0], half - slot_count), jnp.bfloat16)
    rows = jnp.concatenate(
        [tokens, high.astype(jnp.bfloat16), pad, (weight - high).astype(jnp.bfloat16), pad], axis=1
    )

    bit = devices // 2
    while bit > 1:
        rows = jnp.concatenate([rows, flip(rows, bit, devices)], axis=0)
        bit //= 2
    first = (lax.axis_index("exp") * per_device).astype(jnp.int32).reshape(1)
    others = flip(rows, bit, devices)
    send = experts(others, full_in, full_out, first, jnp.bfloat16)
    total = experts(rows, full_in, full_out, first, jnp.float32)
    while True:
        total = total + flip(send, bit, devices).astype(jnp.float32)
        bit *= 2
        if bit == devices:
            return total.astype(jnp.bfloat16)
        keep = total.shape[0] // 2
        send, total = total[keep:].astype(jnp.bfloat16), total[:keep]


def reshuffle(chunks, source, cross, rank, most):
    devices = lax.axis_size("exp")
    half = devices // 2
    groups = [list(range(half)), list(range(half, devices))]
    slots = chunks[0][0].shape[0]
    held = half * slots
    mine = lax.axis_index("exp") // half
    local = jnp.arange(held, dtype=jnp.int32)
    crossing = lax.dynamic_slice_in_dim(cross, mine * held, held)
    ranking = lax.dynamic_slice_in_dim(rank, mine * held, held)
    place = jnp.arange(most, dtype=jnp.int32)
    matches = crossing[None, :] & (ranking[None, :] == place[:, None])
    sent_index = jnp.sum(jnp.where(matches, local[None, :], 0), axis=1)

    wanted = lax.dynamic_slice_in_dim(source, mine * held, held)
    here = wanted // held == mine
    far = jnp.arange(devices * slots, dtype=jnp.int32)[None, :] == wanted[:, None]
    far_rank = jnp.sum(jnp.where(far, rank[None, :], 0), axis=1)
    index = jnp.where(here, wanted - mine * held, held + far_rank)

    across = [(d, (d + half) % devices) for d in range(devices)]
    exchange = functools.partial(
        lax.all_to_all,
        axis_name="exp",
        split_axis=0,
        concat_axis=0,
        axis_index_groups=groups,
        tiled=True,
    )
    outs = []
    for arrays in chunks:
        packed = pack(arrays, half)
        spread = exchange(packed).reshape((held,) + packed.shape[2:])
        arrived = lax.ppermute(pick(sent_index, spread), "exp", across)
        picked = pick(index, spread, arrived)
        outs += unpack(exchange(picked.reshape(packed.shape)), arrays)
    return outs


def on_device(
    tokens, w_in, w_out, moments_in, moments_out, expert_ids, route_weights, old_plan, new_plan
):
    slot_count = old_plan.shape[0]
    held = slot_count // 2
    slot_index = jnp.arange(slot_count, dtype=jnp.int32)
    same_expert = new_plan[:, None] == old_plan[None, :]
    source = jnp.min(jnp.where(same_expert, slot_index[None, :], slot_count), axis=1)

    apart = slot_index[:, None] // held != slot_index[None, :] // held
    cross = jnp.any((source[:, None] == slot_index[None, :]) & apart, axis=0)
    before = (~apart) & (slot_index[:, None] < slot_index[None, :])
    rank = jnp.sum((before & cross[:, None]).astype(jnp.int32), axis=0)
    number = jnp.max(jnp.where(cross, rank + 1, 0))
    limits = sorted({-(-held * c // 16) for c in CLASSES})
    branch = sum((number > limit).astype(jnp.int32) for limit in limits[:-1])

    share = route_weights / jnp.sum(route_weights, axis=1, keepdims=True)

    def program(most):
        def run():
            mixed = mixture(tokens, w_in, w_out, expert_ids, share, old_plan)
            new_moments_in, new_w_in, new_w_out, new_moments_out = reshuffle(
                ((moments_in,), (w_in, w_out, moments_out)), source, cross, rank, most
            )
            return mixed, new_w_in, new_w_out, new_moments_in, new_moments_out

        return run

    return lax.switch(branch, [program(limit) for limit in limits])


def solution(mesh):
    return jax.shard_map(
        on_device,
        mesh=mesh,
        in_specs=(
            P(("grp", "exp"), None),
            P("exp", "grp", None),
            P("exp", "grp", None),
            P("exp", None, "grp", None),
            P("exp", None, "grp", None),
            P(("grp", "exp"), None),
            P(("grp", "exp"), None),
            P(),
            P(),
        ),
        out_specs=(
            P(("grp", "exp"), None),
            P("exp", "grp", None),
            P("exp", "grp", None),
            P("exp", None, "grp", None),
            P("exp", None, "grp", None),
        ),
        check_vma=False,
    )
```

```python
import functools

import jax
import jax.numpy as jnp
from jax import lax
from jax.experimental import pallas as pl
from jax.experimental.pallas import tpu as pltpu
from jax.sharding import PartitionSpec as P

SUB = 8
LANE = 128
CLASSES = (7, 8, 9, 10, 16)


def to_tiles(x):
    slots, columns = x.shape[0], x.shape[-1]
    x = x.reshape(slots, -1, SUB, columns // LANE, LANE)
    return x.swapaxes(2, 3).reshape(slots, -1, SUB, LANE)


def from_tiles(x, shape):
    columns = shape[-1]
    x = x.reshape(shape[0], -1, columns // LANE, SUB, LANE)
    return x.swapaxes(2, 3).reshape(shape)


def pack(arrays, parts):
    tiles = [to_tiles(a) for a in arrays]
    slots = tiles[0].shape[0]
    extra = -sum(t.shape[1] for t in tiles) % parts
    if extra:
        tiles.append(jnp.zeros((slots, extra, SUB, LANE), tiles[0].dtype))
    packed = jnp.concatenate(tiles, axis=1) if len(tiles) > 1 else tiles[0]
    return packed.reshape(slots, parts, -1, SUB, LANE).swapaxes(0, 1)


def unpack(landed, arrays):
    slots = landed.shape[1]
    landed = landed.swapaxes(0, 1).reshape(slots, -1, SUB, LANE)
    outs, at = [], 0
    for a in arrays:
        count = a.size // (slots * SUB * LANE)
        outs.append(from_tiles(landed[:, at : at + count], a.shape))
        at += count
    return outs


def expert_kernel(first_ref, x_ref, w_in_ref, w_out_ref, *refs):
    *add_refs, out_ref = refs
    slots, width, _ = w_in_ref.shape
    hidden_size = w_out_ref.shape[1]
    half = (x_ref.shape[1] - width) // 2
    x = x_ref[:, :width]
    weights = x_ref[:, width:].astype(jnp.float32)
    lane = lax.broadcasted_iota(jnp.int32, weights.shape, 1)
    total = jnp.zeros(out_ref.shape, jnp.float32)
    for add_ref in add_refs:
        total = total + add_ref[...].astype(jnp.float32)
    for j in range(slots):
        both = jnp.dot(x, w_in_ref[j], preferred_element_type=jnp.float32)
        gate, up = both[:, :hidden_size], both[:, hidden_size:]
        hidden = (gate / (1.0 + jnp.exp(-gate)) * up).astype(jnp.bfloat16)
        result = jnp.dot(hidden, w_out_ref[j], preferred_element_type=jnp.float32)
        result = result.astype(jnp.bfloat16).astype(jnp.float32)
        at = first_ref[0] + j
        mine = (lane == at) | (lane == at + half)
        weight = jnp.sum(jnp.where(mine, weights, 0.0), axis=1, keepdims=True)
        total = total + weight * result
    out_ref[...] = total.astype(out_ref.dtype)


def experts(x, w_in, w_out, first, dtype, low, high, add=None):
    columns = x.shape[1]
    slots, width, hidden2 = w_in.shape
    rows = high - low
    block = 256 if rows % 256 == 0 and low % 256 == 0 else rows
    at = low // block
    added = [] if add is None else [add]
    return pl.pallas_call(
        expert_kernel,
        grid=(rows // block,),
        in_specs=[
            pl.BlockSpec(memory_space=pltpu.SMEM),
            pl.BlockSpec((block, columns), lambda i: (i + at, 0)),
            pl.BlockSpec(w_in.shape, lambda i: (0, 0, 0)),
            pl.BlockSpec(w_out.shape, lambda i: (0, 0, 0)),
        ]
        + [pl.BlockSpec((block, width), lambda i: (i + at, 0))] * len(added),
        out_specs=pl.BlockSpec((block, width), lambda i: (i, 0)),
        out_shape=jax.ShapeDtypeStruct((rows, width), dtype),
        compiler_params=pltpu.CompilerParams(vmem_limit_bytes=40 * 1024 * 1024),
        cost_estimate=pl.CostEstimate(
            flops=3 * rows * slots * width * hidden2,
            bytes_accessed=rows * columns * 2 + rows * width * 4 + w_in.size * 3,
            transcendentals=rows * slots * hidden2 // 2,
        ),
    )(first, x, w_in, w_out, *added)


def flip(x, bit, devices):
    return lax.ppermute(x, "exp", [(d, d ^ bit) for d in range(devices)])


def mixture(tokens, w_in, w_out, expert_ids, share, old_plan):
    devices = lax.axis_size("exp")
    per_device = w_in.shape[0]
    slot_count = per_device * devices
    slot_index = jnp.arange(slot_count, dtype=jnp.int32)
    full_in = lax.all_gather(w_in, "grp", axis=1, tiled=True)
    full_out = lax.all_gather(w_out, "grp", axis=1, tiled=True)

    earlier = (old_plan[None, :] == old_plan[:, None]) & (slot_index[None, :] < slot_index[:, None])
    is_first = ~jnp.any(earlier, axis=1)
    chosen = (expert_ids[:, :, None] == old_plan[None, None, :]) & is_first[None, None, :]
    weight = jnp.sum(jnp.where(chosen, share[:, :, None], 0.0), axis=1)
    high = lax.reduce_precision(weight, exponent_bits=8, mantissa_bits=7)
    half = -(-2 * slot_count // LANE) * LANE // 2
    pad = jnp.zeros((tokens.shape[0], half - slot_count), jnp.bfloat16)
    rows = jnp.concatenate(
        [tokens, high.astype(jnp.bfloat16), pad, (weight - high).astype(jnp.bfloat16), pad], axis=1
    )

    first = (lax.axis_index("exp") * per_device).astype(jnp.int32).reshape(1)
    bit = devices // 2
    while bit > 1:
        rows = jnp.concatenate([rows, flip(rows, bit, devices)], axis=0)
        bit //= 2
        if bit == 2:
            rows = yield rows
    others = flip(rows, bit, devices)
    rows, others = yield rows, others
    apply = functools.partial(experts, w_in=full_in, w_out=full_out, first=first)
    count = rows.shape[0]
    got = flip(apply(others, dtype=jnp.bfloat16, low=0, high=count), bit, devices)
    send = apply(rows, dtype=jnp.bfloat16, low=count // 2, high=count, add=got)
    total = apply(rows, dtype=jnp.float32, low=0, high=count // 2, add=got)
    while True:
        bit *= 2
        total = total + flip(send, bit, devices).astype(jnp.float32)
        if bit == devices // 2:
            yield total.astype(jnp.bfloat16)
        if bit == 2:
            total = yield total
        keep = total.shape[0] // 2
        send, total = total[keep:].astype(jnp.bfloat16), total[:keep]


def reshuffle(chunks, source, cross, rank, most, other):
    devices = lax.axis_size("exp")
    half = devices // 2
    groups = [list(range(half)), list(range(half, devices))]
    slots = chunks[0][0].shape[0]
    held = half * slots
    mine = lax.axis_index("exp") // half
    local = jnp.arange(held, dtype=jnp.int32)
    crossing = lax.dynamic_slice_in_dim(cross, mine * held, held)
    ranking = lax.dynamic_slice_in_dim(rank, mine * held, held)
    place = jnp.arange(most, dtype=jnp.int32)
    matches = crossing[None, :] & (ranking[None, :] == place[:, None])
    sent_index = jnp.sum(jnp.where(matches, local[None, :], 0), axis=1)

    wanted = lax.dynamic_slice_in_dim(source, mine * held, held)
    here = wanted // held == mine
    far = jnp.arange(devices * slots, dtype=jnp.int32)[None, :] == wanted[:, None]
    far_rank = jnp.sum(jnp.where(far, rank[None, :], 0), axis=1)
    index = jnp.where(here, wanted - mine * held, held + far_rank)

    across = [(d, (d + half) % devices) for d in range(devices)]
    exchange = functools.partial(
        lax.all_to_all,
        axis_name="exp",
        split_axis=0,
        concat_axis=0,
        axis_index_groups=groups,
        tiled=True,
    )
    spread = []
    for arrays in chunks:
        packed = pack(arrays, half)
        spread.append(exchange(packed).reshape((held,) + packed.shape[2:]))
    arrived = []
    sent = [jnp.take(s, sent_index, axis=0, mode="clip") for s in spread]
    point = next(other)
    sent[0], point = lax.optimization_barrier((sent[0], point))
    point = other.send(point)
    arrived = [lax.ppermute(s, "exp", across) for s in sent]
    arrived[0], point = lax.optimization_barrier((arrived[0], point))
    point = other.send(point)
    outs = []
    for number, (arrays, s, a) in enumerate(zip(chunks, spread, arrived)):
        picked = jnp.take(jnp.concatenate([s, a], axis=0), index, axis=0, mode="clip")
        picked = picked.reshape((half, slots) + picked.shape[1:])
        if number == len(chunks) - 1:
            picked, point = lax.optimization_barrier((picked, point))
            point = other.send(point)
        outs += unpack(exchange(picked), arrays)
    return [point] + outs


def on_device(
    tokens, w_in, w_out, moments_in, moments_out, expert_ids, route_weights, old_plan, new_plan
):
    slot_count = old_plan.shape[0]
    held = slot_count // 2
    slot_index = jnp.arange(slot_count, dtype=jnp.int32)
    same_expert = new_plan[:, None] == old_plan[None, :]
    source = jnp.min(jnp.where(same_expert, slot_index[None, :], slot_count), axis=1)

    apart = slot_index[:, None] // held != slot_index[None, :] // held
    cross = jnp.any((source[:, None] == slot_index[None, :]) & apart, axis=0)
    before = (~apart) & (slot_index[:, None] < slot_index[None, :])
    rank = jnp.sum((before & cross[:, None]).astype(jnp.int32), axis=0)
    number = jnp.max(jnp.where(cross, rank + 1, 0))
    limits = sorted({-(-held * c // 16) for c in CLASSES})
    branch = sum((number > limit).astype(jnp.int32) for limit in limits[:-1])

    share = route_weights / jnp.sum(route_weights, axis=1, keepdims=True)

    def program(most):
        def run():
            other = mixture(tokens, w_in, w_out, expert_ids, share, old_plan)
            mixed, new_moments_in, new_w_in, new_w_out, new_moments_out = reshuffle(
                ((moments_in,), (w_in, w_out, moments_out)), source, cross, rank, most, other
            )
            return mixed, new_w_in, new_w_out, new_moments_in, new_moments_out

        return run

    return lax.switch(branch, [program(limit) for limit in limits])


def solution(mesh):
    return jax.shard_map(
        on_device,
        mesh=mesh,
        in_specs=(
            P(("grp", "exp"), None),
            P("exp", "grp", None),
            P("exp", "grp", None),
            P("exp", None, "grp", None),
            P("exp", None, "grp", None),
            P(("grp", "exp"), None),
            P(("grp", "exp"), None),
            P(),
            P(),
        ),
        out_specs=(
            P(("grp", "exp"), None),
            P("exp", "grp", None),
            P("exp", "grp", None),
            P("exp", None, "grp", None),
            P("exp", None, "grp", None),
        ),
        check_vma=False,
    )
```

```python
import functools

import jax
import jax.numpy as jnp
from jax import lax
from jax.experimental import pallas as pl
from jax.experimental.pallas import tpu as pltpu
from jax.sharding import PartitionSpec as P

SUB = 8
LANE = 128
CLASSES = (7, 8, 9, 10, 16)


def to_tiles(x):
    slots, columns = x.shape[0], x.shape[-1]
    x = x.reshape(slots, -1, SUB, columns // LANE, LANE)
    return x.swapaxes(2, 3).reshape(slots, -1, SUB, LANE)


def from_tiles(x, shape):
    columns = shape[-1]
    x = x.reshape(shape[0], -1, columns // LANE, SUB, LANE)
    return x.swapaxes(2, 3).reshape(shape)


def pack(arrays, parts):
    tiles = [to_tiles(a) for a in arrays]
    slots = tiles[0].shape[0]
    extra = -sum(t.shape[1] for t in tiles) % parts
    if extra:
        tiles.append(jnp.zeros((slots, extra, SUB, LANE), tiles[0].dtype))
    packed = jnp.concatenate(tiles, axis=1) if len(tiles) > 1 else tiles[0]
    return packed.reshape(slots, parts, -1, SUB, LANE).swapaxes(0, 1)


def unpack(landed, arrays):
    slots = landed.shape[1]
    landed = landed.swapaxes(0, 1).reshape(slots, -1, SUB, LANE)
    outs, at = [], 0
    for a in arrays:
        count = a.size // (slots * SUB * LANE)
        outs.append(from_tiles(landed[:, at : at + count], a.shape))
        at += count
    return outs


def expert_kernel(first_ref, x_ref, w_in_ref, w_out_ref, *refs):
    *add_refs, out_ref = refs
    slots, width, _ = w_in_ref.shape
    hidden_size = w_out_ref.shape[1]
    half = (x_ref.shape[1] - width) // 2
    x = x_ref[:, :width]
    weights = x_ref[:, width:].astype(jnp.float32)
    lane = lax.broadcasted_iota(jnp.int32, weights.shape, 1)
    total = jnp.zeros(out_ref.shape, jnp.float32)
    for add_ref in add_refs:
        total = total + add_ref[...].astype(jnp.float32)
    for j in range(slots):
        both = jnp.dot(x, w_in_ref[j], preferred_element_type=jnp.float32)
        gate, up = both[:, :hidden_size], both[:, hidden_size:]
        hidden = (gate / (1.0 + jnp.exp(-gate)) * up).astype(jnp.bfloat16)
        result = jnp.dot(hidden, w_out_ref[j], preferred_element_type=jnp.float32)
        result = result.astype(jnp.bfloat16).astype(jnp.float32)
        at = first_ref[0] + j
        mine = (lane == at) | (lane == at + half)
        weight = jnp.sum(jnp.where(mine, weights, 0.0), axis=1, keepdims=True)
        total = total + weight * result
    out_ref[...] = total.astype(out_ref.dtype)


def experts(x, w_in, w_out, first, dtype, low, high, add=None):
    columns = x.shape[1]
    slots, width, hidden2 = w_in.shape
    rows = high - low
    block = 256 if rows % 256 == 0 and low % 256 == 0 else rows
    at = low // block
    added = [] if add is None else [add]
    return pl.pallas_call(
        expert_kernel,
        grid=(rows // block,),
        in_specs=[
            pl.BlockSpec(memory_space=pltpu.SMEM),
            pl.BlockSpec((block, columns), lambda i: (i + at, 0)),
            pl.BlockSpec(w_in.shape, lambda i: (0, 0, 0)),
            pl.BlockSpec(w_out.shape, lambda i: (0, 0, 0)),
        ]
        + [pl.BlockSpec((block, width), lambda i: (i + at, 0))] * len(added),
        out_specs=pl.BlockSpec((block, width), lambda i: (i, 0)),
        out_shape=jax.ShapeDtypeStruct((rows, width), dtype),
        compiler_params=pltpu.CompilerParams(vmem_limit_bytes=40 * 1024 * 1024),
        cost_estimate=pl.CostEstimate(flops=0, bytes_accessed=0, transcendentals=0),
    )(first, x, w_in, w_out, *added)


def flip(x, bit, devices):
    return lax.ppermute(x, "exp", [(d, d ^ bit) for d in range(devices)])


def weighted_rows(tokens, expert_ids, route_weights, old_plan):
    slot_count = old_plan.shape[0]
    slot_index = jnp.arange(slot_count, dtype=jnp.int32)
    share = route_weights / jnp.sum(route_weights, axis=1, keepdims=True)
    earlier = (old_plan[None, :] == old_plan[:, None]) & (slot_index[None, :] < slot_index[:, None])
    is_first = ~jnp.any(earlier, axis=1)
    chosen = (expert_ids[:, :, None] == old_plan[None, None, :]) & is_first[None, None, :]
    weight = jnp.sum(jnp.where(chosen, share[:, :, None], 0.0), axis=1)
    high = lax.reduce_precision(weight, exponent_bits=8, mantissa_bits=7)
    half = -(-2 * slot_count // LANE) * LANE // 2
    pad = jnp.zeros((tokens.shape[0], half - slot_count), jnp.bfloat16)
    return jnp.concatenate(
        [tokens, high.astype(jnp.bfloat16), pad, (weight - high).astype(jnp.bfloat16), pad], axis=1
    )


def crossing(old_plan, new_plan):
    slot_count = old_plan.shape[0]
    held = slot_count // 2
    slot_index = jnp.arange(slot_count, dtype=jnp.int32)
    same_expert = new_plan[:, None] == old_plan[None, :]
    source = jnp.min(jnp.where(same_expert, slot_index[None, :], slot_count), axis=1)
    apart = slot_index[:, None] // held != slot_index[None, :] // held
    cross = jnp.any((source[:, None] == slot_index[None, :]) & apart, axis=0)
    before = (~apart) & (slot_index[:, None] < slot_index[None, :])
    rank = jnp.sum((before & cross[:, None]).astype(jnp.int32), axis=0)
    number = jnp.max(jnp.where(cross, rank + 1, 0))
    return source, cross, rank, number


def exchange(x, devices):
    half = devices // 2
    groups = [list(range(half)), list(range(half, devices))]
    return lax.all_to_all(
        x, "exp", split_axis=0, concat_axis=0, axis_index_groups=groups, tiled=True
    )


def middle(most, spread, packed, rows, full_in, w_out, plan):
    devices = lax.axis_size("exp")
    half = devices // 2
    slots = packed.shape[1]
    held = half * slots
    source, cross, rank = plan
    full_out = lax.all_gather(w_out, "grp", axis=1, tiled=True)
    mine = lax.axis_index("exp") // half
    local = jnp.arange(held, dtype=jnp.int32)
    leaving = lax.dynamic_slice_in_dim(cross, mine * held, held)
    ranking = lax.dynamic_slice_in_dim(rank, mine * held, held)
    place = jnp.arange(most, dtype=jnp.int32)
    matches = leaving[None, :] & (ranking[None, :] == place[:, None])
    sent_index = jnp.sum(jnp.where(matches, local[None, :], 0), axis=1)
    wanted = lax.dynamic_slice_in_dim(source, mine * held, held)
    here = wanted // held == mine
    far = jnp.arange(devices * slots, dtype=jnp.int32)[None, :] == wanted[:, None]
    far_rank = jnp.sum(jnp.where(far, rank[None, :], 0), axis=1)
    index = jnp.where(here, wanted - mine * held, held + far_rank)
    across = [(d, (d + half) % devices) for d in range(devices)]

    def cross_over(x):
        sent = jnp.take(x, sent_index, axis=0, mode="clip")
        table = jnp.pad(x, [(0, most)] + [(0, 0)] * (x.ndim - 1))
        return sent, table

    def picked(table, arrived):
        table = lax.dynamic_update_slice_in_dim(table, arrived, held, axis=0)
        out = jnp.take(table, index, axis=0, mode="clip")
        return out.reshape((half, slots) + out.shape[1:])

    sent_a, table_a = cross_over(spread)
    sent_a, packed = lax.optimization_barrier((sent_a, packed))
    arrived_a = lax.ppermute(sent_a, "exp", across)
    spread_b = exchange(packed, devices).reshape((held,) + packed.shape[2:])
    sent_b, table_b = cross_over(spread_b)

    bit = half // 2
    while bit > 1:
        rows = jnp.concatenate([rows, flip(rows, bit, devices)], axis=0)
        bit //= 2
    others = flip(rows, bit, devices)

    arrived_b = lax.ppermute(sent_b, "exp", across)
    arrived_a, table_a, table_b = lax.optimization_barrier((arrived_a, table_a, table_b))
    picked_a = picked(table_a, arrived_a)
    picked_a, rows, others, _ = lax.optimization_barrier((picked_a, rows, others, sent_b))
    landed_a = exchange(picked_a, devices)

    first = (lax.axis_index("exp") * slots).astype(jnp.int32).reshape(1)
    apply = functools.partial(experts, w_in=full_in, w_out=full_out, first=first)
    count = rows.shape[0]
    got = flip(apply(others, dtype=jnp.bfloat16, low=0, high=count), bit, devices)
    send = apply(rows, dtype=jnp.bfloat16, low=count // 2, high=count, add=got)
    total = apply(rows, dtype=jnp.float32, low=0, high=count // 2, add=got)
    bit *= 2
    while bit < half:
        total = total + flip(send, bit, devices).astype(jnp.float32)
        keep = total.shape[0] // 2
        send, total = total[keep:].astype(jnp.bfloat16), total[:keep]
        bit *= 2
    arrived_b, send, total = lax.optimization_barrier((arrived_b, send, total))
    return landed_a, picked(table_b, arrived_b), send, total


def on_device(
    tokens, w_in, w_out, moments_in, moments_out, expert_ids, route_weights, old_plan, new_plan
):
    devices = lax.axis_size("exp")
    half = devices // 2
    held = old_plan.shape[0] // 2
    chunk_a, chunk_b = (w_in, w_out, moments_out), (moments_in,)
    full_in = lax.all_gather(w_in, "grp", axis=1, tiled=True)
    rows = weighted_rows(tokens, expert_ids, route_weights, old_plan)
    packed_a, packed_b = pack(chunk_a, half), pack(chunk_b, half)
    packed_a, rows = lax.optimization_barrier((packed_a, rows))
    rows = jnp.concatenate([rows, flip(rows, half, devices)], axis=0)
    spread = exchange(packed_a, devices).reshape((held,) + packed_a.shape[2:])

    *plan, number = crossing(old_plan, new_plan)
    limits = sorted({-(-held * c // 16) for c in CLASSES})
    branch = sum((number > limit).astype(jnp.int32) for limit in limits[:-1])
    landed_a, picked_b, send, total = lax.switch(
        branch,
        [functools.partial(middle, limit) for limit in limits],
        spread,
        packed_b,
        rows,
        full_in,
        w_out,
        tuple(plan),
    )
    new_w_in, new_w_out, new_moments_out = unpack(landed_a, chunk_a)
    (new_moments_in,) = unpack(exchange(picked_b, devices), chunk_b)
    mixed = (total + flip(send, half, devices).astype(jnp.float32)).astype(jnp.bfloat16)
    return mixed, new_w_in, new_w_out, new_moments_in, new_moments_out


def solution(mesh):
    return jax.shard_map(
        on_device,
        mesh=mesh,
        in_specs=(
            P(("grp", "exp"), None),
            P("exp", "grp", None),
            P("exp", "grp", None),
            P("exp", None, "grp", None),
            P("exp", None, "grp", None),
            P(("grp", "exp"), None),
            P(("grp", "exp"), None),
            P(),
            P(),
        ),
        out_specs=(
            P(("grp", "exp"), None),
            P("exp", "grp", None),
            P("exp", "grp", None),
            P("exp", None, "grp", None),
            P("exp", None, "grp", None),
        ),
        check_vma=False,
    )
```

```python
import functools

import jax
import jax.numpy as jnp
from jax import lax
from jax.experimental import pallas as pl
from jax.experimental.pallas import tpu as pltpu
from jax.sharding import PartitionSpec as P

SUB = 8
LANE = 128
CLASSES = (7, 8, 9, 10, 16)


def to_tiles(x):
    slots, columns = x.shape[0], x.shape[-1]
    x = x.reshape(slots, -1, SUB, columns // LANE, LANE)
    return x.swapaxes(2, 3).reshape(slots, -1, SUB, LANE)


def from_tiles(x, shape):
    columns = shape[-1]
    x = x.reshape(shape[0], -1, columns // LANE, SUB, LANE)
    return x.swapaxes(2, 3).reshape(shape)


def pack(arrays, parts, after=None):
    tiles = [to_tiles(a) for a in arrays]
    slots = tiles[0].shape[0]
    extra = -sum(t.shape[1] for t in tiles) % parts
    if extra:
        tiles.append(jnp.zeros((slots, extra, SUB, LANE), tiles[0].dtype))
    packed = jnp.concatenate(tiles, axis=1) if len(tiles) > 1 else tiles[0]
    if after is not None:
        packed, after = lax.optimization_barrier((packed, after))
    return packed.reshape(slots, parts, -1, SUB, LANE).swapaxes(0, 1), after


def unpack(landed, arrays):
    slots = landed.shape[1]
    landed = landed.swapaxes(0, 1).reshape(slots, -1, SUB, LANE)
    outs, at = [], 0
    for a in arrays:
        count = a.size // (slots * SUB * LANE)
        outs.append(from_tiles(landed[:, at : at + count], a.shape))
        at += count
    return outs


def expert_kernel(first_ref, x_ref, w_in_ref, w_out_ref, out_ref):
    slots, width, _ = w_in_ref.shape
    hidden_size = w_out_ref.shape[1]
    half = (x_ref.shape[1] - width) // 2
    x = x_ref[:, :width]
    weights = x_ref[:, width:].astype(jnp.float32)
    lane = lax.broadcasted_iota(jnp.int32, weights.shape, 1)
    total = jnp.zeros(out_ref.shape, jnp.float32)
    for j in range(slots):
        both = jnp.dot(x, w_in_ref[j], preferred_element_type=jnp.float32)
        gate, up = both[:, :hidden_size], both[:, hidden_size:]
        hidden = (gate / (1.0 + jnp.exp(-gate)) * up).astype(jnp.bfloat16)
        result = jnp.dot(hidden, w_out_ref[j], preferred_element_type=jnp.float32)
        result = result.astype(jnp.bfloat16).astype(jnp.float32)
        at = first_ref[0] + j
        mine = (lane == at) | (lane == at + half)
        weight = jnp.sum(jnp.where(mine, weights, 0.0), axis=1, keepdims=True)
        total = total + weight * result
    out_ref[...] = total.astype(out_ref.dtype)


def experts(x, w_in, w_out, first):
    rows, columns = x.shape
    _, width, _ = w_in.shape
    block = 256 if rows % 256 == 0 else rows
    return pl.pallas_call(
        expert_kernel,
        grid=(rows // block,),
        in_specs=[
            pl.BlockSpec(memory_space=pltpu.SMEM),
            pl.BlockSpec((block, columns), lambda i: (i, 0)),
            pl.BlockSpec(w_in.shape, lambda i: (0, 0, 0)),
            pl.BlockSpec(w_out.shape, lambda i: (0, 0, 0)),
        ],
        out_specs=pl.BlockSpec((block, width), lambda i: (i, 0)),
        out_shape=jax.ShapeDtypeStruct((rows, width), jnp.bfloat16),
        compiler_params=pltpu.CompilerParams(vmem_limit_bytes=40 * 1024 * 1024),
        cost_estimate=pl.CostEstimate(flops=0, bytes_accessed=0, transcendentals=0),
    )(first, x, w_in, w_out)


def planes(devices):
    inner = 1
    while 4 * inner * inner <= devices:
        inner *= 2
    outer = devices // inner
    across = [[p * inner + q for p in range(outer)] for q in range(inner)]
    inside = [[p * inner + q for q in range(inner)] for p in range(outer)]
    return across, inside


def swap(x, axis, groups=None):
    return lax.all_to_all(
        x, axis, split_axis=0, concat_axis=0, axis_index_groups=groups, tiled=True
    )


def spread_out(x, count):
    return jnp.broadcast_to(x[None], (count,) + x.shape)


def add_up(x):
    return jnp.sum(x.astype(jnp.float32), axis=0).astype(jnp.bfloat16)


def weighted_rows(tokens, expert_ids, route_weights, old_plan):
    slot_count = old_plan.shape[0]
    slot_index = jnp.arange(slot_count, dtype=jnp.int32)
    share = route_weights / jnp.sum(route_weights, axis=1, keepdims=True)
    earlier = (old_plan[None, :] == old_plan[:, None]) & (slot_index[None, :] < slot_index[:, None])
    is_first = ~jnp.any(earlier, axis=1)
    chosen = (expert_ids[:, :, None] == old_plan[None, None, :]) & is_first[None, None, :]
    weight = jnp.sum(jnp.where(chosen, share[:, :, None], 0.0), axis=1)
    high = lax.reduce_precision(weight, exponent_bits=8, mantissa_bits=7)
    half = -(-2 * slot_count // LANE) * LANE // 2
    pad = jnp.zeros((tokens.shape[0], half - slot_count), jnp.bfloat16)
    return jnp.concatenate(
        [tokens, high.astype(jnp.bfloat16), pad, (weight - high).astype(jnp.bfloat16), pad], axis=1
    )


def crossing(old_plan, new_plan):
    slot_count = old_plan.shape[0]
    held = slot_count // 2
    slot_index = jnp.arange(slot_count, dtype=jnp.int32)
    same_expert = new_plan[:, None] == old_plan[None, :]
    source = jnp.min(jnp.where(same_expert, slot_index[None, :], slot_count), axis=1)
    apart = slot_index[:, None] // held != slot_index[None, :] // held
    cross = jnp.any((source[:, None] == slot_index[None, :]) & apart, axis=0)
    before = (~apart) & (slot_index[:, None] < slot_index[None, :])
    rank = jnp.sum((before & cross[:, None]).astype(jnp.int32), axis=0)
    number = jnp.max(jnp.where(cross, rank + 1, 0))
    return source, cross, rank, number


def exchange(x, devices):
    half = devices // 2
    return swap(x, "exp", [list(range(half)), list(range(half, devices))])


def middle(most, spread, packed, rows, full_in, full_out, plan):
    devices = lax.axis_size("exp")
    half = devices // 2
    slots = packed.shape[1]
    held = half * slots
    source, cross, rank = plan
    mine = lax.axis_index("exp") // half
    local = jnp.arange(held, dtype=jnp.int32)
    leaving = lax.dynamic_slice_in_dim(cross, mine * held, held)
    ranking = lax.dynamic_slice_in_dim(rank, mine * held, held)
    place = jnp.arange(most, dtype=jnp.int32)
    matches = leaving[None, :] & (ranking[None, :] == place[:, None])
    sent_index = jnp.sum(jnp.where(matches, local[None, :], 0), axis=1)
    wanted = lax.dynamic_slice_in_dim(source, mine * held, held)
    here = wanted // held == mine
    far = jnp.arange(devices * slots, dtype=jnp.int32)[None, :] == wanted[:, None]
    far_rank = jnp.sum(jnp.where(far, rank[None, :], 0), axis=1)
    index = jnp.where(here, wanted - mine * held, held + far_rank)
    across = [(d, (d + half) % devices) for d in range(devices)]

    def cross_over(x):
        sent = jnp.take(x, sent_index, axis=0, mode="clip")
        table = jnp.pad(x, [(0, most)] + [(0, 0)] * (x.ndim - 1))
        return sent, table

    def picked(table, arrived):
        table = lax.dynamic_update_slice_in_dim(table, arrived, held, axis=0)
        out = jnp.take(table, index, axis=0, mode="clip")
        return out.reshape((half, slots) + out.shape[1:])

    sent_a, table_a = cross_over(spread)
    sent_a, packed = lax.optimization_barrier((sent_a, packed))
    arrived_a = lax.ppermute(sent_a, "exp", across)
    spread_b = exchange(packed, devices).reshape((held,) + packed.shape[2:])
    sent_b, table_b = cross_over(spread_b)

    _, inside = planes(devices)
    rows = swap(spread_out(rows, len(inside[0])), "exp", inside)
    arrived_b = lax.ppermute(sent_b, "exp", across)
    arrived_a, table_a, table_b = lax.optimization_barrier((arrived_a, table_a, table_b))
    picked_a = picked(table_a, arrived_a)
    picked_a, rows, _ = lax.optimization_barrier((picked_a, rows, sent_b))
    landed_a = exchange(picked_a, devices)

    first = (lax.axis_index("exp") * slots).astype(jnp.int32).reshape(1)
    partial = experts(rows.reshape(-1, rows.shape[-1]), full_in, full_out, first)
    partial = add_up(swap(partial.reshape(rows.shape[:-1] + (-1,)), "exp", inside))
    arrived_b, partial = lax.optimization_barrier((arrived_b, partial))
    return landed_a, picked(table_b, arrived_b), partial


def on_device(
    tokens, w_in, w_out, moments_in, moments_out, expert_ids, route_weights, old_plan, new_plan
):
    devices = lax.axis_size("exp")
    half = devices // 2
    held = old_plan.shape[0] // 2
    chunk_a, chunk_b = (w_in, w_out, moments_out), (moments_in,)
    full_in = lax.all_gather(w_in, "grp", axis=1, tiled=True)
    rows = weighted_rows(tokens, expert_ids, route_weights, old_plan)
    over, _ = planes(devices)
    packed_a, copies = pack(chunk_a, half, after=spread_out(rows, len(over[0])))
    rows = swap(copies, "exp", over)
    full_out = jnp.concatenate(list(swap(spread_out(w_out, lax.axis_size("grp")), "grp")), axis=1)
    packed_b, _ = pack(chunk_b, half)
    spread = exchange(packed_a, devices).reshape((held,) + packed_a.shape[2:])

    *plan, number = crossing(old_plan, new_plan)
    limits = sorted({-(-held * c // 16) for c in CLASSES})
    branch = sum((number > limit).astype(jnp.int32) for limit in limits[:-1])
    landed_a, picked_b, partial = lax.switch(
        branch,
        [functools.partial(middle, limit) for limit in limits],
        spread,
        packed_b,
        rows,
        full_in,
        full_out,
        tuple(plan),
    )
    new_w_in, new_w_out, new_moments_out = unpack(landed_a, chunk_a)
    (new_moments_in,) = unpack(exchange(picked_b, devices), chunk_b)
    mixed = add_up(swap(partial, "exp", over))
    return mixed, new_w_in, new_w_out, new_moments_in, new_moments_out


def solution(mesh):
    return jax.shard_map(
        on_device,
        mesh=mesh,
        in_specs=(
            P(("grp", "exp"), None),
            P("exp", "grp", None),
            P("exp", "grp", None),
            P("exp", None, "grp", None),
            P("exp", None, "grp", None),
            P(("grp", "exp"), None),
            P(("grp", "exp"), None),
            P(),
            P(),
        ),
        out_specs=(
            P(("grp", "exp"), None),
            P("exp", "grp", None),
            P("exp", "grp", None),
            P("exp", None, "grp", None),
            P("exp", None, "grp", None),
        ),
        check_vma=False,
    )
```

```python
import functools

import jax
import jax.numpy as jnp
from jax import lax
from jax.experimental import pallas as pl
from jax.experimental.pallas import tpu as pltpu
from jax.sharding import PartitionSpec as P

SUB = 8
LANE = 128
CLASSES = (7, 8, 9, 10, 16)


def to_tiles(x):
    slots, columns = x.shape[0], x.shape[-1]
    x = x.reshape(slots, -1, SUB, columns // LANE, LANE)
    return x.swapaxes(2, 3).reshape(slots, -1, SUB, LANE)


def from_tiles(x, shape):
    columns = shape[-1]
    x = x.reshape(shape[0], -1, columns // LANE, SUB, LANE)
    return x.swapaxes(2, 3).reshape(shape)


def pack(arrays, parts, after=None):
    tiles = [to_tiles(a) for a in arrays]
    slots = tiles[0].shape[0]
    extra = -sum(t.shape[1] for t in tiles) % parts
    if extra:
        tiles.append(jnp.zeros((slots, extra, SUB, LANE), tiles[0].dtype))
    packed = jnp.concatenate(tiles, axis=1) if len(tiles) > 1 else tiles[0]
    if after is not None:
        packed, after = lax.optimization_barrier((packed, after))
    return packed.reshape(slots, parts, -1, SUB, LANE).swapaxes(0, 1), after


def unpack(landed, arrays):
    slots = landed.shape[1]
    landed = landed.swapaxes(0, 1).reshape(slots, -1, SUB, LANE)
    outs, at = [], 0
    for a in arrays:
        count = a.size // (slots * SUB * LANE)
        outs.append(from_tiles(landed[:, at : at + count], a.shape))
        at += count
    return outs


def expert_kernel(first_ref, x_ref, w_in_ref, w_out_ref, out_ref):
    slots, width, _ = w_in_ref.shape
    hidden_size = w_out_ref.shape[1]
    half = (x_ref.shape[1] - width) // 2
    x = x_ref[:, :width]
    weights = x_ref[:, width:].astype(jnp.float32)
    lane = lax.broadcasted_iota(jnp.int32, weights.shape, 1)
    total = jnp.zeros(out_ref.shape, jnp.float32)
    for j in range(slots):
        both = jnp.dot(x, w_in_ref[j], preferred_element_type=jnp.float32)
        gate, up = both[:, :hidden_size], both[:, hidden_size:]
        hidden = (gate / (1.0 + jnp.exp(-gate)) * up).astype(jnp.bfloat16)
        result = jnp.dot(hidden, w_out_ref[j], preferred_element_type=jnp.float32)
        result = result.astype(jnp.bfloat16).astype(jnp.float32)
        at = first_ref[0] + j
        mine = (lane == at) | (lane == at + half)
        weight = jnp.sum(jnp.where(mine, weights, 0.0), axis=1, keepdims=True)
        total = total + weight * result
    out_ref[...] = total.astype(out_ref.dtype)


def experts(x, w_in, w_out, first):
    rows, columns = x.shape
    _, width, _ = w_in.shape
    block = 256 if rows % 256 == 0 else rows
    return pl.pallas_call(
        expert_kernel,
        grid=(rows // block,),
        in_specs=[
            pl.BlockSpec(memory_space=pltpu.SMEM),
            pl.BlockSpec((block, columns), lambda i: (i, 0)),
            pl.BlockSpec(w_in.shape, lambda i: (0, 0, 0)),
            pl.BlockSpec(w_out.shape, lambda i: (0, 0, 0)),
        ],
        out_specs=pl.BlockSpec((block, width), lambda i: (i, 0)),
        out_shape=jax.ShapeDtypeStruct((rows, width), jnp.bfloat16),
        compiler_params=pltpu.CompilerParams(vmem_limit_bytes=40 * 1024 * 1024),
        cost_estimate=pl.CostEstimate(flops=0, bytes_accessed=0, transcendentals=0),
    )(first, x, w_in, w_out)


def plane_size(devices):
    size = 1
    while 4 * size * size <= devices:
        size *= 2
    return size


def swap(x, axis, groups=None):
    return lax.all_to_all(
        x, axis, split_axis=0, concat_axis=0, axis_index_groups=groups, tiled=True
    )


def flip(x, axis, bits):
    if bits == 0:
        return x
    return lax.ppermute(x, axis, [(d, d ^ bits) for d in range(lax.axis_size(axis))])


def gather_in_order(x, axis):
    count = lax.axis_size(axis)
    blocks = jnp.stack([flip(x, axis, i) for i in range(count)])
    order = lax.axis_index(axis) ^ jnp.arange(count, dtype=jnp.int32)
    return jnp.take(blocks, order, axis=0, mode="clip")


def add_up(blocks):
    return sum(x.astype(jnp.float32) for x in blocks).astype(jnp.bfloat16)


def weighted_rows(tokens, expert_ids, route_weights, old_plan):
    slot_count = old_plan.shape[0]
    slot_index = jnp.arange(slot_count, dtype=jnp.int32)
    share = route_weights / jnp.sum(route_weights, axis=1, keepdims=True)
    earlier = (old_plan[None, :] == old_plan[:, None]) & (slot_index[None, :] < slot_index[:, None])
    is_first = ~jnp.any(earlier, axis=1)
    chosen = (expert_ids[:, :, None] == old_plan[None, None, :]) & is_first[None, None, :]
    weight = jnp.sum(jnp.where(chosen, share[:, :, None], 0.0), axis=1)
    high = lax.reduce_precision(weight, exponent_bits=8, mantissa_bits=7)
    half = -(-2 * slot_count // LANE) * LANE // 2
    pad = jnp.zeros((tokens.shape[0], half - slot_count), jnp.bfloat16)
    return jnp.concatenate(
        [tokens, high.astype(jnp.bfloat16), pad, (weight - high).astype(jnp.bfloat16), pad], axis=1
    )


def crossing(old_plan, new_plan):
    slot_count = old_plan.shape[0]
    held = slot_count // 2
    slot_index = jnp.arange(slot_count, dtype=jnp.int32)
    same_expert = new_plan[:, None] == old_plan[None, :]
    source = jnp.min(jnp.where(same_expert, slot_index[None, :], slot_count), axis=1)
    apart = slot_index[:, None] // held != slot_index[None, :] // held
    cross = jnp.any((source[:, None] == slot_index[None, :]) & apart, axis=0)
    before = (~apart) & (slot_index[:, None] < slot_index[None, :])
    rank = jnp.sum((before & cross[:, None]).astype(jnp.int32), axis=0)
    number = jnp.max(jnp.where(cross, rank + 1, 0))
    return source, cross, rank, number


def exchange(x, devices):
    half = devices // 2
    return swap(x, "exp", [list(range(half)), list(range(half, devices))])


def middle(most, spread, packed, rows, full_in, full_out, plan):
    devices = lax.axis_size("exp")
    half = devices // 2
    slots = packed.shape[1]
    held = half * slots
    source, cross, rank = plan
    mine = lax.axis_index("exp") // half
    local = jnp.arange(held, dtype=jnp.int32)
    leaving = lax.dynamic_slice_in_dim(cross, mine * held, held)
    ranking = lax.dynamic_slice_in_dim(rank, mine * held, held)
    place = jnp.arange(most, dtype=jnp.int32)
    matches = leaving[None, :] & (ranking[None, :] == place[:, None])
    sent_index = jnp.sum(jnp.where(matches, local[None, :], 0), axis=1)
    wanted = lax.dynamic_slice_in_dim(source, mine * held, held)
    here = wanted // held == mine
    far = jnp.arange(devices * slots, dtype=jnp.int32)[None, :] == wanted[:, None]
    far_rank = jnp.sum(jnp.where(far, rank[None, :], 0), axis=1)
    index = jnp.where(here, wanted - mine * held, held + far_rank)
    across = [(d, (d + half) % devices) for d in range(devices)]

    def cross_over(x):
        sent = jnp.take(x, sent_index, axis=0, mode="clip")
        table = jnp.pad(x, [(0, most)] + [(0, 0)] * (x.ndim - 1))
        return sent, table

    def picked(table, arrived):
        table = lax.dynamic_update_slice_in_dim(table, arrived, held, axis=0)
        out = jnp.take(table, index, axis=0, mode="clip")
        return out.reshape((half, slots) + out.shape[1:])

    sent_a, table_a = cross_over(spread)
    sent_a, packed = lax.optimization_barrier((sent_a, packed))
    arrived_a = lax.ppermute(sent_a, "exp", across)
    spread_b = exchange(packed, devices).reshape((held,) + packed.shape[2:])
    sent_b, table_b = cross_over(spread_b)

    inner = plane_size(devices)
    blocks = [flip(rows, "exp", i) for i in range(inner)]
    first = (lax.axis_index("exp") * slots).astype(jnp.int32).reshape(1)
    parts = [experts(x, full_in, full_out, first) for x in blocks]
    arrived_a, table_a, table_b, sent_b, parts = lax.optimization_barrier(
        (arrived_a, table_a, table_b, sent_b, parts)
    )
    arrived_b = lax.ppermute(sent_b, "exp", across)
    landed_a = exchange(picked(table_a, arrived_a), devices)
    partial = add_up([flip(x, "exp", i) for i, x in enumerate(parts)])
    arrived_b, partial = lax.optimization_barrier((arrived_b, partial))
    return landed_a, picked(table_b, arrived_b), partial


def on_device(
    tokens, w_in, w_out, moments_in, moments_out, expert_ids, route_weights, old_plan, new_plan
):
    devices = lax.axis_size("exp")
    half = devices // 2
    held = old_plan.shape[0] // 2
    chunk_a, chunk_b = (w_in, w_out, moments_out), (moments_in,)
    full_in = lax.all_gather(w_in, "grp", axis=1, tiled=True)
    rows = weighted_rows(tokens, expert_ids, route_weights, old_plan)
    packed_a, rows = pack(chunk_a, half, after=rows)
    inner = plane_size(devices)
    outer = range(0, devices, inner)
    rows = jnp.concatenate([flip(rows, "exp", i) for i in outer], axis=0)
    full_out = gather_in_order(w_out, "grp").swapaxes(0, 1).reshape(w_out.shape[0], -1, w_out.shape[2])
    packed_b, _ = pack(chunk_b, half)
    spread = exchange(packed_a, devices).reshape((held,) + packed_a.shape[2:])

    *plan, number = crossing(old_plan, new_plan)
    limits = sorted({-(-held * c // 16) for c in CLASSES})
    branch = sum((number > limit).astype(jnp.int32) for limit in limits[:-1])
    landed_a, picked_b, partial = lax.switch(
        branch,
        [functools.partial(middle, limit) for limit in limits],
        spread,
        packed_b,
        rows,
        full_in,
        full_out,
        tuple(plan),
    )
    new_w_in, new_w_out, new_moments_out = unpack(landed_a, chunk_a)
    (new_moments_in,) = unpack(exchange(picked_b, devices), chunk_b)
    size = tokens.shape[0]
    mixed = add_up([flip(partial[n * size : (n + 1) * size], "exp", i) for n, i in enumerate(outer)])
    return mixed, new_w_in, new_w_out, new_moments_in, new_moments_out


def solution(mesh):
    return jax.shard_map(
        on_device,
        mesh=mesh,
        in_specs=(
            P(("grp", "exp"), None),
            P("exp", "grp", None),
            P("exp", "grp", None),
            P("exp", None, "grp", None),
            P("exp", None, "grp", None),
            P(("grp", "exp"), None),
            P(("grp", "exp"), None),
            P(),
            P(),
        ),
        out_specs=(
            P(("grp", "exp"), None),
            P("exp", "grp", None),
            P("exp", "grp", None),
            P("exp", None, "grp", None),
            P("exp", None, "grp", None),
        ),
        check_vma=False,
    )
```

```python
import jax
import jax.numpy as jnp
from jax import lax
from jax.experimental import pallas as pl
from jax.experimental.pallas import tpu as pltpu
from jax.sharding import PartitionSpec as P

SUB = 8
LANE = 128
FIXED = 9


def to_tiles(x):
    slots, columns = x.shape[0], x.shape[-1]
    x = x.reshape(slots, -1, SUB, columns // LANE, LANE)
    return x.swapaxes(2, 3).reshape(slots, -1, SUB, LANE)


def from_tiles(x, shape):
    columns = shape[-1]
    x = x.reshape(shape[0], -1, columns // LANE, SUB, LANE)
    return x.swapaxes(2, 3).reshape(shape)


def pack(arrays, parts, after=None):
    tiles = [to_tiles(a) for a in arrays]
    slots = tiles[0].shape[0]
    extra = -sum(t.shape[1] for t in tiles) % parts
    if extra:
        tiles.append(jnp.zeros((slots, extra, SUB, LANE), tiles[0].dtype))
    packed = jnp.concatenate(tiles, axis=1) if len(tiles) > 1 else tiles[0]
    if after is not None:
        packed, after = lax.optimization_barrier((packed, after))
    return packed.reshape(slots, parts, -1, SUB, LANE).swapaxes(0, 1), after


def unpack(landed, arrays):
    slots = landed.shape[1]
    landed = landed.swapaxes(0, 1).reshape(slots, -1, SUB, LANE)
    outs, at = [], 0
    for a in arrays:
        count = a.size // (slots * SUB * LANE)
        outs.append(from_tiles(landed[:, at : at + count], a.shape))
        at += count
    return outs


def expert_kernel(first_ref, x_ref, *refs):
    *weight_refs, out_ref = refs
    width = out_ref.shape[1]
    half = (x_ref.shape[1] - width) // 2
    x = x_ref[:, :width]
    weights = x_ref[:, width:].astype(jnp.float32)
    lane = lax.broadcasted_iota(jnp.int32, weights.shape, 1)
    total = jnp.zeros(out_ref.shape, jnp.float32)
    for n in range(len(weight_refs) // 2):
        w_in_ref, w_out_ref = weight_refs[2 * n : 2 * n + 2]
        hidden_size = w_out_ref.shape[1]
        for j in range(w_in_ref.shape[0]):
            both = jnp.dot(x, w_in_ref[j], preferred_element_type=jnp.float32)
            gate, up = both[:, :hidden_size], both[:, hidden_size:]
            hidden = (gate / (1.0 + jnp.exp(-gate)) * up).astype(jnp.bfloat16)
            result = jnp.dot(hidden, w_out_ref[j], preferred_element_type=jnp.float32)
            result = result.astype(jnp.bfloat16).astype(jnp.float32)
            at = first_ref[n] + j
            mine = (lane == at) | (lane == at + half)
            weight = jnp.sum(jnp.where(mine, weights, 0.0), axis=1, keepdims=True)
            total = total + weight * result
    out_ref[...] = total.astype(out_ref.dtype)


def experts(x, first, weights):
    rows, columns = x.shape
    width = weights[0].shape[1]
    block = 256 if rows % 256 == 0 else rows
    return pl.pallas_call(
        expert_kernel,
        grid=(rows // block,),
        in_specs=[
            pl.BlockSpec(memory_space=pltpu.SMEM),
            pl.BlockSpec((block, columns), lambda i: (i, 0)),
        ]
        + [pl.BlockSpec(w.shape, lambda i: (0, 0, 0)) for w in weights],
        out_specs=pl.BlockSpec((block, width), lambda i: (i, 0)),
        out_shape=jax.ShapeDtypeStruct((rows, width), jnp.bfloat16),
        compiler_params=pltpu.CompilerParams(vmem_limit_bytes=40 * 1024 * 1024),
        cost_estimate=pl.CostEstimate(flops=0, bytes_accessed=0, transcendentals=0),
    )(first, x, *weights)


def plane_size(devices):
    size = 1
    while 4 * size * size <= devices:
        size *= 2
    return size


def swap(x, axis, groups=None):
    return lax.all_to_all(
        x, axis, split_axis=0, concat_axis=0, axis_index_groups=groups, tiled=True
    )


def flip(x, axis, bits):
    if bits == 0:
        return x
    return lax.ppermute(x, axis, [(d, d ^ bits) for d in range(lax.axis_size(axis))])


def add_up(blocks):
    return sum(x.astype(jnp.float32) for x in blocks).astype(jnp.bfloat16)


def weighted_rows(tokens, expert_ids, route_weights, old_plan):
    slot_count = old_plan.shape[0]
    slot_index = jnp.arange(slot_count, dtype=jnp.int32)
    share = route_weights / jnp.sum(route_weights, axis=1, keepdims=True)
    earlier = (old_plan[None, :] == old_plan[:, None]) & (slot_index[None, :] < slot_index[:, None])
    is_first = ~jnp.any(earlier, axis=1)
    chosen = (expert_ids[:, :, None] == old_plan[None, None, :]) & is_first[None, None, :]
    weight = jnp.sum(jnp.where(chosen, share[:, :, None], 0.0), axis=1)
    high = lax.reduce_precision(weight, exponent_bits=8, mantissa_bits=7)
    half = -(-2 * slot_count // LANE) * LANE // 2
    pad = jnp.zeros((tokens.shape[0], half - slot_count), jnp.bfloat16)
    return jnp.concatenate(
        [tokens, high.astype(jnp.bfloat16), pad, (weight - high).astype(jnp.bfloat16), pad], axis=1
    )


def crossing(old_plan, new_plan):
    slot_count = old_plan.shape[0]
    held = slot_count // 2
    slot_index = jnp.arange(slot_count, dtype=jnp.int32)
    same_expert = new_plan[:, None] == old_plan[None, :]
    source = jnp.min(jnp.where(same_expert, slot_index[None, :], slot_count), axis=1)
    apart = slot_index[:, None] // held != slot_index[None, :] // held
    cross = jnp.any((source[:, None] == slot_index[None, :]) & apart, axis=0)
    before = (~apart) & (slot_index[:, None] < slot_index[None, :])
    rank = jnp.sum((before & cross[:, None]).astype(jnp.int32), axis=0)
    number = jnp.max(jnp.where(cross, rank + 1, 0))
    return source, cross, rank, number


def exchange(x, devices):
    half = devices // 2
    return swap(x, "exp", [list(range(half)), list(range(half, devices))])


def places(plan, held, most):
    source, cross, rank = plan
    mine = lax.axis_index("exp") * 2 // lax.axis_size("exp")
    local = jnp.arange(held, dtype=jnp.int32)
    leaving = lax.dynamic_slice_in_dim(cross, mine * held, held)
    ranking = lax.dynamic_slice_in_dim(rank, mine * held, held)
    place = jnp.arange(most, dtype=jnp.int32)
    matches = leaving[None, :] & (ranking[None, :] == place[:, None])
    sent_index = jnp.sum(jnp.where(matches, local[None, :], 0), axis=1)
    wanted = lax.dynamic_slice_in_dim(source, mine * held, held)
    here = wanted // held == mine
    far = jnp.arange(source.shape[0], dtype=jnp.int32)[None, :] == wanted[:, None]
    far_rank = jnp.sum(jnp.where(far, rank[None, :], 0), axis=1)
    return sent_index, jnp.where(here, wanted - mine * held, held + far_rank)


def on_device(
    tokens, w_in, w_out, moments_in, moments_out, expert_ids, route_weights, old_plan, new_plan
):
    devices = lax.axis_size("exp")
    half = devices // 2
    slots = w_in.shape[0]
    held = half * slots
    chunk_a, chunk_b = (w_in, w_out, moments_out), (moments_in,)
    full_in = lax.all_gather(w_in, "grp", axis=1, tiled=True)
    full_out = lax.all_gather(w_out, "grp", axis=1, tiled=True)

    rows = weighted_rows(tokens, expert_ids, route_weights, old_plan)
    packed_a, rows = pack(chunk_a, half, after=rows)
    inner = plane_size(devices)
    outer = range(0, devices, inner)
    spread_a = exchange(packed_a, devices).reshape((held,) + packed_a.shape[2:])
    rows = jnp.concatenate([flip(rows, "exp", i) for i in outer], axis=0)

    *plan, number = crossing(old_plan, new_plan)
    most = -(-held * FIXED // 16)
    sent_index, index = places(plan, held, held)
    across = [(d, (d + half) % devices) for d in range(devices)]

    def cross_over(x):
        sent = jnp.take(x, sent_index[:most], axis=0, mode="clip")
        return sent, jnp.pad(x, [(0, held)] + [(0, 0)] * (x.ndim - 1))

    def picked(table, arrived):
        table = lax.dynamic_update_slice_in_dim(table, arrived, held, axis=0)
        out = jnp.take(table, index, axis=0, mode="clip")
        return out.reshape((half, slots) + out.shape[1:])

    packed_b, _ = pack(chunk_b, half)
    sent_a, table_a = cross_over(spread_a)
    sent_a, packed_b, rows = lax.optimization_barrier((sent_a, packed_b, rows))
    arrived_a = lax.ppermute(sent_a, "exp", across)
    spread_b = exchange(packed_b, devices).reshape((held,) + packed_b.shape[2:])
    sent_b, table_b = cross_over(spread_b)
    steps = range(0, inner, 2)
    blocks = [flip(rows, "exp", i) for i in steps]
    weights = [full_in, full_out, flip(full_in, "exp", 1), flip(full_out, "exp", 1)]
    me = lax.axis_index("exp").astype(jnp.int32)
    first = jnp.stack([me, me ^ 1]) * slots
    blocks[1:], sent_b, table_b, table_a = lax.optimization_barrier(
        (blocks[1:], sent_b, table_b, table_a)
    )
    parts = [experts(x, first, weights) for x in blocks]

    def more(state):
        place, *tables = state
        at = lax.dynamic_index_in_dim(sent_index, place, keepdims=False)
        out = []
        for spread, table in zip((spread_a, spread_b), tables):
            row = lax.dynamic_slice_in_dim(spread, at, 1, axis=0)
            row = lax.ppermute(row, "exp", across)
            out.append(lax.dynamic_update_slice_in_dim(table, row, held + place, axis=0))
        return place + 1, *out

    arrived_a, table_a, table_b, sent_b, parts = lax.optimization_barrier(
        (arrived_a, table_a, table_b, sent_b, parts)
    )
    _, table_a, table_b = lax.while_loop(
        lambda state: state[0] < number, more, (jnp.int32(most), table_a, table_b)
    )

    arrived_b = lax.ppermute(sent_b, "exp", across)
    landed_a = exchange(picked(table_a, arrived_a), devices)
    partial = add_up([flip(x, "exp", i) for i, x in zip(steps, parts)])
    arrived_b, partial = lax.optimization_barrier((arrived_b, partial))

    (new_moments_in,) = unpack(exchange(picked(table_b, arrived_b), devices), chunk_b)
    new_w_in, new_w_out, new_moments_out = unpack(landed_a, chunk_a)
    size = tokens.shape[0]
    mixed = add_up([flip(partial[n * size : (n + 1) * size], "exp", i) for n, i in enumerate(outer)])
    return mixed, new_w_in, new_w_out, new_moments_in, new_moments_out


def solution(mesh):
    return jax.shard_map(
        on_device,
        mesh=mesh,
        in_specs=(
            P(("grp", "exp"), None),
            P("exp", "grp", None),
            P("exp", "grp", None),
            P("exp", None, "grp", None),
            P("exp", None, "grp", None),
            P(("grp", "exp"), None),
            P(("grp", "exp"), None),
            P(),
            P(),
        ),
        out_specs=(
            P(("grp", "exp"), None),
            P("exp", "grp", None),
            P("exp", "grp", None),
            P("exp", None, "grp", None),
            P("exp", None, "grp", None),
        ),
        check_vma=False,
    )
```

```python
import jax
import jax.numpy as jnp
from jax import lax
from jax.experimental import pallas as pl
from jax.experimental.pallas import tpu as pltpu
from jax.sharding import PartitionSpec as P

SUB = 8
LANE = 128
FIXED = 9


def to_tiles(x):
    slots, columns = x.shape[0], x.shape[-1]
    x = x.reshape(slots, -1, SUB, columns // LANE, LANE)
    return x.swapaxes(2, 3).reshape(slots, -1, SUB, LANE)


def from_tiles(x, shape):
    columns = shape[-1]
    x = x.reshape(shape[0], -1, columns // LANE, SUB, LANE)
    return x.swapaxes(2, 3).reshape(shape)


def in_parts(tiles, parts):
    return tiles.reshape(tiles.shape[0], parts, -1, SUB, LANE).swapaxes(0, 1)


def pack(arrays, parts):
    tiles = [to_tiles(a) for a in arrays]
    if all(t.shape[1] % parts == 0 for t in tiles):
        return jnp.concatenate([in_parts(t, parts) for t in tiles], axis=2)
    slots = tiles[0].shape[0]
    extra = -sum(t.shape[1] for t in tiles) % parts
    tiles.append(jnp.zeros((slots, extra, SUB, LANE), tiles[0].dtype))
    return in_parts(jnp.concatenate(tiles, axis=1), parts)


def unpack(landed, arrays):
    parts, slots = landed.shape[:2]
    counts = [a.size // (slots * SUB * LANE) for a in arrays]
    whole = all(count % parts == 0 for count in counts)
    if not whole:
        landed = landed.swapaxes(0, 1).reshape(slots, -1, SUB, LANE)
    outs, at = [], 0
    for a, count in zip(arrays, counts):
        if whole:
            part = landed[:, :, at // parts : (at + count) // parts].swapaxes(0, 1)
            outs.append(from_tiles(part.reshape(slots, count, SUB, LANE), a.shape))
        else:
            outs.append(from_tiles(landed[:, at : at + count], a.shape))
        at += count
    return outs


def pick_kernel(index_ref, *refs):
    *tables, out_ref, rows, in_sems, out_sems = refs
    count = out_ref.shape[0]
    for d in range(count):
        i = index_ref[d]
        low = 0
        for table in tables:
            size = table.shape[0]

            @pl.when((i >= low) & (i < low + size))
            def _(table=table, low=low):
                pltpu.make_async_copy(table.at[i - low], rows.at[d], in_sems.at[d]).start()

            low += size
    for d in range(count):
        pltpu.make_async_copy(tables[0].at[0], rows.at[d], in_sems.at[d]).wait()
        pltpu.make_async_copy(rows.at[d], out_ref.at[d], out_sems.at[d]).start()
    for d in range(count):
        pltpu.make_async_copy(rows.at[d], out_ref.at[d], out_sems.at[d]).wait()


def pick(index, *tables):
    count = index.shape[0]
    shape = (count,) + tables[0].shape[1:]
    return pl.pallas_call(
        pick_kernel,
        in_specs=[pl.BlockSpec(memory_space=pltpu.SMEM)]
        + [pl.BlockSpec(memory_space=pl.ANY)] * len(tables),
        out_specs=pl.BlockSpec(memory_space=pl.ANY),
        out_shape=jax.ShapeDtypeStruct(shape, tables[0].dtype),
        scratch_shapes=[
            pltpu.VMEM(shape, tables[0].dtype),
            pltpu.SemaphoreType.DMA((count,)),
            pltpu.SemaphoreType.DMA((count,)),
        ],
        compiler_params=pltpu.CompilerParams(vmem_limit_bytes=16 * 1024 * 1024),
        cost_estimate=pl.CostEstimate(flops=0, bytes_accessed=0, transcendentals=0),
    )(index, *tables)


def expert_kernel(first_ref, x_ref, *refs):
    *weight_refs, out_ref = refs
    width = out_ref.shape[1]
    half = (x_ref.shape[1] - width) // 2
    x = x_ref[:, :width]
    weights = x_ref[:, width:].astype(jnp.float32)
    lane = lax.broadcasted_iota(jnp.int32, weights.shape, 1)
    total = jnp.zeros(out_ref.shape, jnp.float32)
    for n in range(len(weight_refs) // 2):
        w_in_ref, w_out_ref = weight_refs[2 * n : 2 * n + 2]
        hidden_size = w_out_ref.shape[1]
        for j in range(w_in_ref.shape[0]):
            both = jnp.dot(x, w_in_ref[j], preferred_element_type=jnp.float32)
            gate, up = both[:, :hidden_size], both[:, hidden_size:]
            hidden = (gate / (1.0 + jnp.exp(-gate)) * up).astype(jnp.bfloat16)
            result = jnp.dot(hidden, w_out_ref[j], preferred_element_type=jnp.float32)
            result = result.astype(jnp.bfloat16).astype(jnp.float32)
            at = first_ref[n] + j
            mine = (lane == at) | (lane == at + half)
            weight = jnp.sum(jnp.where(mine, weights, 0.0), axis=1, keepdims=True)
            total = total + weight * result
    out_ref[...] = total.astype(out_ref.dtype)


def experts(x, first, weights):
    rows, columns = x.shape
    width = weights[0].shape[1]
    block = 256 if rows % 256 == 0 else rows
    return pl.pallas_call(
        expert_kernel,
        grid=(rows // block,),
        in_specs=[
            pl.BlockSpec(memory_space=pltpu.SMEM),
            pl.BlockSpec((block, columns), lambda i: (i, 0)),
        ]
        + [pl.BlockSpec(w.shape, lambda i: (0, 0, 0)) for w in weights],
        out_specs=pl.BlockSpec((block, width), lambda i: (i, 0)),
        out_shape=jax.ShapeDtypeStruct((rows, width), jnp.bfloat16),
        compiler_params=pltpu.CompilerParams(vmem_limit_bytes=40 * 1024 * 1024),
        cost_estimate=pl.CostEstimate(flops=0, bytes_accessed=0, transcendentals=0),
    )(first, x, *weights)


def plane_size(devices):
    size = 1
    while 4 * size * size <= devices:
        size *= 2
    return size


def swap(x, axis, groups=None):
    return lax.all_to_all(
        x, axis, split_axis=0, concat_axis=0, axis_index_groups=groups, tiled=True
    )


def flip(x, axis, bits):
    if bits == 0:
        return x
    return lax.ppermute(x, axis, [(d, d ^ bits) for d in range(lax.axis_size(axis))])


def add_up(blocks):
    return sum(x.astype(jnp.float32) for x in blocks).astype(jnp.bfloat16)


def weighted_rows(tokens, expert_ids, route_weights, old_plan):
    slot_count = old_plan.shape[0]
    slot_index = jnp.arange(slot_count, dtype=jnp.int32)
    share = route_weights / jnp.sum(route_weights, axis=1, keepdims=True)
    earlier = (old_plan[None, :] == old_plan[:, None]) & (slot_index[None, :] < slot_index[:, None])
    is_first = ~jnp.any(earlier, axis=1)
    chosen = (expert_ids[:, :, None] == old_plan[None, None, :]) & is_first[None, None, :]
    weight = jnp.sum(jnp.where(chosen, share[:, :, None], 0.0), axis=1)
    high = lax.reduce_precision(weight, exponent_bits=8, mantissa_bits=7)
    half = -(-2 * slot_count // LANE) * LANE // 2
    pad = jnp.zeros((tokens.shape[0], half - slot_count), jnp.bfloat16)
    return jnp.concatenate(
        [tokens, high.astype(jnp.bfloat16), pad, (weight - high).astype(jnp.bfloat16), pad], axis=1
    )


def crossing(old_plan, new_plan):
    slot_count = old_plan.shape[0]
    held = slot_count // 2
    slot_index = jnp.arange(slot_count, dtype=jnp.int32)
    same_expert = new_plan[:, None] == old_plan[None, :]
    source = jnp.min(jnp.where(same_expert, slot_index[None, :], slot_count), axis=1)
    apart = slot_index[:, None] // held != slot_index[None, :] // held
    cross = jnp.any((source[:, None] == slot_index[None, :]) & apart, axis=0)
    before = (~apart) & (slot_index[:, None] < slot_index[None, :])
    rank = jnp.sum((before & cross[:, None]).astype(jnp.int32), axis=0)
    number = jnp.max(jnp.where(cross, rank + 1, 0))
    return source, cross, rank, number


def exchange(x, devices):
    half = devices // 2
    return swap(x, "exp", [list(range(half)), list(range(half, devices))])


def places(plan, held, most):
    source, cross, rank = plan
    mine = lax.axis_index("exp") * 2 // lax.axis_size("exp")
    local = jnp.arange(held, dtype=jnp.int32)
    leaving = lax.dynamic_slice_in_dim(cross, mine * held, held)
    ranking = lax.dynamic_slice_in_dim(rank, mine * held, held)
    place = jnp.arange(most, dtype=jnp.int32)
    matches = leaving[None, :] & (ranking[None, :] == place[:, None])
    sent_index = jnp.sum(jnp.where(matches, local[None, :], 0), axis=1)
    wanted = lax.dynamic_slice_in_dim(source, mine * held, held)
    here = wanted // held == mine
    far = jnp.arange(source.shape[0], dtype=jnp.int32)[None, :] == wanted[:, None]
    far_rank = jnp.sum(jnp.where(far, rank[None, :], 0), axis=1)
    return sent_index, jnp.where(here, wanted - mine * held, held + far_rank)


def on_device(
    tokens, w_in, w_out, moments_in, moments_out, expert_ids, route_weights, old_plan, new_plan
):
    devices = lax.axis_size("exp")
    half = devices // 2
    slots = w_in.shape[0]
    held = half * slots
    chunk_a, chunk_b = (w_in, w_out, moments_out), (moments_in,)
    full_in = lax.all_gather(w_in, "grp", axis=1, tiled=True)
    full_out = lax.all_gather(w_out, "grp", axis=1, tiled=True)

    rows = weighted_rows(tokens, expert_ids, route_weights, old_plan)
    rows, *firsts = lax.optimization_barrier((rows, *chunk_a))
    inner = plane_size(devices)
    outer = range(0, devices, inner)
    column = [flip(rows, "exp", i) for i in outer]
    packed_a = pack(firsts, half)
    spread_a = exchange(packed_a, devices).reshape((held,) + packed_a.shape[2:])

    *plan, number = crossing(old_plan, new_plan)
    most = -(-held * FIXED // 16)
    sent_index, index = places(plan, held, held)
    across = [(d, (d + half) % devices) for d in range(devices)]

    sent_a = pick(sent_index[:most], spread_a)
    arrived_a = lax.ppermute(sent_a, "exp", across)
    packed_b = pack(chunk_b, half)
    spread_b = exchange(packed_b, devices).reshape((held,) + packed_b.shape[2:])
    sent_b = pick(sent_index[:most], spread_b)
    column, _ = lax.optimization_barrier((column, sent_a))
    steps = range(0, inner, 2)
    rows = jnp.concatenate(column, axis=0)
    blocks = [flip(rows, "exp", i) for i in steps]
    weights = [full_in, full_out, flip(full_in, "exp", 1), flip(full_out, "exp", 1)]
    me = lax.axis_index("exp").astype(jnp.int32)
    first = jnp.stack([me, me ^ 1]) * slots
    blocks[1:], sent_b = lax.optimization_barrier((blocks[1:], sent_b))
    parts = [experts(x, first, weights) for x in blocks]

    def more(state):
        place, *extra = state
        at = lax.dynamic_index_in_dim(sent_index, place, keepdims=False)
        out = []
        for spread, table in zip((spread_a, spread_b), extra):
            row = lax.dynamic_slice_in_dim(spread, at, 1, axis=0)
            row = lax.ppermute(row, "exp", across)
            out.append(lax.dynamic_update_slice_in_dim(table, row, place - most, axis=0))
        return place + 1, *out

    arrived_a, sent_b, parts = lax.optimization_barrier((arrived_a, sent_b, parts))
    extra = [
        jnp.zeros((max(held - most, 1),) + x.shape[1:], x.dtype) for x in (spread_a, spread_b)
    ]
    _, *extra = lax.while_loop(
        lambda state: state[0] < number, more, (jnp.int32(most), *extra)
    )

    arrived_b = lax.ppermute(sent_b, "exp", across)
    picked_a = pick(index, spread_a, arrived_a, extra[0])
    landed_a = exchange(picked_a.reshape(packed_a.shape), devices)
    partial = add_up([flip(x, "exp", i) for i, x in zip(steps, parts)])
    arrived_b, partial = lax.optimization_barrier((arrived_b, partial))

    picked_b = pick(index, spread_b, arrived_b, extra[1])
    (new_moments_in,) = unpack(exchange(picked_b.reshape(packed_b.shape), devices), chunk_b)
    new_w_in, new_w_out, new_moments_out = unpack(landed_a, chunk_a)
    size = tokens.shape[0]
    mixed = add_up([flip(partial[n * size : (n + 1) * size], "exp", i) for n, i in enumerate(outer)])
    return mixed, new_w_in, new_w_out, new_moments_in, new_moments_out


def solution(mesh):
    return jax.shard_map(
        on_device,
        mesh=mesh,
        in_specs=(
            P(("grp", "exp"), None),
            P("exp", "grp", None),
            P("exp", "grp", None),
            P("exp", None, "grp", None),
            P("exp", None, "grp", None),
            P(("grp", "exp"), None),
            P(("grp", "exp"), None),
            P(),
            P(),
        ),
        out_specs=(
            P(("grp", "exp"), None),
            P("exp", "grp", None),
            P("exp", "grp", None),
            P("exp", None, "grp", None),
            P("exp", None, "grp", None),
        ),
        check_vma=False,
    )
```

```python
import jax
import jax.numpy as jnp
from jax import lax
from jax.experimental import pallas as pl
from jax.experimental.pallas import tpu as pltpu
from jax.sharding import PartitionSpec as P

SUB = 8
LANE = 128
FIXED = 9


def to_tiles(x):
    slots, columns = x.shape[0], x.shape[-1]
    x = x.reshape(slots, -1, SUB, columns // LANE, LANE)
    return x.swapaxes(2, 3).reshape(slots, -1, SUB, LANE)


def from_tiles(x, shape):
    columns = shape[-1]
    x = x.reshape(shape[0], -1, columns // LANE, SUB, LANE)
    return x.swapaxes(2, 3).reshape(shape)


def in_parts(tiles, parts):
    return tiles.reshape(tiles.shape[0], parts, -1, SUB, LANE).swapaxes(0, 1)


def pack_kernel(*refs):
    *sources, out_ref, rows, in_sems, out_sems = refs
    parts, slots = out_ref.shape[:2]

    def copies(p):
        at = 0
        for n, source in enumerate(sources):
            count = source.shape[1] // parts
            for s in range(slots):
                yield pltpu.make_async_copy(
                    source.at[s, pl.ds(p * count, count)],
                    rows.at[p, s, pl.ds(at, count)],
                    in_sems.at[p, n, s],
                )
            at += count

    for p in range(parts):
        for copy in copies(p):
            copy.start()
    for p in range(parts):
        for copy in copies(p):
            copy.wait()
        pltpu.make_async_copy(rows.at[p], out_ref.at[p], out_sems.at[p]).start()
    for p in range(parts):
        pltpu.make_async_copy(rows.at[p], out_ref.at[p], out_sems.at[p]).wait()


def pack(arrays, parts):
    tiles = [to_tiles(a) for a in arrays]
    slots = tiles[0].shape[0]
    total = sum(t.shape[1] for t in tiles)
    if all(t.shape[1] % parts == 0 for t in tiles):
        shape = (parts, slots, total // parts, SUB, LANE)
        return pl.pallas_call(
            pack_kernel,
            in_specs=[pl.BlockSpec(memory_space=pl.ANY)] * len(tiles),
            out_specs=pl.BlockSpec(memory_space=pl.ANY),
            out_shape=jax.ShapeDtypeStruct(shape, tiles[0].dtype),
            scratch_shapes=[
                pltpu.VMEM(shape, tiles[0].dtype),
                pltpu.SemaphoreType.DMA((parts, len(tiles), slots)),
                pltpu.SemaphoreType.DMA((parts,)),
            ],
            compiler_params=pltpu.CompilerParams(vmem_limit_bytes=16 * 1024 * 1024),
            cost_estimate=pl.CostEstimate(flops=0, bytes_accessed=0, transcendentals=0),
        )(*tiles)
    tiles.append(jnp.zeros((slots, -total % parts, SUB, LANE), tiles[0].dtype))
    return in_parts(jnp.concatenate(tiles, axis=1), parts)


def unpack(landed, arrays):
    parts, slots = landed.shape[:2]
    counts = [a.size // (slots * SUB * LANE) for a in arrays]
    whole = all(count % parts == 0 for count in counts)
    if not whole:
        landed = landed.swapaxes(0, 1).reshape(slots, -1, SUB, LANE)
    outs, at = [], 0
    for a, count in zip(arrays, counts):
        if whole:
            part = landed[:, :, at // parts : (at + count) // parts].swapaxes(0, 1)
            outs.append(from_tiles(part.reshape(slots, count, SUB, LANE), a.shape))
        else:
            outs.append(from_tiles(landed[:, at : at + count], a.shape))
        at += count
    return outs


def pick_kernel(index_ref, *refs):
    *tables, out_ref, rows, in_sems, out_sems = refs
    count = out_ref.shape[0]
    for d in range(count):
        i = index_ref[d]
        low = 0
        for table in tables:
            size = table.shape[0]

            @pl.when((i >= low) & (i < low + size))
            def _(table=table, low=low):
                pltpu.make_async_copy(table.at[i - low], rows.at[d], in_sems.at[d]).start()

            low += size
    for d in range(count):
        pltpu.make_async_copy(tables[0].at[0], rows.at[d], in_sems.at[d]).wait()
        pltpu.make_async_copy(rows.at[d], out_ref.at[d], out_sems.at[d]).start()
    for d in range(count):
        pltpu.make_async_copy(rows.at[d], out_ref.at[d], out_sems.at[d]).wait()


def pick(index, *tables):
    count = index.shape[0]
    shape = (count,) + tables[0].shape[1:]
    return pl.pallas_call(
        pick_kernel,
        in_specs=[pl.BlockSpec(memory_space=pltpu.SMEM)]
        + [pl.BlockSpec(memory_space=pl.ANY)] * len(tables),
        out_specs=pl.BlockSpec(memory_space=pl.ANY),
        out_shape=jax.ShapeDtypeStruct(shape, tables[0].dtype),
        scratch_shapes=[
            pltpu.VMEM(shape, tables[0].dtype),
            pltpu.SemaphoreType.DMA((count,)),
            pltpu.SemaphoreType.DMA((count,)),
        ],
        compiler_params=pltpu.CompilerParams(vmem_limit_bytes=16 * 1024 * 1024),
        cost_estimate=pl.CostEstimate(flops=0, bytes_accessed=0, transcendentals=0),
    )(index, *tables)


def lay(blocks):
    laid = pick(jnp.arange(len(blocks), dtype=jnp.int32), *(x[None] for x in blocks))
    return laid.reshape((-1,) + blocks[0].shape[1:])


def expert_kernel(first_ref, x_ref, share_ref, *refs):
    *weight_refs, out_ref = refs
    half = share_ref.shape[1] // 2
    x = x_ref[...]
    weights = share_ref[...].astype(jnp.float32)
    lane = lax.broadcasted_iota(jnp.int32, weights.shape, 1)
    total = jnp.zeros(out_ref.shape, jnp.float32)
    for n in range(len(weight_refs) // 2):
        w_in_ref, w_out_ref = weight_refs[2 * n : 2 * n + 2]
        hidden_size = w_out_ref.shape[1]
        for j in range(w_in_ref.shape[0]):
            both = jnp.dot(x, w_in_ref[j], preferred_element_type=jnp.float32)
            gate, up = both[:, :hidden_size], both[:, hidden_size:]
            hidden = (gate / (1.0 + jnp.exp(-gate)) * up).astype(jnp.bfloat16)
            result = jnp.dot(hidden, w_out_ref[j], preferred_element_type=jnp.float32)
            result = result.astype(jnp.bfloat16).astype(jnp.float32)
            at = first_ref[n] + j
            mine = (lane == at) | (lane == at + half)
            weight = jnp.sum(jnp.where(mine, weights, 0.0), axis=1, keepdims=True)
            total = total + weight * result
    out_ref[...] = total.astype(out_ref.dtype)


def experts(x, shares, first, weights):
    rows, width = x.shape
    block = 256 if rows % 256 == 0 else rows
    return pl.pallas_call(
        expert_kernel,
        grid=(rows // block,),
        in_specs=[
            pl.BlockSpec(memory_space=pltpu.SMEM),
            pl.BlockSpec((block, width), lambda i: (i, 0)),
            pl.BlockSpec((block, shares.shape[1]), lambda i: (i, 0)),
        ]
        + [pl.BlockSpec(w.shape, lambda i: (0, 0, 0)) for w in weights],
        out_specs=pl.BlockSpec((block, width), lambda i: (i, 0)),
        out_shape=jax.ShapeDtypeStruct((rows, width), jnp.bfloat16),
        compiler_params=pltpu.CompilerParams(vmem_limit_bytes=40 * 1024 * 1024),
        cost_estimate=pl.CostEstimate(flops=0, bytes_accessed=0, transcendentals=0),
    )(first, x, shares, *weights)


def plane_size(devices):
    size = 1
    while 4 * size * size <= devices:
        size *= 2
    return size


def swap(x, axis, groups=None):
    return lax.all_to_all(
        x, axis, split_axis=0, concat_axis=0, axis_index_groups=groups, tiled=True
    )


def flip(x, axis, bits):
    if bits == 0:
        return x
    return lax.ppermute(x, axis, [(d, d ^ bits) for d in range(lax.axis_size(axis))])


def add_up(blocks):
    return sum(x.astype(jnp.float32) for x in blocks).astype(jnp.bfloat16)


def slot_shares(expert_ids, route_weights, old_plan):
    slot_count = old_plan.shape[0]
    slot_index = jnp.arange(slot_count, dtype=jnp.int32)
    share = route_weights / jnp.sum(route_weights, axis=1, keepdims=True)
    earlier = (old_plan[None, :] == old_plan[:, None]) & (slot_index[None, :] < slot_index[:, None])
    is_first = ~jnp.any(earlier, axis=1)
    chosen = (expert_ids[:, :, None] == old_plan[None, None, :]) & is_first[None, None, :]
    weight = jnp.sum(jnp.where(chosen, share[:, :, None], 0.0), axis=1)
    high = lax.reduce_precision(weight, exponent_bits=8, mantissa_bits=7)
    half = -(-2 * slot_count // LANE) * LANE // 2
    pad = jnp.zeros((weight.shape[0], half - slot_count), jnp.bfloat16)
    return jnp.concatenate(
        [high.astype(jnp.bfloat16), pad, (weight - high).astype(jnp.bfloat16), pad], axis=1
    )


def crossing(old_plan, new_plan):
    slot_count = old_plan.shape[0]
    held = slot_count // 2
    slot_index = jnp.arange(slot_count, dtype=jnp.int32)
    same_expert = new_plan[:, None] == old_plan[None, :]
    source = jnp.min(jnp.where(same_expert, slot_index[None, :], slot_count), axis=1)
    apart = slot_index[:, None] // held != slot_index[None, :] // held
    cross = jnp.any((source[:, None] == slot_index[None, :]) & apart, axis=0)
    before = (~apart) & (slot_index[:, None] < slot_index[None, :])
    rank = jnp.sum((before & cross[:, None]).astype(jnp.int32), axis=0)
    number = jnp.max(jnp.where(cross, rank + 1, 0))
    return source, cross, rank, number


def exchange(x, devices):
    half = devices // 2
    return swap(x, "exp", [list(range(half)), list(range(half, devices))])


def places(plan, held, most):
    source, cross, rank = plan
    mine = lax.axis_index("exp") * 2 // lax.axis_size("exp")
    local = jnp.arange(held, dtype=jnp.int32)
    leaving = lax.dynamic_slice_in_dim(cross, mine * held, held)
    ranking = lax.dynamic_slice_in_dim(rank, mine * held, held)
    place = jnp.arange(most, dtype=jnp.int32)
    matches = leaving[None, :] & (ranking[None, :] == place[:, None])
    sent_index = jnp.sum(jnp.where(matches, local[None, :], 0), axis=1)
    wanted = lax.dynamic_slice_in_dim(source, mine * held, held)
    here = wanted // held == mine
    far = jnp.arange(source.shape[0], dtype=jnp.int32)[None, :] == wanted[:, None]
    far_rank = jnp.sum(jnp.where(far, rank[None, :], 0), axis=1)
    return sent_index, jnp.where(here, wanted - mine * held, held + far_rank)


def on_device(
    tokens, w_in, w_out, moments_in, moments_out, expert_ids, route_weights, old_plan, new_plan
):
    devices = lax.axis_size("exp")
    half = devices // 2
    slots = w_in.shape[0]
    held = half * slots
    chunk_a, chunk_b = (w_in, w_out, moments_out), (moments_in,)
    full_in = lax.all_gather(w_in, "grp", axis=1, tiled=True)
    full_out = lax.all_gather(w_out, "grp", axis=1, tiled=True)

    shares = slot_shares(expert_ids, route_weights, old_plan)
    inner = plane_size(devices)
    outer = range(0, devices, inner)
    column = [[flip(x, "exp", i) for i in outer] for x in (tokens, shares)]
    packed_a, column = lax.optimization_barrier((pack(chunk_a, half), column))
    spread_a = exchange(packed_a, devices).reshape((held,) + packed_a.shape[2:])
    rows = [lay(x) for x in column]

    *plan, number = crossing(old_plan, new_plan)
    most = -(-held * FIXED // 16)
    sent_index, index = places(plan, held, held)
    across = [(d, (d + half) % devices) for d in range(devices)]

    sent_a = pick(sent_index[:most], spread_a)
    arrived_a = lax.ppermute(sent_a, "exp", across)
    packed_b = pack(chunk_b, half)
    spread_b = exchange(packed_b, devices).reshape((held,) + packed_b.shape[2:])
    sent_b = pick(sent_index[:most], spread_b)
    steps = range(0, inner, 2)
    blocks = [[flip(x, "exp", i) for x in rows] for i in steps]
    weights = [full_in, full_out, flip(full_in, "exp", 1), flip(full_out, "exp", 1)]
    me = lax.axis_index("exp").astype(jnp.int32)
    first = jnp.stack([me, me ^ 1]) * slots
    blocks[1:], sent_b = lax.optimization_barrier((blocks[1:], sent_b))
    parts = [experts(*x, first, weights) for x in blocks]

    def more(state):
        place, *extra = state
        at = lax.dynamic_index_in_dim(sent_index, place, keepdims=False)
        out = []
        for spread, table in zip((spread_a, spread_b), extra):
            row = lax.dynamic_slice_in_dim(spread, at, 1, axis=0)
            row = lax.ppermute(row, "exp", across)
            out.append(lax.dynamic_update_slice_in_dim(table, row, place - most, axis=0))
        return place + 1, *out

    extra = [
        jnp.zeros((max(held - most, 1),) + x.shape[1:], x.dtype) for x in (spread_a, spread_b)
    ]
    arrived_a, sent_b, parts, extra = lax.optimization_barrier((arrived_a, sent_b, parts, extra))
    _, *extra = lax.while_loop(
        lambda state: state[0] < number, more, (jnp.int32(most), *extra)
    )

    arrived_b = lax.ppermute(sent_b, "exp", across)
    picked_a = pick(index, spread_a, arrived_a, extra[0])
    landed_a = exchange(picked_a.reshape(packed_a.shape), devices)
    partial = add_up([flip(x, "exp", i) for i, x in zip(steps, parts)])
    outs_a = unpack(landed_a, chunk_a)
    arrived_b, partial, outs_a = lax.optimization_barrier((arrived_b, partial, outs_a))

    picked_b = pick(index, spread_b, arrived_b, extra[1])
    (new_moments_in,) = unpack(exchange(picked_b.reshape(packed_b.shape), devices), chunk_b)
    new_w_in, new_w_out, new_moments_out = outs_a
    size = tokens.shape[0]
    mixed = add_up([flip(partial[n * size : (n + 1) * size], "exp", i) for n, i in enumerate(outer)])
    return mixed, new_w_in, new_w_out, new_moments_in, new_moments_out


def solution(mesh):
    return jax.shard_map(
        on_device,
        mesh=mesh,
        in_specs=(
            P(("grp", "exp"), None),
            P("exp", "grp", None),
            P("exp", "grp", None),
            P("exp", None, "grp", None),
            P("exp", None, "grp", None),
            P(("grp", "exp"), None),
            P(("grp", "exp"), None),
            P(),
            P(),
        ),
        out_specs=(
            P(("grp", "exp"), None),
            P("exp", "grp", None),
            P("exp", "grp", None),
            P("exp", None, "grp", None),
            P("exp", None, "grp", None),
        ),
        check_vma=False,
    )
```

```python
import jax
import jax.numpy as jnp
from jax import lax
from jax.experimental import pallas as pl
from jax.experimental.pallas import tpu as pltpu
from jax.sharding import PartitionSpec as P

SUB = 8
LANE = 128
FIXED = 9


def to_tiles(x):
    slots, columns = x.shape[0], x.shape[-1]
    x = x.reshape(slots, -1, SUB, columns // LANE, LANE)
    return x.swapaxes(2, 3).reshape(slots, -1, SUB, LANE)


def from_tiles(x, shape):
    columns = shape[-1]
    x = x.reshape(shape[0], -1, columns // LANE, SUB, LANE)
    return x.swapaxes(2, 3).reshape(shape)


def in_parts(tiles, parts):
    return tiles.reshape(tiles.shape[0], parts, -1, SUB, LANE).swapaxes(0, 1)


def pack(arrays, parts):
    tiles = [to_tiles(a) for a in arrays]
    if all(t.shape[1] % parts == 0 for t in tiles):
        return jnp.concatenate([in_parts(t, parts) for t in tiles], axis=2)
    slots = tiles[0].shape[0]
    extra = -sum(t.shape[1] for t in tiles) % parts
    tiles.append(jnp.zeros((slots, extra, SUB, LANE), tiles[0].dtype))
    return in_parts(jnp.concatenate(tiles, axis=1), parts)


def unpack(landed, arrays):
    parts, slots = landed.shape[:2]
    counts = [a.size // (slots * SUB * LANE) for a in arrays]
    whole = all(count % parts == 0 for count in counts)
    if not whole:
        landed = landed.swapaxes(0, 1).reshape(slots, -1, SUB, LANE)
    outs, at = [], 0
    for a, count in zip(arrays, counts):
        if whole:
            part = landed[:, :, at // parts : (at + count) // parts].swapaxes(0, 1)
            outs.append(from_tiles(part.reshape(slots, count, SUB, LANE), a.shape))
        else:
            outs.append(from_tiles(landed[:, at : at + count], a.shape))
        at += count
    return outs


def pick_kernel(index_ref, *refs):
    *tables, out_ref, rows, in_sems, out_sems = refs
    count = out_ref.shape[0]
    for d in range(count):
        i = index_ref[d]
        low = 0
        for table in tables:
            size = table.shape[0]

            @pl.when((i >= low) & (i < low + size))
            def _(table=table, low=low):
                pltpu.make_async_copy(table.at[i - low], rows.at[d], in_sems.at[d]).start()

            low += size
    for d in range(count):
        pltpu.make_async_copy(tables[0].at[0], rows.at[d], in_sems.at[d]).wait()
        pltpu.make_async_copy(rows.at[d], out_ref.at[d], out_sems.at[d]).start()
    for d in range(count):
        pltpu.make_async_copy(rows.at[d], out_ref.at[d], out_sems.at[d]).wait()


def pick(index, *tables):
    count = index.shape[0]
    shape = (count,) + tables[0].shape[1:]
    return pl.pallas_call(
        pick_kernel,
        in_specs=[pl.BlockSpec(memory_space=pltpu.SMEM)]
        + [pl.BlockSpec(memory_space=pl.ANY)] * len(tables),
        out_specs=pl.BlockSpec(memory_space=pl.ANY),
        out_shape=jax.ShapeDtypeStruct(shape, tables[0].dtype),
        scratch_shapes=[
            pltpu.VMEM(shape, tables[0].dtype),
            pltpu.SemaphoreType.DMA((count,)),
            pltpu.SemaphoreType.DMA((count,)),
        ],
        compiler_params=pltpu.CompilerParams(vmem_limit_bytes=16 * 1024 * 1024),
        cost_estimate=pl.CostEstimate(flops=0, bytes_accessed=0, transcendentals=0),
    )(index, *tables)


def lay(blocks):
    laid = pick(jnp.arange(len(blocks), dtype=jnp.int32), *(x[None] for x in blocks))
    return laid.reshape((-1,) + blocks[0].shape[1:])


def expert_kernel(first_ref, x_ref, share_ref, *refs):
    *weight_refs, out_ref = refs
    half = share_ref.shape[1] // 2
    x = x_ref[...]
    weights = share_ref[...].astype(jnp.float32)
    lane = lax.broadcasted_iota(jnp.int32, weights.shape, 1)
    total = jnp.zeros(out_ref.shape, jnp.float32)
    for n in range(len(weight_refs) // 2):
        w_in_ref, w_out_ref = weight_refs[2 * n : 2 * n + 2]
        hidden_size = w_out_ref.shape[1]
        for j in range(w_in_ref.shape[0]):
            both = jnp.dot(x, w_in_ref[j], preferred_element_type=jnp.float32)
            gate, up = both[:, :hidden_size], both[:, hidden_size:]
            hidden = (gate / (1.0 + jnp.exp(-gate)) * up).astype(jnp.bfloat16)
            result = jnp.dot(hidden, w_out_ref[j], preferred_element_type=jnp.float32)
            result = result.astype(jnp.bfloat16).astype(jnp.float32)
            at = first_ref[n] + j
            mine = (lane == at) | (lane == at + half)
            weight = jnp.sum(jnp.where(mine, weights, 0.0), axis=1, keepdims=True)
            total = total + weight * result
    out_ref[...] = total.astype(out_ref.dtype)


def experts(x, shares, first, weights):
    rows, width = x.shape
    block = 256 if rows % 256 == 0 else rows
    return pl.pallas_call(
        expert_kernel,
        grid=(rows // block,),
        in_specs=[
            pl.BlockSpec(memory_space=pltpu.SMEM),
            pl.BlockSpec((block, width), lambda i: (i, 0)),
            pl.BlockSpec((block, shares.shape[1]), lambda i: (i, 0)),
        ]
        + [pl.BlockSpec(w.shape, lambda i: (0, 0, 0)) for w in weights],
        out_specs=pl.BlockSpec((block, width), lambda i: (i, 0)),
        out_shape=jax.ShapeDtypeStruct((rows, width), jnp.bfloat16),
        compiler_params=pltpu.CompilerParams(vmem_limit_bytes=40 * 1024 * 1024),
        cost_estimate=pl.CostEstimate(flops=0, bytes_accessed=0, transcendentals=0),
    )(first, x, shares, *weights)


def plane_size(devices):
    size = 1
    while 4 * size * size <= devices:
        size *= 2
    return size


def swap(x, axis, groups=None):
    return lax.all_to_all(
        x, axis, split_axis=0, concat_axis=0, axis_index_groups=groups, tiled=True
    )


def flip(x, axis, bits):
    if bits == 0:
        return x
    return lax.ppermute(x, axis, [(d, d ^ bits) for d in range(lax.axis_size(axis))])


def add_up(blocks):
    return sum(x.astype(jnp.float32) for x in blocks).astype(jnp.bfloat16)


def slot_shares(expert_ids, route_weights, old_plan):
    slot_count = old_plan.shape[0]
    slot_index = jnp.arange(slot_count, dtype=jnp.int32)
    share = route_weights / jnp.sum(route_weights, axis=1, keepdims=True)
    earlier = (old_plan[None, :] == old_plan[:, None]) & (slot_index[None, :] < slot_index[:, None])
    is_first = ~jnp.any(earlier, axis=1)
    chosen = (expert_ids[:, :, None] == old_plan[None, None, :]) & is_first[None, None, :]
    weight = jnp.sum(jnp.where(chosen, share[:, :, None], 0.0), axis=1)
    high = lax.reduce_precision(weight, exponent_bits=8, mantissa_bits=7)
    half = -(-2 * slot_count // LANE) * LANE // 2
    pad = jnp.zeros((weight.shape[0], half - slot_count), jnp.bfloat16)
    return jnp.concatenate(
        [high.astype(jnp.bfloat16), pad, (weight - high).astype(jnp.bfloat16), pad], axis=1
    )


def crossing(old_plan, new_plan):
    slot_count = old_plan.shape[0]
    held = slot_count // 2
    slot_index = jnp.arange(slot_count, dtype=jnp.int32)
    same_expert = new_plan[:, None] == old_plan[None, :]
    source = jnp.min(jnp.where(same_expert, slot_index[None, :], slot_count), axis=1)
    apart = slot_index[:, None] // held != slot_index[None, :] // held
    cross = jnp.any((source[:, None] == slot_index[None, :]) & apart, axis=0)
    before = (~apart) & (slot_index[:, None] < slot_index[None, :])
    rank = jnp.sum((before & cross[:, None]).astype(jnp.int32), axis=0)
    number = jnp.max(jnp.where(cross, rank + 1, 0))
    return source, cross, rank, number


def exchange(x, devices):
    half = devices // 2
    return swap(x, "exp", [list(range(half)), list(range(half, devices))])


def places(plan, held, most):
    source, cross, rank = plan
    mine = lax.axis_index("exp") * 2 // lax.axis_size("exp")
    local = jnp.arange(held, dtype=jnp.int32)
    leaving = lax.dynamic_slice_in_dim(cross, mine * held, held)
    ranking = lax.dynamic_slice_in_dim(rank, mine * held, held)
    place = jnp.arange(most, dtype=jnp.int32)
    matches = leaving[None, :] & (ranking[None, :] == place[:, None])
    sent_index = jnp.sum(jnp.where(matches, local[None, :], 0), axis=1)
    wanted = lax.dynamic_slice_in_dim(source, mine * held, held)
    here = wanted // held == mine
    far = jnp.arange(source.shape[0], dtype=jnp.int32)[None, :] == wanted[:, None]
    far_rank = jnp.sum(jnp.where(far, rank[None, :], 0), axis=1)
    return sent_index, jnp.where(here, wanted - mine * held, held + far_rank)


def on_device(
    tokens, w_in, w_out, moments_in, moments_out, expert_ids, route_weights, old_plan, new_plan
):
    devices = lax.axis_size("exp")
    half = devices // 2
    slots = w_in.shape[0]
    held = half * slots
    chunk_a, chunk_b = (w_in, w_out, moments_out), (moments_in,)
    full_in = lax.all_gather(w_in, "grp", axis=1, tiled=True)
    full_out = lax.all_gather(w_out, "grp", axis=1, tiled=True)

    shares = slot_shares(expert_ids, route_weights, old_plan)
    inner = plane_size(devices)
    outer = range(0, devices, inner)
    column = [[flip(x, "exp", i) for i in outer] for x in (tokens, shares)]
    packed_a, column[0] = lax.optimization_barrier((pack(chunk_a, half), column[0]))
    spread_a = exchange(packed_a, devices).reshape((held,) + packed_a.shape[2:])
    rows = [lay(x) for x in column]

    *plan, number = crossing(old_plan, new_plan)
    most = -(-held * FIXED // 16)
    sent_index, index = places(plan, held, held)
    across = [(d, (d + half) % devices) for d in range(devices)]

    sent_a = pick(sent_index[:most], spread_a)
    arrived_a = lax.ppermute(sent_a, "exp", across)
    packed_b = pack(chunk_b, half)
    spread_b = exchange(packed_b, devices).reshape((held,) + packed_b.shape[2:])
    sent_b = pick(sent_index[:most], spread_b)
    steps = range(0, inner, 2)
    blocks = [[flip(x, "exp", i) for x in rows] for i in steps]
    weights = [full_in, full_out, flip(full_in, "exp", 1), flip(full_out, "exp", 1)]
    me = lax.axis_index("exp").astype(jnp.int32)
    first = jnp.stack([me, me ^ 1]) * slots
    blocks[1:], sent_b = lax.optimization_barrier((blocks[1:], sent_b))
    parts = [experts(*x, first, weights) for x in blocks]

    def more(state):
        place, *extra = state
        at = lax.dynamic_index_in_dim(sent_index, place, keepdims=False)
        out = []
        for spread, table in zip((spread_a, spread_b), extra):
            row = lax.dynamic_slice_in_dim(spread, at, 1, axis=0)
            row = lax.ppermute(row, "exp", across)
            out.append(lax.dynamic_update_slice_in_dim(table, row, place - most, axis=0))
        return place + 1, *out

    extra = [x[: max(held - most, 1)] for x in (spread_a, spread_b)]
    arrived_a, sent_b, parts, extra = lax.optimization_barrier((arrived_a, sent_b, parts, extra))
    _, *extra = lax.while_loop(
        lambda state: state[0] < number, more, (jnp.int32(most), *extra)
    )

    arrived_b = lax.ppermute(sent_b, "exp", across)
    picked_a = pick(index, spread_a, arrived_a, extra[0])
    landed_a = exchange(picked_a.reshape(packed_a.shape), devices)
    partial = add_up([flip(x, "exp", i) for i, x in zip(steps, parts)])
    arrived_b, partial = lax.optimization_barrier((arrived_b, partial))

    picked_b = pick(index, spread_b, arrived_b, extra[1])
    (new_moments_in,) = unpack(exchange(picked_b.reshape(packed_b.shape), devices), chunk_b)
    size = tokens.shape[0]
    pieces = [partial[n * size : (n + 1) * size] for n in range(len(outer))]
    outs_a, pieces[1] = lax.optimization_barrier((unpack(landed_a, chunk_a), pieces[1]))
    new_w_in, new_w_out, new_moments_out = outs_a
    mixed = add_up([flip(x, "exp", i) for i, x in zip(outer, pieces)])
    return mixed, new_w_in, new_w_out, new_moments_in, new_moments_out


def solution(mesh):
    return jax.shard_map(
        on_device,
        mesh=mesh,
        in_specs=(
            P(("grp", "exp"), None),
            P("exp", "grp", None),
            P("exp", "grp", None),
            P("exp", None, "grp", None),
            P("exp", None, "grp", None),
            P(("grp", "exp"), None),
            P(("grp", "exp"), None),
            P(),
            P(),
        ),
        out_specs=(
            P(("grp", "exp"), None),
            P("exp", "grp", None),
            P("exp", "grp", None),
            P("exp", None, "grp", None),
            P("exp", None, "grp", None),
        ),
        check_vma=False,
    )
```

```python
import jax
import jax.numpy as jnp
from jax import lax
from jax.experimental import pallas as pl
from jax.experimental.pallas import tpu as pltpu
from jax.sharding import PartitionSpec as P

SUB = 8
LANE = 128
FIXED = 9


def to_tiles(x):
    slots, columns = x.shape[0], x.shape[-1]
    x = x.reshape(slots, -1, SUB, columns // LANE, LANE)
    return x.swapaxes(2, 3).reshape(slots, -1, SUB, LANE)


def from_tiles(x, shape):
    columns = shape[-1]
    x = x.reshape(shape[0], -1, columns // LANE, SUB, LANE)
    return x.swapaxes(2, 3).reshape(shape)


def in_parts(tiles, parts):
    return tiles.reshape(tiles.shape[0], parts, -1, SUB, LANE).swapaxes(0, 1)


def pack(arrays, parts):
    tiles = [to_tiles(a) for a in arrays]
    if all(t.shape[1] % parts == 0 for t in tiles):
        return jnp.concatenate([in_parts(t, parts) for t in tiles], axis=2)
    slots = tiles[0].shape[0]
    extra = -sum(t.shape[1] for t in tiles) % parts
    tiles.append(jnp.zeros((slots, extra, SUB, LANE), tiles[0].dtype))
    return in_parts(jnp.concatenate(tiles, axis=1), parts)


def unpack(landed, arrays):
    parts, slots = landed.shape[:2]
    counts = [a.size // (slots * SUB * LANE) for a in arrays]
    whole = all(count % parts == 0 for count in counts)
    if not whole:
        landed = landed.swapaxes(0, 1).reshape(slots, -1, SUB, LANE)
    outs, at = [], 0
    for a, count in zip(arrays, counts):
        if whole:
            part = landed[:, :, at // parts : (at + count) // parts].swapaxes(0, 1)
            outs.append(from_tiles(part.reshape(slots, count, SUB, LANE), a.shape))
        else:
            outs.append(from_tiles(landed[:, at : at + count], a.shape))
        at += count
    return outs


def pick_kernel(index_ref, *refs):
    *tables, out_ref, rows, in_sems, out_sems = refs
    count = out_ref.shape[0]
    for d in range(count):
        i = index_ref[d]
        low = 0
        for table in tables:
            size = table.shape[0]

            @pl.when((i >= low) & (i < low + size))
            def _(table=table, low=low):
                pltpu.make_async_copy(table.at[i - low], rows.at[d], in_sems.at[d]).start()

            low += size
    for d in range(count):
        pltpu.make_async_copy(tables[0].at[0], rows.at[d], in_sems.at[d]).wait()
        pltpu.make_async_copy(rows.at[d], out_ref.at[d], out_sems.at[d]).start()
    for d in range(count):
        pltpu.make_async_copy(rows.at[d], out_ref.at[d], out_sems.at[d]).wait()


def pick(index, *tables):
    count = index.shape[0]
    shape = (count,) + tables[0].shape[1:]
    return pl.pallas_call(
        pick_kernel,
        in_specs=[pl.BlockSpec(memory_space=pltpu.SMEM)]
        + [pl.BlockSpec(memory_space=pl.ANY)] * len(tables),
        out_specs=pl.BlockSpec(memory_space=pl.ANY),
        out_shape=jax.ShapeDtypeStruct(shape, tables[0].dtype),
        scratch_shapes=[
            pltpu.VMEM(shape, tables[0].dtype),
            pltpu.SemaphoreType.DMA((count,)),
            pltpu.SemaphoreType.DMA((count,)),
        ],
        compiler_params=pltpu.CompilerParams(vmem_limit_bytes=16 * 1024 * 1024),
        cost_estimate=pl.CostEstimate(flops=0, bytes_accessed=0, transcendentals=0),
    )(index, *tables)


def lay(blocks):
    laid = pick(jnp.arange(len(blocks), dtype=jnp.int32), *(x[None] for x in blocks))
    return laid.reshape((-1,) + blocks[0].shape[1:])


def expert_kernel(first_ref, x_ref, *refs):
    *weight_refs, out_ref = refs
    width = out_ref.shape[1]
    half = (x_ref.shape[1] - width) // 2
    x = x_ref[:, :width]
    weights = x_ref[:, width:].astype(jnp.float32)
    lane = lax.broadcasted_iota(jnp.int32, weights.shape, 1)
    total = jnp.zeros(out_ref.shape, jnp.float32)
    for n in range(len(weight_refs) // 2):
        w_in_ref, w_out_ref = weight_refs[2 * n : 2 * n + 2]
        hidden_size = w_out_ref.shape[1]
        for j in range(w_in_ref.shape[0]):
            both = jnp.dot(x, w_in_ref[j], preferred_element_type=jnp.float32)
            gate, up = both[:, :hidden_size], both[:, hidden_size:]
            hidden = (gate / (1.0 + jnp.exp(-gate)) * up).astype(jnp.bfloat16)
            result = jnp.dot(hidden, w_out_ref[j], preferred_element_type=jnp.float32)
            result = result.astype(jnp.bfloat16).astype(jnp.float32)
            at = first_ref[n] + j
            mine = (lane == at) | (lane == at + half)
            weight = jnp.sum(jnp.where(mine, weights, 0.0), axis=1, keepdims=True)
            total = total + weight * result
    out_ref[...] = total.astype(out_ref.dtype)


def experts(x, first, weights):
    rows, columns = x.shape
    width = weights[0].shape[1]
    block = 256 if rows % 256 == 0 else rows
    return pl.pallas_call(
        expert_kernel,
        grid=(rows // block,),
        in_specs=[
            pl.BlockSpec(memory_space=pltpu.SMEM),
            pl.BlockSpec((block, columns), lambda i: (i, 0)),
        ]
        + [pl.BlockSpec(w.shape, lambda i: (0, 0, 0)) for w in weights],
        out_specs=pl.BlockSpec((block, width), lambda i: (i, 0)),
        out_shape=jax.ShapeDtypeStruct((rows, width), jnp.bfloat16),
        compiler_params=pltpu.CompilerParams(vmem_limit_bytes=40 * 1024 * 1024),
        cost_estimate=pl.CostEstimate(flops=0, bytes_accessed=0, transcendentals=0),
    )(first, x, *weights)


def plane_size(devices):
    size = 1
    while 4 * size * size <= devices:
        size *= 2
    return size


def swap(x, axis, groups=None):
    return lax.all_to_all(
        x, axis, split_axis=0, concat_axis=0, axis_index_groups=groups, tiled=True
    )


def flip(x, axis, bits):
    if bits == 0:
        return x
    return lax.ppermute(x, axis, [(d, d ^ bits) for d in range(lax.axis_size(axis))])


def add_up(blocks):
    return sum(x.astype(jnp.float32) for x in blocks).astype(jnp.bfloat16)


def weighted_rows(tokens, expert_ids, route_weights, old_plan):
    slot_count = old_plan.shape[0]
    slot_index = jnp.arange(slot_count, dtype=jnp.int32)
    share = route_weights / jnp.sum(route_weights, axis=1, keepdims=True)
    earlier = (old_plan[None, :] == old_plan[:, None]) & (slot_index[None, :] < slot_index[:, None])
    is_first = ~jnp.any(earlier, axis=1)
    chosen = (expert_ids[:, :, None] == old_plan[None, None, :]) & is_first[None, None, :]
    weight = jnp.sum(jnp.where(chosen, share[:, :, None], 0.0), axis=1)
    high = lax.reduce_precision(weight, exponent_bits=8, mantissa_bits=7)
    half = -(-2 * slot_count // LANE) * LANE // 2
    pad = jnp.zeros((tokens.shape[0], half - slot_count), jnp.bfloat16)
    return jnp.concatenate(
        [tokens, high.astype(jnp.bfloat16), pad, (weight - high).astype(jnp.bfloat16), pad], axis=1
    )


def crossing(old_plan, new_plan):
    slot_count = old_plan.shape[0]
    held = slot_count // 2
    slot_index = jnp.arange(slot_count, dtype=jnp.int32)
    same_expert = new_plan[:, None] == old_plan[None, :]
    source = jnp.min(jnp.where(same_expert, slot_index[None, :], slot_count), axis=1)
    apart = slot_index[:, None] // held != slot_index[None, :] // held
    cross = jnp.any((source[:, None] == slot_index[None, :]) & apart, axis=0)
    before = (~apart) & (slot_index[:, None] < slot_index[None, :])
    rank = jnp.sum((before & cross[:, None]).astype(jnp.int32), axis=0)
    number = jnp.max(jnp.where(cross, rank + 1, 0))
    return source, cross, rank, number


def exchange(x, devices):
    half = devices // 2
    return swap(x, "exp", [list(range(half)), list(range(half, devices))])


def places(plan, held, most):
    source, cross, rank = plan
    mine = lax.axis_index("exp") * 2 // lax.axis_size("exp")
    local = jnp.arange(held, dtype=jnp.int32)
    leaving = lax.dynamic_slice_in_dim(cross, mine * held, held)
    ranking = lax.dynamic_slice_in_dim(rank, mine * held, held)
    place = jnp.arange(most, dtype=jnp.int32)
    matches = leaving[None, :] & (ranking[None, :] == place[:, None])
    sent_index = jnp.sum(jnp.where(matches, local[None, :], 0), axis=1)
    wanted = lax.dynamic_slice_in_dim(source, mine * held, held)
    here = wanted // held == mine
    far = jnp.arange(source.shape[0], dtype=jnp.int32)[None, :] == wanted[:, None]
    far_rank = jnp.sum(jnp.where(far, rank[None, :], 0), axis=1)
    return sent_index, jnp.where(here, wanted - mine * held, held + far_rank)


def on_device(
    tokens, w_in, w_out, moments_in, moments_out, expert_ids, route_weights, old_plan, new_plan
):
    devices = lax.axis_size("exp")
    half = devices // 2
    slots = w_in.shape[0]
    held = half * slots
    chunk_a, chunk_b, chunk_c = (w_in, w_out), (moments_in,), (moments_out,)
    full_in = lax.all_gather(w_in, "grp", axis=1, tiled=True)
    full_out = lax.all_gather(w_out, "grp", axis=1, tiled=True)
    *plan, number = crossing(old_plan, new_plan)
    most = -(-held * FIXED // 16)
    sent_index, index = places(plan, held, held)
    across = [(d, (d + half) % devices) for d in range(devices)]

    def leave(spread):
        return pick(sent_index[:most], spread)

    def spread_out(packed):
        return exchange(packed, devices).reshape((held,) + packed.shape[2:])

    def collect(spread, arrived, extra):
        picked = pick(index, spread, arrived, extra)
        return exchange(picked.reshape((half, slots) + picked.shape[1:]), devices)

    def beyond(*spreads):
        def more(state):
            place, *extra = state
            at = lax.dynamic_index_in_dim(sent_index, place, keepdims=False)
            out = []
            for spread, table in zip(spreads, extra):
                row = lax.dynamic_slice_in_dim(spread, at, 1, axis=0)
                row = lax.ppermute(row, "exp", across)
                out.append(lax.dynamic_update_slice_in_dim(table, row, place - most, axis=0))
            return place + 1, *out

        extra = [x[: max(held - most, 1)] for x in spreads]
        state = lax.while_loop(
            lambda state: state[0] < number, more, (jnp.int32(most), *extra)
        )
        return state[1:]

    rows = weighted_rows(tokens, expert_ids, route_weights, old_plan)
    inner = plane_size(devices)
    outer = range(0, devices, inner)
    column = [flip(rows, "exp", i) for i in outer]
    packed_a, column = lax.optimization_barrier((pack(chunk_a, half), column))
    spread_a, packed_b, packed_c = lax.optimization_barrier(
        (spread_out(packed_a), pack(chunk_b, half), pack(chunk_c, half))
    )
    rows = lay(column)

    arrived_a = lax.ppermute(leave(spread_a), "exp", across)
    spread_b, packed_c = lax.optimization_barrier((spread_out(packed_b), packed_c))
    sent_b = leave(spread_b)
    spread_c = spread_out(packed_c)
    steps = range(0, inner, 2)
    blocks = [flip(rows, "exp", i) for i in steps]
    weights = [full_in, full_out, flip(full_in, "exp", 1), flip(full_out, "exp", 1)]
    arrived_a, sent_b, blocks = lax.optimization_barrier((arrived_a, sent_b, blocks))

    extra_a, extra_b = beyond(spread_a, spread_b)
    arrived_b = lax.ppermute(sent_b, "exp", across)
    landed_a = collect(spread_a, arrived_a, extra_a)
    me = lax.axis_index("exp").astype(jnp.int32)
    first = jnp.stack([me, me ^ 1]) * slots
    parts = [experts(x, first, weights) for x in blocks]
    arrived_b, sent_c, parts = lax.optimization_barrier((arrived_b, leave(spread_c), parts))

    (extra_c,) = beyond(spread_c)
    arrived_c = lax.ppermute(sent_c, "exp", across)
    landed_b = collect(spread_b, arrived_b, extra_b)
    partial = add_up([flip(x, "exp", i) for i, x in zip(steps, parts)])
    arrived_c, partial = lax.optimization_barrier((arrived_c, partial))

    landed_c = collect(spread_c, arrived_c, extra_c)
    size = tokens.shape[0]
    pieces = [partial[n * size : (n + 1) * size] for n in range(len(outer))]
    outs_a, pieces[1] = lax.optimization_barrier((unpack(landed_a, chunk_a), pieces[1]))
    mixed = add_up([flip(x, "exp", i) for i, x in zip(outer, pieces)])
    new_w_in, new_w_out = outs_a
    (new_moments_in,) = unpack(landed_b, chunk_b)
    (new_moments_out,) = unpack(landed_c, chunk_c)
    return mixed, new_w_in, new_w_out, new_moments_in, new_moments_out


def solution(mesh):
    return jax.shard_map(
        on_device,
        mesh=mesh,
        in_specs=(
            P(("grp", "exp"), None),
            P("exp", "grp", None),
            P("exp", "grp", None),
            P("exp", None, "grp", None),
            P("exp", None, "grp", None),
            P(("grp", "exp"), None),
            P(("grp", "exp"), None),
            P(),
            P(),
        ),
        out_specs=(
            P(("grp", "exp"), None),
            P("exp", "grp", None),
            P("exp", "grp", None),
            P("exp", None, "grp", None),
            P("exp", None, "grp", None),
        ),
        check_vma=False,
    )
```

```python
import jax
import jax.numpy as jnp
from jax import lax
from jax.experimental import pallas as pl
from jax.experimental.pallas import tpu as pltpu
from jax.sharding import PartitionSpec as P

SUB = 8
LANE = 128
FIXED = 9


def to_tiles(x):
    slots, columns = x.shape[0], x.shape[-1]
    x = x.reshape(slots, -1, SUB, columns // LANE, LANE)
    return x.swapaxes(2, 3).reshape(slots, -1, SUB, LANE)


def from_tiles(x, shape):
    columns = shape[-1]
    x = x.reshape(shape[0], -1, columns // LANE, SUB, LANE)
    return x.swapaxes(2, 3).reshape(shape)


def in_parts(tiles, parts):
    return tiles.reshape(tiles.shape[0], parts, -1, SUB, LANE).swapaxes(0, 1)


def pack(arrays, parts):
    tiles = [to_tiles(a) for a in arrays]
    if all(t.shape[1] % parts == 0 for t in tiles):
        return jnp.concatenate([in_parts(t, parts) for t in tiles], axis=2)
    slots = tiles[0].shape[0]
    extra = -sum(t.shape[1] for t in tiles) % parts
    tiles.append(jnp.zeros((slots, extra, SUB, LANE), tiles[0].dtype))
    return in_parts(jnp.concatenate(tiles, axis=1), parts)


def unpack(landed, arrays):
    parts, slots = landed.shape[:2]
    counts = [a.size // (slots * SUB * LANE) for a in arrays]
    whole = all(count % parts == 0 for count in counts)
    if not whole:
        landed = landed.swapaxes(0, 1).reshape(slots, -1, SUB, LANE)
    outs, at = [], 0
    for a, count in zip(arrays, counts):
        if whole:
            part = landed[:, :, at // parts : (at + count) // parts].swapaxes(0, 1)
            outs.append(from_tiles(part.reshape(slots, count, SUB, LANE), a.shape))
        else:
            outs.append(from_tiles(landed[:, at : at + count], a.shape))
        at += count
    return outs


def pick_kernel(index_ref, *refs):
    *tables, out_ref, rows, in_sems, out_sems = refs
    count = out_ref.shape[0]
    for d in range(count):
        i = index_ref[d]
        low = 0
        for table in tables:
            size = table.shape[0]

            @pl.when((i >= low) & (i < low + size))
            def _(table=table, low=low):
                pltpu.make_async_copy(table.at[i - low], rows.at[d], in_sems.at[d]).start()

            low += size
    for d in range(count):
        pltpu.make_async_copy(tables[0].at[0], rows.at[d], in_sems.at[d]).wait()
        pltpu.make_async_copy(rows.at[d], out_ref.at[d], out_sems.at[d]).start()
    for d in range(count):
        pltpu.make_async_copy(rows.at[d], out_ref.at[d], out_sems.at[d]).wait()


def pick(index, *tables):
    count = index.shape[0]
    shape = (count,) + tables[0].shape[1:]
    return pl.pallas_call(
        pick_kernel,
        in_specs=[pl.BlockSpec(memory_space=pltpu.SMEM)]
        + [pl.BlockSpec(memory_space=pl.ANY)] * len(tables),
        out_specs=pl.BlockSpec(memory_space=pl.ANY),
        out_shape=jax.ShapeDtypeStruct(shape, tables[0].dtype),
        scratch_shapes=[
            pltpu.VMEM(shape, tables[0].dtype),
            pltpu.SemaphoreType.DMA((count,)),
            pltpu.SemaphoreType.DMA((count,)),
        ],
        compiler_params=pltpu.CompilerParams(vmem_limit_bytes=16 * 1024 * 1024),
        cost_estimate=pl.CostEstimate(flops=0, bytes_accessed=0, transcendentals=0),
    )(index, *tables)


def lay(blocks):
    laid = pick(jnp.arange(len(blocks), dtype=jnp.int32), *(x[None] for x in blocks))
    return laid.reshape((-1,) + blocks[0].shape[1:])


def expert_kernel(first_ref, x_ref, *refs):
    *weight_refs, out_ref = refs
    width = out_ref.shape[1]
    half = (x_ref.shape[1] - width) // 2
    x = x_ref[:, :width]
    weights = x_ref[:, width:].astype(jnp.float32)
    lane = lax.broadcasted_iota(jnp.int32, weights.shape, 1)
    total = jnp.zeros(out_ref.shape, jnp.float32)
    for n in range(len(weight_refs) // 2):
        w_in_ref, w_out_ref = weight_refs[2 * n : 2 * n + 2]
        hidden_size = w_out_ref.shape[1]
        for j in range(w_in_ref.shape[0]):
            both = jnp.dot(x, w_in_ref[j], preferred_element_type=jnp.float32)
            gate, up = both[:, :hidden_size], both[:, hidden_size:]
            hidden = (gate / (1.0 + jnp.exp(-gate)) * up).astype(jnp.bfloat16)
            result = jnp.dot(hidden, w_out_ref[j], preferred_element_type=jnp.float32)
            result = result.astype(jnp.bfloat16).astype(jnp.float32)
            at = first_ref[n] + j
            mine = (lane == at) | (lane == at + half)
            weight = jnp.sum(jnp.where(mine, weights, 0.0), axis=1, keepdims=True)
            total = total + weight * result
    out_ref[...] = total.astype(out_ref.dtype)


def experts(x, first, weights):
    rows, columns = x.shape
    width = weights[0].shape[1]
    block = 256 if rows % 256 == 0 else rows
    return pl.pallas_call(
        expert_kernel,
        grid=(rows // block,),
        in_specs=[
            pl.BlockSpec(memory_space=pltpu.SMEM),
            pl.BlockSpec((block, columns), lambda i: (i, 0)),
        ]
        + [pl.BlockSpec(w.shape, lambda i: (0, 0, 0)) for w in weights],
        out_specs=pl.BlockSpec((block, width), lambda i: (i, 0)),
        out_shape=jax.ShapeDtypeStruct((rows, width), jnp.bfloat16),
        compiler_params=pltpu.CompilerParams(vmem_limit_bytes=40 * 1024 * 1024),
        cost_estimate=pl.CostEstimate(flops=0, bytes_accessed=0, transcendentals=0),
    )(first, x, *weights)


def plane_size(devices):
    size = 1
    while 4 * size * size <= devices:
        size *= 2
    return size


def swap(x, axis, groups=None):
    return lax.all_to_all(
        x, axis, split_axis=0, concat_axis=0, axis_index_groups=groups, tiled=True
    )


def flip(x, axis, bits):
    if bits == 0:
        return x
    return lax.ppermute(x, axis, [(d, d ^ bits) for d in range(lax.axis_size(axis))])


def add_up(blocks):
    return sum(x.astype(jnp.float32) for x in blocks).astype(jnp.bfloat16)


def weighted_rows(tokens, expert_ids, route_weights, old_plan):
    slot_count = old_plan.shape[0]
    slot_index = jnp.arange(slot_count, dtype=jnp.int32)
    share = route_weights / jnp.sum(route_weights, axis=1, keepdims=True)
    earlier = (old_plan[None, :] == old_plan[:, None]) & (slot_index[None, :] < slot_index[:, None])
    is_first = ~jnp.any(earlier, axis=1)
    chosen = (expert_ids[:, :, None] == old_plan[None, None, :]) & is_first[None, None, :]
    weight = jnp.sum(jnp.where(chosen, share[:, :, None], 0.0), axis=1)
    high = lax.reduce_precision(weight, exponent_bits=8, mantissa_bits=7)
    half = -(-2 * slot_count // LANE) * LANE // 2
    pad = jnp.zeros((tokens.shape[0], half - slot_count), jnp.bfloat16)
    return jnp.concatenate(
        [tokens, high.astype(jnp.bfloat16), pad, (weight - high).astype(jnp.bfloat16), pad], axis=1
    )


def crossing(old_plan, new_plan):
    slot_count = old_plan.shape[0]
    held = slot_count // 2
    slot_index = jnp.arange(slot_count, dtype=jnp.int32)
    same_expert = new_plan[:, None] == old_plan[None, :]
    source = jnp.min(jnp.where(same_expert, slot_index[None, :], slot_count), axis=1)
    apart = slot_index[:, None] // held != slot_index[None, :] // held
    cross = jnp.any((source[:, None] == slot_index[None, :]) & apart, axis=0)
    before = (~apart) & (slot_index[:, None] < slot_index[None, :])
    rank = jnp.sum((before & cross[:, None]).astype(jnp.int32), axis=0)
    number = jnp.max(jnp.where(cross, rank + 1, 0))
    return source, cross, rank, number


def exchange(x, devices):
    half = devices // 2
    return swap(x, "exp", [list(range(half)), list(range(half, devices))])


def places(plan, held, most):
    source, cross, rank = plan
    mine = lax.axis_index("exp") * 2 // lax.axis_size("exp")
    local = jnp.arange(held, dtype=jnp.int32)
    leaving = lax.dynamic_slice_in_dim(cross, mine * held, held)
    ranking = lax.dynamic_slice_in_dim(rank, mine * held, held)
    place = jnp.arange(most, dtype=jnp.int32)
    matches = leaving[None, :] & (ranking[None, :] == place[:, None])
    sent_index = jnp.sum(jnp.where(matches, local[None, :], 0), axis=1)
    wanted = lax.dynamic_slice_in_dim(source, mine * held, held)
    here = wanted // held == mine
    far = jnp.arange(source.shape[0], dtype=jnp.int32)[None, :] == wanted[:, None]
    far_rank = jnp.sum(jnp.where(far, rank[None, :], 0), axis=1)
    return sent_index, jnp.where(here, wanted - mine * held, held + far_rank)


def on_device(
    tokens, w_in, w_out, moments_in, moments_out, expert_ids, route_weights, old_plan, new_plan
):
    devices = lax.axis_size("exp")
    half = devices // 2
    slots = w_in.shape[0]
    held = half * slots
    chunk_a, chunk_b, chunk_c = (w_in, w_out), (moments_in,), (moments_out,)
    full_in = lax.all_gather(w_in, "grp", axis=1, tiled=True)
    full_out = lax.all_gather(w_out, "grp", axis=1, tiled=True)
    *plan, number = crossing(old_plan, new_plan)
    most = -(-held * FIXED // 16)
    sent_index, index = places(plan, held, held)
    across = [(d, (d + half) % devices) for d in range(devices)]

    def leave(spread):
        return pick(sent_index[:most], spread)

    def spread_out(packed):
        return exchange(packed, devices).reshape((held,) + packed.shape[2:])

    def stay(spread, arrived, extra):
        picked = pick(index, spread, arrived, extra)
        return picked.reshape((half, slots) + picked.shape[1:])

    def beyond(*spreads):
        def more(state):
            place, *extra = state
            at = lax.dynamic_index_in_dim(sent_index, place, keepdims=False)
            out = []
            for spread, table in zip(spreads, extra):
                row = lax.dynamic_slice_in_dim(spread, at, 1, axis=0)
                row = lax.ppermute(row, "exp", across)
                out.append(lax.dynamic_update_slice_in_dim(table, row, place - most, axis=0))
            return place + 1, *out

        extra = [x[: max(held - most, 1)] for x in spreads]
        state = lax.while_loop(
            lambda state: state[0] < number, more, (jnp.int32(most), *extra)
        )
        return state[1:]

    rows = weighted_rows(tokens, expert_ids, route_weights, old_plan)
    inner = plane_size(devices)
    outer = range(0, devices, inner)
    column = [flip(rows, "exp", i) for i in outer]
    packed_a, column = lax.optimization_barrier((pack(chunk_a, half), column))
    spread_a, packed_b, packed_c = lax.optimization_barrier(
        (spread_out(packed_a), pack(chunk_b, half), pack(chunk_c, half))
    )
    rows = lay(column)

    arrived_a = lax.ppermute(leave(spread_a), "exp", across)
    spread_b, packed_c = lax.optimization_barrier((spread_out(packed_b), packed_c))
    sent_b = leave(spread_b)
    spread_c = spread_out(packed_c)
    steps = range(0, inner, 2)
    blocks = [flip(rows, "exp", i) for i in steps]
    weights = [full_in, full_out, flip(full_in, "exp", 1), flip(full_out, "exp", 1)]
    arrived_a, sent_b, blocks = lax.optimization_barrier((arrived_a, sent_b, blocks))

    extra_a, extra_b = beyond(spread_a, spread_b)
    arrived_b = lax.ppermute(sent_b, "exp", across)
    landed_a = exchange(stay(spread_a, arrived_a, extra_a), devices)
    me = lax.axis_index("exp").astype(jnp.int32)
    first = jnp.stack([me, me ^ 1]) * slots
    parts = [experts(x, first, weights) for x in blocks]
    arrived_b, sent_c, parts = lax.optimization_barrier((arrived_b, leave(spread_c), parts))

    (extra_c,) = beyond(spread_c)
    arrived_c = lax.ppermute(sent_c, "exp", across)
    landed_b = exchange(stay(spread_b, arrived_b, extra_b), devices)
    partial = add_up([flip(x, "exp", i) for i, x in zip(steps, parts)])
    arrived_c, partial = lax.optimization_barrier((arrived_c, partial))

    landed_b, picked_c = lax.optimization_barrier(
        (landed_b, stay(spread_c, arrived_c, extra_c))
    )
    landed_c = exchange(picked_c, devices)
    size = tokens.shape[0]
    pieces = [partial[n * size : (n + 1) * size] for n in range(len(outer))]
    outs_a, pieces[1] = lax.optimization_barrier((unpack(landed_a, chunk_a), pieces[1]))
    mixed = add_up([flip(x, "exp", i) for i, x in zip(outer, pieces)])
    new_w_in, new_w_out = outs_a
    (new_moments_in,) = unpack(landed_b, chunk_b)
    (new_moments_out,) = unpack(landed_c, chunk_c)
    return mixed, new_w_in, new_w_out, new_moments_in, new_moments_out


def solution(mesh):
    return jax.shard_map(
        on_device,
        mesh=mesh,
        in_specs=(
            P(("grp", "exp"), None),
            P("exp", "grp", None),
            P("exp", "grp", None),
            P("exp", None, "grp", None),
            P("exp", None, "grp", None),
            P(("grp", "exp"), None),
            P(("grp", "exp"), None),
            P(),
            P(),
        ),
        out_specs=(
            P(("grp", "exp"), None),
            P("exp", "grp", None),
            P("exp", "grp", None),
            P("exp", None, "grp", None),
            P("exp", None, "grp", None),
        ),
        check_vma=False,
    )
```

```python
import jax
import jax.numpy as jnp
from jax import lax
from jax.experimental import pallas as pl
from jax.experimental.pallas import tpu as pltpu
from jax.sharding import PartitionSpec as P

SUB = 8
LANE = 128
FIXED = 9


def to_tiles(x):
    slots, columns = x.shape[0], x.shape[-1]
    x = x.reshape(slots, -1, SUB, columns // LANE, LANE)
    return x.swapaxes(2, 3).reshape(slots, -1, SUB, LANE)


def from_tiles(x, shape):
    columns = shape[-1]
    x = x.reshape(shape[0], -1, columns // LANE, SUB, LANE)
    return x.swapaxes(2, 3).reshape(shape)


def in_parts(tiles, parts):
    return tiles.reshape(tiles.shape[0], parts, -1, SUB, LANE).swapaxes(0, 1)


def pack(arrays, parts):
    tiles = [to_tiles(a) for a in arrays]
    if all(t.shape[1] % parts == 0 for t in tiles):
        return jnp.concatenate([in_parts(t, parts) for t in tiles], axis=2)
    slots = tiles[0].shape[0]
    extra = -sum(t.shape[1] for t in tiles) % parts
    tiles.append(jnp.zeros((slots, extra, SUB, LANE), tiles[0].dtype))
    return in_parts(jnp.concatenate(tiles, axis=1), parts)


def unpack(landed, arrays):
    parts, slots = landed.shape[:2]
    counts = [a.size // (slots * SUB * LANE) for a in arrays]
    whole = all(count % parts == 0 for count in counts)
    if not whole:
        landed = landed.swapaxes(0, 1).reshape(slots, -1, SUB, LANE)
    outs, at = [], 0
    for a, count in zip(arrays, counts):
        if whole:
            part = landed[:, :, at // parts : (at + count) // parts].swapaxes(0, 1)
            outs.append(from_tiles(part.reshape(slots, count, SUB, LANE), a.shape))
        else:
            outs.append(from_tiles(landed[:, at : at + count], a.shape))
        at += count
    return outs


def pick_kernel(index_ref, *refs):
    *tables, out_ref, rows, in_sems, out_sems = refs
    count = out_ref.shape[0]
    for d in range(count):
        i = index_ref[d]
        low = 0
        for table in tables:
            size = table.shape[0]

            @pl.when((i >= low) & (i < low + size))
            def _(table=table, low=low):
                pltpu.make_async_copy(table.at[i - low], rows.at[d], in_sems.at[d]).start()

            low += size
    for d in range(count):
        pltpu.make_async_copy(tables[0].at[0], rows.at[d], in_sems.at[d]).wait()
        pltpu.make_async_copy(rows.at[d], out_ref.at[d], out_sems.at[d]).start()
    for d in range(count):
        pltpu.make_async_copy(rows.at[d], out_ref.at[d], out_sems.at[d]).wait()


def pick(index, *tables):
    count = index.shape[0]
    shape = (count,) + tables[0].shape[1:]
    return pl.pallas_call(
        pick_kernel,
        in_specs=[pl.BlockSpec(memory_space=pltpu.SMEM)]
        + [pl.BlockSpec(memory_space=pl.ANY)] * len(tables),
        out_specs=pl.BlockSpec(memory_space=pl.ANY),
        out_shape=jax.ShapeDtypeStruct(shape, tables[0].dtype),
        scratch_shapes=[
            pltpu.VMEM(shape, tables[0].dtype),
            pltpu.SemaphoreType.DMA((count,)),
            pltpu.SemaphoreType.DMA((count,)),
        ],
        compiler_params=pltpu.CompilerParams(vmem_limit_bytes=16 * 1024 * 1024),
        cost_estimate=pl.CostEstimate(flops=0, bytes_accessed=0, transcendentals=0),
    )(index, *tables)


def lay(blocks):
    laid = pick(jnp.arange(len(blocks), dtype=jnp.int32), *(x[None] for x in blocks))
    return laid.reshape((-1,) + blocks[0].shape[1:])


def expert_kernel(first_ref, x_ref, *refs):
    *weight_refs, out_ref = refs
    width = out_ref.shape[1]
    half = (x_ref.shape[1] - width) // 2
    x = x_ref[:, :width]
    weights = x_ref[:, width:].astype(jnp.float32)
    lane = lax.broadcasted_iota(jnp.int32, weights.shape, 1)
    total = jnp.zeros(out_ref.shape, jnp.float32)
    for n in range(len(weight_refs) // 2):
        w_in_ref, w_out_ref = weight_refs[2 * n : 2 * n + 2]
        hidden_size = w_out_ref.shape[1]
        for j in range(w_in_ref.shape[0]):
            both = jnp.dot(x, w_in_ref[j], preferred_element_type=jnp.float32)
            gate, up = both[:, :hidden_size], both[:, hidden_size:]
            hidden = (gate / (1.0 + jnp.exp(-gate)) * up).astype(jnp.bfloat16)
            result = jnp.dot(hidden, w_out_ref[j], preferred_element_type=jnp.float32)
            result = result.astype(jnp.bfloat16).astype(jnp.float32)
            at = first_ref[n] + j
            mine = (lane == at) | (lane == at + half)
            weight = jnp.sum(jnp.where(mine, weights, 0.0), axis=1, keepdims=True)
            total = total + weight * result
    out_ref[...] = total.astype(out_ref.dtype)


def experts(x, first, weights):
    rows, columns = x.shape
    width = weights[0].shape[1]
    block = 256 if rows % 256 == 0 else rows
    return pl.pallas_call(
        expert_kernel,
        grid=(rows // block,),
        in_specs=[
            pl.BlockSpec(memory_space=pltpu.SMEM),
            pl.BlockSpec((block, columns), lambda i: (i, 0)),
        ]
        + [pl.BlockSpec(w.shape, lambda i: (0, 0, 0)) for w in weights],
        out_specs=pl.BlockSpec((block, width), lambda i: (i, 0)),
        out_shape=jax.ShapeDtypeStruct((rows, width), jnp.bfloat16),
        compiler_params=pltpu.CompilerParams(vmem_limit_bytes=40 * 1024 * 1024),
        cost_estimate=pl.CostEstimate(flops=0, bytes_accessed=0, transcendentals=0),
    )(first, x, *weights)


def plane_size(devices):
    size = 1
    while 4 * size * size <= devices:
        size *= 2
    return size


def swap(x, axis, groups=None):
    return lax.all_to_all(
        x, axis, split_axis=0, concat_axis=0, axis_index_groups=groups, tiled=True
    )


def flip(x, axis, bits):
    if bits == 0:
        return x
    return lax.ppermute(x, axis, [(d, d ^ bits) for d in range(lax.axis_size(axis))])


def add_up(blocks):
    return sum(x.astype(jnp.float32) for x in blocks).astype(jnp.bfloat16)


def weighted_rows(tokens, expert_ids, route_weights, old_plan):
    slot_count = old_plan.shape[0]
    slot_index = jnp.arange(slot_count, dtype=jnp.int32)
    share = route_weights / jnp.sum(route_weights, axis=1, keepdims=True)
    earlier = (old_plan[None, :] == old_plan[:, None]) & (slot_index[None, :] < slot_index[:, None])
    is_first = ~jnp.any(earlier, axis=1)
    chosen = (expert_ids[:, :, None] == old_plan[None, None, :]) & is_first[None, None, :]
    weight = jnp.sum(jnp.where(chosen, share[:, :, None], 0.0), axis=1)
    high = lax.reduce_precision(weight, exponent_bits=8, mantissa_bits=7)
    half = -(-2 * slot_count // LANE) * LANE // 2
    pad = jnp.zeros((tokens.shape[0], half - slot_count), jnp.bfloat16)
    return jnp.concatenate(
        [tokens, high.astype(jnp.bfloat16), pad, (weight - high).astype(jnp.bfloat16), pad], axis=1
    )


def crossing(old_plan, new_plan):
    slot_count = old_plan.shape[0]
    held = slot_count // 2
    slot_index = jnp.arange(slot_count, dtype=jnp.int32)
    same_expert = new_plan[:, None] == old_plan[None, :]
    source = jnp.min(jnp.where(same_expert, slot_index[None, :], slot_count), axis=1)
    apart = slot_index[:, None] // held != slot_index[None, :] // held
    cross = jnp.any((source[:, None] == slot_index[None, :]) & apart, axis=0)
    before = (~apart) & (slot_index[:, None] < slot_index[None, :])
    rank = jnp.sum((before & cross[:, None]).astype(jnp.int32), axis=0)
    number = jnp.max(jnp.where(cross, rank + 1, 0))
    return source, cross, rank, number


def exchange(x, devices):
    half = devices // 2
    return swap(x, "exp", [list(range(half)), list(range(half, devices))])


def places(plan, held, most):
    source, cross, rank = plan
    mine = lax.axis_index("exp") * 2 // lax.axis_size("exp")
    local = jnp.arange(held, dtype=jnp.int32)
    leaving = lax.dynamic_slice_in_dim(cross, mine * held, held)
    ranking = lax.dynamic_slice_in_dim(rank, mine * held, held)
    place = jnp.arange(most, dtype=jnp.int32)
    matches = leaving[None, :] & (ranking[None, :] == place[:, None])
    sent_index = jnp.sum(jnp.where(matches, local[None, :], 0), axis=1)
    wanted = lax.dynamic_slice_in_dim(source, mine * held, held)
    here = wanted // held == mine
    far = jnp.arange(source.shape[0], dtype=jnp.int32)[None, :] == wanted[:, None]
    far_rank = jnp.sum(jnp.where(far, rank[None, :], 0), axis=1)
    return sent_index, jnp.where(here, wanted - mine * held, held + far_rank)


def on_device(
    tokens, w_in, w_out, moments_in, moments_out, expert_ids, route_weights, old_plan, new_plan
):
    devices = lax.axis_size("exp")
    half = devices // 2
    slots = w_in.shape[0]
    held = half * slots
    chunk_a, chunk_b = (w_in, w_out, moments_out), (moments_in,)
    full_in = lax.all_gather(w_in, "grp", axis=1, tiled=True)
    full_out = lax.all_gather(w_out, "grp", axis=1, tiled=True)

    rows = weighted_rows(tokens, expert_ids, route_weights, old_plan)
    inner = plane_size(devices)
    outer = range(0, devices, inner)
    column = [flip(rows, "exp", i) for i in outer]
    packed_a, column = lax.optimization_barrier((pack(chunk_a, half), column))
    spread_a = exchange(packed_a, devices).reshape((held,) + packed_a.shape[2:])
    rows = lay(column)

    *plan, number = crossing(old_plan, new_plan)
    most = -(-held * FIXED // 16)
    sent_index, index = places(plan, held, held)
    across = [(d, (d + half) % devices) for d in range(devices)]

    sent_a = pick(sent_index[:most], spread_a)
    arrived_a = lax.ppermute(sent_a, "exp", across)
    packed_b = pack(chunk_b, half)
    spread_b = exchange(packed_b, devices).reshape((held,) + packed_b.shape[2:])
    sent_b = pick(sent_index[:most], spread_b)
    steps = range(0, inner, 2)
    blocks = [flip(rows, "exp", i) for i in steps]
    weights = [full_in, full_out, flip(full_in, "exp", 1), flip(full_out, "exp", 1)]
    me = lax.axis_index("exp").astype(jnp.int32)
    first = jnp.stack([me, me ^ 1]) * slots
    blocks[1:], sent_b = lax.optimization_barrier((blocks[1:], sent_b))
    parts = [experts(x, first, weights) for x in blocks]

    def more(state):
        place, *extra = state
        at = lax.dynamic_index_in_dim(sent_index, place, keepdims=False)
        out = []
        for spread, table in zip((spread_a, spread_b), extra):
            row = lax.dynamic_slice_in_dim(spread, at, 1, axis=0)
            row = lax.ppermute(row, "exp", across)
            out.append(lax.dynamic_update_slice_in_dim(table, row, place - most, axis=0))
        return place + 1, *out

    extra = [
        jnp.zeros((max(held - most, 1),) + x.shape[1:], x.dtype) for x in (spread_a, spread_b)
    ]
    arrived_a, sent_b, parts, extra = lax.optimization_barrier((arrived_a, sent_b, parts, extra))
    _, *extra = lax.while_loop(
        lambda state: state[0] < number, more, (jnp.int32(most), *extra)
    )

    arrived_b = lax.ppermute(sent_b, "exp", across)
    picked_a = pick(index, spread_a, arrived_a, extra[0])
    landed_a = exchange(picked_a.reshape(packed_a.shape), devices)
    partial = add_up([flip(x, "exp", i) for i, x in zip(steps, parts)])
    arrived_b, partial = lax.optimization_barrier((arrived_b, partial))

    picked_b = pick(index, spread_b, arrived_b, extra[1])
    (new_moments_in,) = unpack(exchange(picked_b.reshape(packed_b.shape), devices), chunk_b)
    size = tokens.shape[0]
    pieces = [partial[n * size : (n + 1) * size] for n in range(len(outer))]
    outs_a, pieces[1] = lax.optimization_barrier((unpack(landed_a, chunk_a), pieces[1]))
    new_w_in, new_w_out, new_moments_out = outs_a
    mixed = add_up([flip(x, "exp", i) for i, x in zip(outer, pieces)])
    return mixed, new_w_in, new_w_out, new_moments_in, new_moments_out


def solution(mesh):
    return jax.shard_map(
        on_device,
        mesh=mesh,
        in_specs=(
            P(("grp", "exp"), None),
            P("exp", "grp", None),
            P("exp", "grp", None),
            P("exp", None, "grp", None),
            P("exp", None, "grp", None),
            P(("grp", "exp"), None),
            P(("grp", "exp"), None),
            P(),
            P(),
        ),
        out_specs=(
            P(("grp", "exp"), None),
            P("exp", "grp", None),
            P("exp", "grp", None),
            P("exp", None, "grp", None),
            P("exp", None, "grp", None),
        ),
        check_vma=False,
    )
```

```python
import jax
import jax.numpy as jnp
from jax import lax
from jax.experimental import pallas as pl
from jax.experimental.pallas import tpu as pltpu
from jax.sharding import PartitionSpec as P

SUB = 8
LANE = 128
FIXED = 9


def to_tiles(x):
    slots, columns = x.shape[0], x.shape[-1]
    x = x.reshape(slots, -1, SUB, columns // LANE, LANE)
    return x.swapaxes(2, 3).reshape(slots, -1, SUB, LANE)


def from_tiles(x, shape):
    columns = shape[-1]
    x = x.reshape(shape[0], -1, columns // LANE, SUB, LANE)
    return x.swapaxes(2, 3).reshape(shape)


def in_parts(tiles, parts):
    return tiles.reshape(tiles.shape[0], parts, -1, SUB, LANE).swapaxes(0, 1)


def pack(arrays, parts):
    tiles = [to_tiles(a) for a in arrays]
    if all(t.shape[1] % parts == 0 for t in tiles):
        return jnp.concatenate([in_parts(t, parts) for t in tiles], axis=2)
    slots = tiles[0].shape[0]
    extra = -sum(t.shape[1] for t in tiles) % parts
    tiles.append(jnp.zeros((slots, extra, SUB, LANE), tiles[0].dtype))
    return in_parts(jnp.concatenate(tiles, axis=1), parts)


def unpack(landed, arrays):
    parts, slots = landed.shape[:2]
    counts = [a.size // (slots * SUB * LANE) for a in arrays]
    whole = all(count % parts == 0 for count in counts)
    if not whole:
        landed = landed.swapaxes(0, 1).reshape(slots, -1, SUB, LANE)
    outs, at = [], 0
    for a, count in zip(arrays, counts):
        if whole:
            part = landed[:, :, at // parts : (at + count) // parts].swapaxes(0, 1)
            outs.append(from_tiles(part.reshape(slots, count, SUB, LANE), a.shape))
        else:
            outs.append(from_tiles(landed[:, at : at + count], a.shape))
        at += count
    return outs


def pick_kernel(index_ref, *refs):
    *tables, out_ref, sems = refs
    count = out_ref.shape[0]
    for d in range(count):
        i = index_ref[d]
        low = 0
        for table in tables:
            size = table.shape[0]

            @pl.when((i >= low) & (i < low + size))
            def _(table=table, low=low):
                pltpu.make_async_copy(table.at[i - low], out_ref.at[d], sems.at[d]).start()

            low += size
    for d in range(count):
        pltpu.make_async_copy(tables[0].at[0], out_ref.at[d], sems.at[d]).wait()


def pick(index, *tables):
    count = index.shape[0]
    shape = (count,) + tables[0].shape[1:]
    return pl.pallas_call(
        pick_kernel,
        in_specs=[pl.BlockSpec(memory_space=pltpu.SMEM)]
        + [pl.BlockSpec(memory_space=pl.ANY)] * len(tables),
        out_specs=pl.BlockSpec(memory_space=pltpu.VMEM),
        out_shape=jax.ShapeDtypeStruct(shape, tables[0].dtype),
        scratch_shapes=[pltpu.SemaphoreType.DMA((count,))],
        compiler_params=pltpu.CompilerParams(vmem_limit_bytes=16 * 1024 * 1024),
        cost_estimate=pl.CostEstimate(flops=0, bytes_accessed=0, transcendentals=0),
    )(index, *tables)


def lay(blocks):
    laid = pick(jnp.arange(len(blocks), dtype=jnp.int32), *(x[None] for x in blocks))
    return laid.reshape((-1,) + blocks[0].shape[1:])


def expert_kernel(first_ref, x_ref, *refs):
    *weight_refs, out_ref = refs
    width = out_ref.shape[1]
    half = (x_ref.shape[1] - width) // 2
    x = x_ref[:, :width]
    weights = x_ref[:, width:].astype(jnp.float32)
    lane = lax.broadcasted_iota(jnp.int32, weights.shape, 1)
    total = jnp.zeros(out_ref.shape, jnp.float32)
    for n in range(len(weight_refs) // 2):
        w_in_ref, w_out_ref = weight_refs[2 * n : 2 * n + 2]
        hidden_size = w_out_ref.shape[1]
        for j in range(w_in_ref.shape[0]):
            both = jnp.dot(x, w_in_ref[j], preferred_element_type=jnp.float32)
            gate, up = both[:, :hidden_size], both[:, hidden_size:]
            hidden = (gate / (1.0 + jnp.exp(-gate)) * up).astype(jnp.bfloat16)
            result = jnp.dot(hidden, w_out_ref[j], preferred_element_type=jnp.float32)
            result = result.astype(jnp.bfloat16).astype(jnp.float32)
            at = first_ref[n] + j
            mine = (lane == at) | (lane == at + half)
            weight = jnp.sum(jnp.where(mine, weights, 0.0), axis=1, keepdims=True)
            total = total + weight * result
    out_ref[...] = total.astype(out_ref.dtype)


def experts(x, first, weights):
    rows, columns = x.shape
    width = weights[0].shape[1]
    block = 256 if rows % 256 == 0 else rows
    return pl.pallas_call(
        expert_kernel,
        grid=(rows // block,),
        in_specs=[
            pl.BlockSpec(memory_space=pltpu.SMEM),
            pl.BlockSpec((block, columns), lambda i: (i, 0)),
        ]
        + [pl.BlockSpec(w.shape, lambda i: (0, 0, 0)) for w in weights],
        out_specs=pl.BlockSpec((block, width), lambda i: (i, 0)),
        out_shape=jax.ShapeDtypeStruct((rows, width), jnp.bfloat16),
        compiler_params=pltpu.CompilerParams(vmem_limit_bytes=40 * 1024 * 1024),
        cost_estimate=pl.CostEstimate(flops=0, bytes_accessed=0, transcendentals=0),
    )(first, x, *weights)


def plane_size(devices):
    size = 1
    while 4 * size * size <= devices:
        size *= 2
    return size


def swap(x, axis, groups=None):
    return lax.all_to_all(
        x, axis, split_axis=0, concat_axis=0, axis_index_groups=groups, tiled=True
    )


def flip(x, axis, bits):
    if bits == 0:
        return x
    return lax.ppermute(x, axis, [(d, d ^ bits) for d in range(lax.axis_size(axis))])


def add_up(blocks):
    return sum(x.astype(jnp.float32) for x in blocks).astype(jnp.bfloat16)


def weighted_rows(tokens, expert_ids, route_weights, old_plan):
    slot_count = old_plan.shape[0]
    slot_index = jnp.arange(slot_count, dtype=jnp.int32)
    share = route_weights / jnp.sum(route_weights, axis=1, keepdims=True)
    earlier = (old_plan[None, :] == old_plan[:, None]) & (slot_index[None, :] < slot_index[:, None])
    is_first = ~jnp.any(earlier, axis=1)
    chosen = (expert_ids[:, :, None] == old_plan[None, None, :]) & is_first[None, None, :]
    weight = jnp.sum(jnp.where(chosen, share[:, :, None], 0.0), axis=1)
    high = lax.reduce_precision(weight, exponent_bits=8, mantissa_bits=7)
    half = -(-2 * slot_count // LANE) * LANE // 2
    pad = jnp.zeros((tokens.shape[0], half - slot_count), jnp.bfloat16)
    return jnp.concatenate(
        [tokens, high.astype(jnp.bfloat16), pad, (weight - high).astype(jnp.bfloat16), pad], axis=1
    )


def crossing(old_plan, new_plan):
    slot_count = old_plan.shape[0]
    held = slot_count // 2
    slot_index = jnp.arange(slot_count, dtype=jnp.int32)
    same_expert = new_plan[:, None] == old_plan[None, :]
    source = jnp.min(jnp.where(same_expert, slot_index[None, :], slot_count), axis=1)
    apart = slot_index[:, None] // held != slot_index[None, :] // held
    cross = jnp.any((source[:, None] == slot_index[None, :]) & apart, axis=0)
    before = (~apart) & (slot_index[:, None] < slot_index[None, :])
    rank = jnp.sum((before & cross[:, None]).astype(jnp.int32), axis=0)
    number = jnp.max(jnp.where(cross, rank + 1, 0))
    return source, cross, rank, number


def exchange(x, devices):
    half = devices // 2
    return swap(x, "exp", [list(range(half)), list(range(half, devices))])


def places(plan, held, most):
    source, cross, rank = plan
    mine = lax.axis_index("exp") * 2 // lax.axis_size("exp")
    local = jnp.arange(held, dtype=jnp.int32)
    leaving = lax.dynamic_slice_in_dim(cross, mine * held, held)
    ranking = lax.dynamic_slice_in_dim(rank, mine * held, held)
    place = jnp.arange(most, dtype=jnp.int32)
    matches = leaving[None, :] & (ranking[None, :] == place[:, None])
    sent_index = jnp.sum(jnp.where(matches, local[None, :], 0), axis=1)
    wanted = lax.dynamic_slice_in_dim(source, mine * held, held)
    here = wanted // held == mine
    far = jnp.arange(source.shape[0], dtype=jnp.int32)[None, :] == wanted[:, None]
    far_rank = jnp.sum(jnp.where(far, rank[None, :], 0), axis=1)
    return sent_index, jnp.where(here, wanted - mine * held, held + far_rank)


def on_device(
    tokens, w_in, w_out, moments_in, moments_out, expert_ids, route_weights, old_plan, new_plan
):
    devices = lax.axis_size("exp")
    half = devices // 2
    slots = w_in.shape[0]
    held = half * slots
    chunk_a, chunk_b = (w_in, w_out, moments_out), (moments_in,)
    full_in = lax.all_gather(w_in, "grp", axis=1, tiled=True)
    full_out = lax.all_gather(w_out, "grp", axis=1, tiled=True)

    rows = weighted_rows(tokens, expert_ids, route_weights, old_plan)
    inner = plane_size(devices)
    outer = range(0, devices, inner)
    column = [flip(rows, "exp", i) for i in outer]
    packed_a, column = lax.optimization_barrier((pack(chunk_a, half), column))
    spread_a = exchange(packed_a, devices).reshape((held,) + packed_a.shape[2:])
    rows = lay(column)

    *plan, number = crossing(old_plan, new_plan)
    most = -(-held * FIXED // 16)
    sent_index, index = places(plan, held, held)
    across = [(d, (d + half) % devices) for d in range(devices)]

    sent_a = pick(sent_index[:most], spread_a)
    arrived_a = lax.ppermute(sent_a, "exp", across)
    packed_b = pack(chunk_b, half)
    spread_b = exchange(packed_b, devices).reshape((held,) + packed_b.shape[2:])
    sent_b = pick(sent_index[:most], spread_b)
    steps = range(0, inner, 2)
    blocks = [flip(rows, "exp", i) for i in steps]
    weights = [full_in, full_out, flip(full_in, "exp", 1), flip(full_out, "exp", 1)]
    me = lax.axis_index("exp").astype(jnp.int32)
    first = jnp.stack([me, me ^ 1]) * slots
    blocks[1:], sent_b = lax.optimization_barrier((blocks[1:], sent_b))
    parts = [experts(x, first, weights) for x in blocks]

    def more(state):
        place, *extra = state
        at = lax.dynamic_index_in_dim(sent_index, place, keepdims=False)
        out = []
        for spread, table in zip((spread_a, spread_b), extra):
            row = lax.dynamic_slice_in_dim(spread, at, 1, axis=0)
            row = lax.ppermute(row, "exp", across)
            out.append(lax.dynamic_update_slice_in_dim(table, row, place - most, axis=0))
        return place + 1, *out

    extra = [x[: max(held - most, 1)] for x in (spread_a, spread_b)]
    arrived_a, sent_b, parts, extra = lax.optimization_barrier((arrived_a, sent_b, parts, extra))
    _, *extra = lax.while_loop(
        lambda state: state[0] < number, more, (jnp.int32(most), *extra)
    )

    arrived_b = lax.ppermute(sent_b, "exp", across)
    picked_a = pick(index, spread_a, arrived_a, extra[0])
    landed_a = exchange(picked_a.reshape(packed_a.shape), devices)
    partial = add_up([flip(x, "exp", i) for i, x in zip(steps, parts)])
    arrived_b, partial = lax.optimization_barrier((arrived_b, partial))

    picked_b = pick(index, spread_b, arrived_b, extra[1])
    (new_moments_in,) = unpack(exchange(picked_b.reshape(packed_b.shape), devices), chunk_b)
    size = tokens.shape[0]
    pieces = [partial[n * size : (n + 1) * size] for n in range(len(outer))]
    outs_a, pieces[1] = lax.optimization_barrier((unpack(landed_a, chunk_a), pieces[1]))
    new_w_in, new_w_out, new_moments_out = outs_a
    mixed = add_up([flip(x, "exp", i) for i, x in zip(outer, pieces)])
    return mixed, new_w_in, new_w_out, new_moments_in, new_moments_out


def solution(mesh):
    return jax.shard_map(
        on_device,
        mesh=mesh,
        in_specs=(
            P(("grp", "exp"), None),
            P("exp", "grp", None),
            P("exp", "grp", None),
            P("exp", None, "grp", None),
            P("exp", None, "grp", None),
            P(("grp", "exp"), None),
            P(("grp", "exp"), None),
            P(),
            P(),
        ),
        out_specs=(
            P(("grp", "exp"), None),
            P("exp", "grp", None),
            P("exp", "grp", None),
            P("exp", None, "grp", None),
            P("exp", None, "grp", None),
        ),
        check_vma=False,
    )
```

```python
import jax
import jax.numpy as jnp
from jax import lax
from jax.experimental import pallas as pl
from jax.experimental.pallas import tpu as pltpu
from jax.sharding import PartitionSpec as P

SUB = 8
LANE = 128
FIXED = 8


def to_tiles(x):
    slots, columns = x.shape[0], x.shape[-1]
    x = x.reshape(slots, -1, SUB, columns // LANE, LANE)
    return x.swapaxes(2, 3).reshape(slots, -1, SUB, LANE)


def from_tiles(x, shape):
    columns = shape[-1]
    x = x.reshape(shape[0], -1, columns // LANE, SUB, LANE)
    return x.swapaxes(2, 3).reshape(shape)


def in_parts(tiles, parts):
    return tiles.reshape(tiles.shape[0], parts, -1, SUB, LANE).swapaxes(0, 1)


def pack(arrays, parts):
    tiles = [to_tiles(a) for a in arrays]
    if all(t.shape[1] % parts == 0 for t in tiles):
        return jnp.concatenate([in_parts(t, parts) for t in tiles], axis=2)
    slots = tiles[0].shape[0]
    extra = -sum(t.shape[1] for t in tiles) % parts
    tiles.append(jnp.zeros((slots, extra, SUB, LANE), tiles[0].dtype))
    return in_parts(jnp.concatenate(tiles, axis=1), parts)


def unpack(landed, arrays):
    parts, slots = landed.shape[:2]
    counts = [a.size // (slots * SUB * LANE) for a in arrays]
    whole = all(count % parts == 0 for count in counts)
    if not whole:
        landed = landed.swapaxes(0, 1).reshape(slots, -1, SUB, LANE)
    outs, at = [], 0
    for a, count in zip(arrays, counts):
        if whole:
            part = landed[:, :, at // parts : (at + count) // parts].swapaxes(0, 1)
            outs.append(from_tiles(part.reshape(slots, count, SUB, LANE), a.shape))
        else:
            outs.append(from_tiles(landed[:, at : at + count], a.shape))
        at += count
    return outs


def pick_kernel(index_ref, *refs):
    *tables, out_ref, sems = refs
    count = out_ref.shape[0]
    for d in range(count):
        i = index_ref[d]
        low = 0
        for table in tables:
            size = table.shape[0]

            @pl.when((i >= low) & (i < low + size))
            def _(table=table, low=low):
                pltpu.make_async_copy(table.at[i - low], out_ref.at[d], sems.at[d]).start()

            low += size
    for d in range(count):
        pltpu.make_async_copy(tables[0].at[0], out_ref.at[d], sems.at[d]).wait()


def pick(index, *tables):
    count = index.shape[0]
    shape = (count,) + tables[0].shape[1:]
    return pl.pallas_call(
        pick_kernel,
        in_specs=[pl.BlockSpec(memory_space=pltpu.SMEM)]
        + [pl.BlockSpec(memory_space=pl.ANY)] * len(tables),
        out_specs=pl.BlockSpec(memory_space=pltpu.VMEM),
        out_shape=jax.ShapeDtypeStruct(shape, tables[0].dtype),
        scratch_shapes=[pltpu.SemaphoreType.DMA((count,))],
        compiler_params=pltpu.CompilerParams(vmem_limit_bytes=16 * 1024 * 1024),
        cost_estimate=pl.CostEstimate(flops=0, bytes_accessed=0, transcendentals=0),
    )(index, *tables)


def lay(blocks):
    laid = pick(jnp.arange(len(blocks), dtype=jnp.int32), *(x[None] for x in blocks))
    return laid.reshape((-1,) + blocks[0].shape[1:])


def expert_kernel(first_ref, x_ref, share_ref, *refs):
    *weight_refs, out_ref = refs
    half = share_ref.shape[1] // 2
    x = x_ref[...]
    weights = share_ref[...].astype(jnp.float32)
    lane = lax.broadcasted_iota(jnp.int32, weights.shape, 1)
    total = jnp.zeros(out_ref.shape, jnp.float32)
    for n in range(len(weight_refs) // 2):
        w_in_ref, w_out_ref = weight_refs[2 * n : 2 * n + 2]
        hidden_size = w_out_ref.shape[1]
        for j in range(w_in_ref.shape[0]):
            both = jnp.dot(x, w_in_ref[j], preferred_element_type=jnp.float32)
            gate, up = both[:, :hidden_size], both[:, hidden_size:]
            hidden = (gate / (1.0 + jnp.exp(-gate)) * up).astype(jnp.bfloat16)
            result = jnp.dot(hidden, w_out_ref[j], preferred_element_type=jnp.float32)
            result = result.astype(jnp.bfloat16).astype(jnp.float32)
            at = first_ref[n] + j
            mine = (lane == at) | (lane == at + half)
            weight = jnp.sum(jnp.where(mine, weights, 0.0), axis=1, keepdims=True)
            total = total + weight * result
    out_ref[...] = total.astype(out_ref.dtype)


def experts(x, shares, first, weights):
    rows, width = x.shape
    block = 256 if rows % 256 == 0 else rows
    return pl.pallas_call(
        expert_kernel,
        grid=(rows // block,),
        in_specs=[
            pl.BlockSpec(memory_space=pltpu.SMEM),
            pl.BlockSpec((block, width), lambda i: (i, 0)),
            pl.BlockSpec((block, shares.shape[1]), lambda i: (i, 0)),
        ]
        + [pl.BlockSpec(w.shape, lambda i: (0, 0, 0)) for w in weights],
        out_specs=pl.BlockSpec((block, width), lambda i: (i, 0)),
        out_shape=jax.ShapeDtypeStruct((rows, width), jnp.bfloat16),
        compiler_params=pltpu.CompilerParams(vmem_limit_bytes=40 * 1024 * 1024),
        cost_estimate=pl.CostEstimate(flops=0, bytes_accessed=0, transcendentals=0),
    )(first, x, shares, *weights)


def plane_size(devices):
    size = 1
    while 4 * size * size <= devices:
        size *= 2
    return size


def swap(x, axis, groups=None):
    return lax.all_to_all(
        x, axis, split_axis=0, concat_axis=0, axis_index_groups=groups, tiled=True
    )


def flip(x, axis, bits):
    if bits == 0:
        return x
    return lax.ppermute(x, axis, [(d, d ^ bits) for d in range(lax.axis_size(axis))])


def add_up(blocks):
    return sum(x.astype(jnp.float32) for x in blocks).astype(jnp.bfloat16)


def slot_shares(expert_ids, route_weights, old_plan):
    slot_count = old_plan.shape[0]
    slot_index = jnp.arange(slot_count, dtype=jnp.int32)
    share = route_weights / jnp.sum(route_weights, axis=1, keepdims=True)
    earlier = (old_plan[None, :] == old_plan[:, None]) & (slot_index[None, :] < slot_index[:, None])
    is_first = ~jnp.any(earlier, axis=1)
    chosen = (expert_ids[:, :, None] == old_plan[None, None, :]) & is_first[None, None, :]
    weight = jnp.sum(jnp.where(chosen, share[:, :, None], 0.0), axis=1)
    high = lax.reduce_precision(weight, exponent_bits=8, mantissa_bits=7)
    half = -(-2 * slot_count // LANE) * LANE // 2
    pad = jnp.zeros((weight.shape[0], half - slot_count), jnp.bfloat16)
    return jnp.concatenate(
        [high.astype(jnp.bfloat16), pad, (weight - high).astype(jnp.bfloat16), pad], axis=1
    )


def crossing(old_plan, new_plan):
    slot_count = old_plan.shape[0]
    held = slot_count // 2
    slot_index = jnp.arange(slot_count, dtype=jnp.int32)
    same_expert = new_plan[:, None] == old_plan[None, :]
    source = jnp.min(jnp.where(same_expert, slot_index[None, :], slot_count), axis=1)
    apart = slot_index[:, None] // held != slot_index[None, :] // held
    cross = jnp.any((source[:, None] == slot_index[None, :]) & apart, axis=0)
    before = (~apart) & (slot_index[:, None] < slot_index[None, :])
    rank = jnp.sum((before & cross[:, None]).astype(jnp.int32), axis=0)
    number = jnp.max(jnp.where(cross, rank + 1, 0))
    return source, cross, rank, number


def exchange(x, devices):
    half = devices // 2
    return swap(x, "exp", [list(range(half)), list(range(half, devices))])


def places(plan, held, most):
    source, cross, rank = plan
    mine = lax.axis_index("exp") * 2 // lax.axis_size("exp")
    local = jnp.arange(held, dtype=jnp.int32)
    leaving = lax.dynamic_slice_in_dim(cross, mine * held, held)
    ranking = lax.dynamic_slice_in_dim(rank, mine * held, held)
    place = jnp.arange(most, dtype=jnp.int32)
    matches = leaving[None, :] & (ranking[None, :] == place[:, None])
    sent_index = jnp.sum(jnp.where(matches, local[None, :], 0), axis=1)
    wanted = lax.dynamic_slice_in_dim(source, mine * held, held)
    here = wanted // held == mine
    far = jnp.arange(source.shape[0], dtype=jnp.int32)[None, :] == wanted[:, None]
    far_rank = jnp.sum(jnp.where(far, rank[None, :], 0), axis=1)
    return sent_index, jnp.where(here, wanted - mine * held, held + far_rank)


def on_device(
    tokens, w_in, w_out, moments_in, moments_out, expert_ids, route_weights, old_plan, new_plan
):
    devices = lax.axis_size("exp")
    half = devices // 2
    slots = w_in.shape[0]
    held = half * slots
    chunk_a, chunk_b = (w_in, w_out, moments_out), (moments_in,)
    full_in = lax.all_gather(w_in, "grp", axis=1, tiled=True)
    full_out = lax.all_gather(w_out, "grp", axis=1, tiled=True)

    inner = plane_size(devices)
    outer = range(0, devices, inner)
    column = [flip(tokens, "exp", i) for i in outer]
    shares = {0: slot_shares(expert_ids, route_weights, old_plan)}
    bits = half
    while bits >= inner:
        got = flip(jnp.stack(list(shares.values())), "exp", bits)
        shares.update({at + bits: got[n] for n, at in enumerate(list(shares))})
        bits //= 2
    shares = [shares[i] for i in outer]
    packed_a, column, shares = lax.optimization_barrier((pack(chunk_a, half), column, shares))
    spread_a = exchange(packed_a, devices).reshape((held,) + packed_a.shape[2:])
    rows = [lay(column), lay(shares)]

    *plan, number = crossing(old_plan, new_plan)
    most = -(-held * FIXED // 16)
    sent_index, index = places(plan, held, held)
    across = [(d, (d + half) % devices) for d in range(devices)]

    sent_a = pick(sent_index[:most], spread_a)
    arrived_a = lax.ppermute(sent_a, "exp", across)
    packed_b = pack(chunk_b, half)
    spread_b = exchange(packed_b, devices).reshape((held,) + packed_b.shape[2:])
    sent_b = pick(sent_index[:most], spread_b)
    steps = range(0, inner, 2)
    blocks = [[flip(x, "exp", i) for x in rows] for i in steps]
    blocks[1:], full_out = lax.optimization_barrier((blocks[1:], full_out))
    weights = [full_in, full_out, flip(full_in, "exp", 1), flip(full_out, "exp", 1)]
    me = lax.axis_index("exp").astype(jnp.int32)
    first = jnp.stack([me, me ^ 1]) * slots
    blocks[1:], sent_b = lax.optimization_barrier((blocks[1:], sent_b))
    parts = [experts(*x, first, weights) for x in blocks]

    def more(state):
        place, *extra = state
        at = lax.dynamic_index_in_dim(sent_index, place, keepdims=False)
        out = []
        for spread, table in zip((spread_a, spread_b), extra):
            row = lax.dynamic_slice_in_dim(spread, at, 1, axis=0)
            row = lax.ppermute(row, "exp", across)
            out.append(lax.dynamic_update_slice_in_dim(table, row, place - most, axis=0))
        return place + 1, *out

    extra = [x[: max(held - most, 1)] for x in (spread_a, spread_b)]
    arrived_a, sent_b, parts, extra = lax.optimization_barrier((arrived_a, sent_b, parts, extra))
    _, *extra = lax.while_loop(
        lambda state: state[0] < number, more, (jnp.int32(most), *extra)
    )

    arrived_b = lax.ppermute(sent_b, "exp", across)
    picked_a = pick(index, spread_a, arrived_a, extra[0])
    landed_a = exchange(picked_a.reshape(packed_a.shape), devices)
    partial = add_up([flip(x, "exp", i) for i, x in zip(steps, parts)])
    arrived_b, partial = lax.optimization_barrier((arrived_b, partial))

    picked_b = pick(index, spread_b, arrived_b, extra[1])
    (new_moments_in,) = unpack(exchange(picked_b.reshape(packed_b.shape), devices), chunk_b)
    size = tokens.shape[0]
    pieces = [partial[n * size : (n + 1) * size] for n in range(len(outer))]
    outs_a, pieces[1] = lax.optimization_barrier((unpack(landed_a, chunk_a), pieces[1]))
    new_w_in, new_w_out, new_moments_out = outs_a
    mixed = add_up([flip(x, "exp", i) for i, x in zip(outer, pieces)])
    return mixed, new_w_in, new_w_out, new_moments_in, new_moments_out


def solution(mesh):
    return jax.shard_map(
        on_device,
        mesh=mesh,
        in_specs=(
            P(("grp", "exp"), None),
            P("exp", "grp", None),
            P("exp", "grp", None),
            P("exp", None, "grp", None),
            P("exp", None, "grp", None),
            P(("grp", "exp"), None),
            P(("grp", "exp"), None),
            P(),
            P(),
        ),
        out_specs=(
            P(("grp", "exp"), None),
            P("exp", "grp", None),
            P("exp", "grp", None),
            P("exp", None, "grp", None),
            P("exp", None, "grp", None),
        ),
        check_vma=False,
    )
```

```python
import jax
import jax.numpy as jnp
from jax import lax
from jax.experimental import pallas as pl
from jax.experimental.pallas import tpu as pltpu
from jax.sharding import PartitionSpec as P

SUB = 8
LANE = 128
FIXED = 8


def to_tiles(x):
    slots, columns = x.shape[0], x.shape[-1]
    x = x.reshape(slots, -1, SUB, columns // LANE, LANE)
    return x.swapaxes(2, 3).reshape(slots, -1, SUB, LANE)


def from_tiles(x, shape):
    columns = shape[-1]
    x = x.reshape(shape[0], -1, columns // LANE, SUB, LANE)
    return x.swapaxes(2, 3).reshape(shape)


def in_parts(tiles, parts):
    return tiles.reshape(tiles.shape[0], parts, -1, SUB, LANE).swapaxes(0, 1)


def pack(arrays, parts):
    tiles = [to_tiles(a) for a in arrays]
    if all(t.shape[1] % parts == 0 for t in tiles):
        return jnp.concatenate([in_parts(t, parts) for t in tiles], axis=2)
    slots = tiles[0].shape[0]
    extra = -sum(t.shape[1] for t in tiles) % parts
    tiles.append(jnp.zeros((slots, extra, SUB, LANE), tiles[0].dtype))
    return in_parts(jnp.concatenate(tiles, axis=1), parts)


def unpack(landed, arrays):
    parts, slots = landed.shape[:2]
    counts = [a.size // (slots * SUB * LANE) for a in arrays]
    whole = all(count % parts == 0 for count in counts)
    if not whole:
        landed = landed.swapaxes(0, 1).reshape(slots, -1, SUB, LANE)
    outs, at = [], 0
    for a, count in zip(arrays, counts):
        if whole:
            part = landed[:, :, at // parts : (at + count) // parts].swapaxes(0, 1)
            outs.append(from_tiles(part.reshape(slots, count, SUB, LANE), a.shape))
        else:
            outs.append(from_tiles(landed[:, at : at + count], a.shape))
        at += count
    return outs


def pick_kernel(index_ref, *refs):
    *tables, out_ref, sems = refs
    count = out_ref.shape[0]
    for d in range(count):
        i = index_ref[d]
        low = 0
        for table in tables:
            size = table.shape[0]

            @pl.when((i >= low) & (i < low + size))
            def _(table=table, low=low):
                pltpu.make_async_copy(table.at[i - low], out_ref.at[d], sems.at[d]).start()

            low += size
    for d in range(count):
        pltpu.make_async_copy(tables[0].at[0], out_ref.at[d], sems.at[d]).wait()


def pick(index, *tables):
    count = index.shape[0]
    shape = (count,) + tables[0].shape[1:]
    return pl.pallas_call(
        pick_kernel,
        in_specs=[pl.BlockSpec(memory_space=pltpu.SMEM)]
        + [pl.BlockSpec(memory_space=pl.ANY)] * len(tables),
        out_specs=pl.BlockSpec(memory_space=pltpu.VMEM),
        out_shape=jax.ShapeDtypeStruct(shape, tables[0].dtype),
        scratch_shapes=[pltpu.SemaphoreType.DMA((count,))],
        compiler_params=pltpu.CompilerParams(vmem_limit_bytes=16 * 1024 * 1024),
        cost_estimate=pl.CostEstimate(flops=0, bytes_accessed=0, transcendentals=0),
    )(index, *tables)


def lay(blocks):
    laid = pick(jnp.arange(len(blocks), dtype=jnp.int32), *(x[None] for x in blocks))
    return laid.reshape((-1,) + blocks[0].shape[1:])


def expert_kernel(first_ref, x_ref, share_ref, *refs):
    *weight_refs, out_ref = refs
    half = share_ref.shape[1] // 2
    x = x_ref[...]
    weights = share_ref[...].astype(jnp.float32)
    lane = lax.broadcasted_iota(jnp.int32, weights.shape, 1)
    total = jnp.zeros(out_ref.shape, jnp.float32)
    for n in range(len(weight_refs) // 2):
        w_in_ref, w_out_ref = weight_refs[2 * n : 2 * n + 2]
        hidden_size = w_out_ref.shape[1]
        for j in range(w_in_ref.shape[0]):
            both = jnp.dot(x, w_in_ref[j], preferred_element_type=jnp.float32)
            gate, up = both[:, :hidden_size], both[:, hidden_size:]
            hidden = (gate / (1.0 + jnp.exp(-gate)) * up).astype(jnp.bfloat16)
            result = jnp.dot(hidden, w_out_ref[j], preferred_element_type=jnp.float32)
            result = result.astype(jnp.bfloat16).astype(jnp.float32)
            at = first_ref[n] + j
            mine = (lane == at) | (lane == at + half)
            weight = jnp.sum(jnp.where(mine, weights, 0.0), axis=1, keepdims=True)
            total = total + weight * result
    out_ref[...] = total.astype(out_ref.dtype)


def experts(x, shares, first, weights):
    rows, width = x.shape
    block = 256 if rows % 256 == 0 else rows
    return pl.pallas_call(
        expert_kernel,
        grid=(rows // block,),
        in_specs=[
            pl.BlockSpec(memory_space=pltpu.SMEM),
            pl.BlockSpec((block, width), lambda i: (i, 0)),
            pl.BlockSpec((block, shares.shape[1]), lambda i: (i, 0)),
        ]
        + [pl.BlockSpec(w.shape, lambda i: (0, 0, 0)) for w in weights],
        out_specs=pl.BlockSpec((block, width), lambda i: (i, 0)),
        out_shape=jax.ShapeDtypeStruct((rows, width), jnp.bfloat16),
        compiler_params=pltpu.CompilerParams(vmem_limit_bytes=40 * 1024 * 1024),
        cost_estimate=pl.CostEstimate(flops=0, bytes_accessed=0, transcendentals=0),
    )(first, x, shares, *weights)


def plane_size(devices):
    size = 1
    while 4 * size * size <= devices:
        size *= 2
    return size


def swap(x, axis, groups=None):
    return lax.all_to_all(
        x, axis, split_axis=0, concat_axis=0, axis_index_groups=groups, tiled=True
    )


def flip(x, axis, bits):
    if bits == 0:
        return x
    return lax.ppermute(x, axis, [(d, d ^ bits) for d in range(lax.axis_size(axis))])


def add_up(blocks):
    return sum(x.astype(jnp.float32) for x in blocks).astype(jnp.bfloat16)


def slot_shares(expert_ids, route_weights, old_plan):
    slot_count = old_plan.shape[0]
    slot_index = jnp.arange(slot_count, dtype=jnp.int32)
    share = route_weights / jnp.sum(route_weights, axis=1, keepdims=True)
    earlier = (old_plan[None, :] == old_plan[:, None]) & (slot_index[None, :] < slot_index[:, None])
    is_first = ~jnp.any(earlier, axis=1)
    chosen = (expert_ids[:, :, None] == old_plan[None, None, :]) & is_first[None, None, :]
    weight = jnp.sum(jnp.where(chosen, share[:, :, None], 0.0), axis=1)
    high = lax.reduce_precision(weight, exponent_bits=8, mantissa_bits=7)
    half = -(-2 * slot_count // LANE) * LANE // 2
    pad = jnp.zeros((weight.shape[0], half - slot_count), jnp.bfloat16)
    return jnp.concatenate(
        [high.astype(jnp.bfloat16), pad, (weight - high).astype(jnp.bfloat16), pad], axis=1
    )


def crossing(old_plan, new_plan):
    slot_count = old_plan.shape[0]
    held = slot_count // 2
    slot_index = jnp.arange(slot_count, dtype=jnp.int32)
    same_expert = new_plan[:, None] == old_plan[None, :]
    source = jnp.min(jnp.where(same_expert, slot_index[None, :], slot_count), axis=1)
    apart = slot_index[:, None] // held != slot_index[None, :] // held
    cross = jnp.any((source[:, None] == slot_index[None, :]) & apart, axis=0)
    before = (~apart) & (slot_index[:, None] < slot_index[None, :])
    rank = jnp.sum((before & cross[:, None]).astype(jnp.int32), axis=0)
    number = jnp.max(jnp.where(cross, rank + 1, 0))
    return source, cross, rank, number


def exchange(x, devices):
    half = devices // 2
    return swap(x, "exp", [list(range(half)), list(range(half, devices))])


def places(plan, held, most):
    source, cross, rank = plan
    mine = lax.axis_index("exp") * 2 // lax.axis_size("exp")
    local = jnp.arange(held, dtype=jnp.int32)
    leaving = lax.dynamic_slice_in_dim(cross, mine * held, held)
    ranking = lax.dynamic_slice_in_dim(rank, mine * held, held)
    place = jnp.arange(most, dtype=jnp.int32)
    matches = leaving[None, :] & (ranking[None, :] == place[:, None])
    sent_index = jnp.sum(jnp.where(matches, local[None, :], 0), axis=1)
    wanted = lax.dynamic_slice_in_dim(source, mine * held, held)
    here = wanted // held == mine
    far = jnp.arange(source.shape[0], dtype=jnp.int32)[None, :] == wanted[:, None]
    far_rank = jnp.sum(jnp.where(far, rank[None, :], 0), axis=1)
    return sent_index, jnp.where(here, wanted - mine * held, held + far_rank)


def on_device(
    tokens, w_in, w_out, moments_in, moments_out, expert_ids, route_weights, old_plan, new_plan
):
    devices = lax.axis_size("exp")
    half = devices // 2
    slots = w_in.shape[0]
    held = half * slots
    chunk_a, chunk_b = (w_in, w_out, moments_out), (moments_in,)
    full_in = lax.all_gather(w_in, "grp", axis=1, tiled=True)
    full_out = lax.all_gather(w_out, "grp", axis=1, tiled=True)

    inner = plane_size(devices)
    outer = range(0, devices, inner)
    column = [flip(tokens, "exp", i) for i in outer]
    shares = {0: slot_shares(expert_ids, route_weights, old_plan)}
    bits = inner
    while bits < devices:
        got = flip(jnp.stack(list(shares.values())), "exp", bits)
        shares.update({at + bits: got[n] for n, at in enumerate(list(shares))})
        bits *= 2
    shares = [shares[i] for i in outer]
    packed_a, column[:-1], shares = lax.optimization_barrier(
        (pack(chunk_a, half), column[:-1], shares)
    )
    spread_a = exchange(packed_a, devices).reshape((held,) + packed_a.shape[2:])
    spread_a, column[-1] = lax.optimization_barrier((spread_a, column[-1]))
    rows = [lay(column), lay(shares)]

    *plan, number = crossing(old_plan, new_plan)
    most = -(-held * FIXED // 16)
    sent_index, index = places(plan, held, held)
    across = [(d, (d + half) % devices) for d in range(devices)]

    sent_a = pick(sent_index[:most], spread_a)
    arrived_a = lax.ppermute(sent_a, "exp", across)
    packed_b = pack(chunk_b, half)
    spread_b = exchange(packed_b, devices).reshape((held,) + packed_b.shape[2:])
    sent_b = pick(sent_index[:most], spread_b)
    steps = range(0, inner, 2)
    blocks = [[flip(x, "exp", i) for x in rows] for i in steps]
    blocks[1:], full_out = lax.optimization_barrier((blocks[1:], full_out))
    weights = [full_in, full_out, flip(full_in, "exp", 1), flip(full_out, "exp", 1)]
    me = lax.axis_index("exp").astype(jnp.int32)
    first = jnp.stack([me, me ^ 1]) * slots
    blocks[1:], sent_b = lax.optimization_barrier((blocks[1:], sent_b))
    parts = [experts(*x, first, weights) for x in blocks]

    def more(state):
        place, *extra = state
        at = lax.dynamic_index_in_dim(sent_index, place, keepdims=False)
        out = []
        for spread, table in zip((spread_a, spread_b), extra):
            row = lax.dynamic_slice_in_dim(spread, at, 1, axis=0)
            row = lax.ppermute(row, "exp", across)
            out.append(lax.dynamic_update_slice_in_dim(table, row, place - most, axis=0))
        return place + 1, *out

    extra = [x[: max(held - most, 1)] for x in (spread_a, spread_b)]
    arrived_a, sent_b, parts, extra = lax.optimization_barrier((arrived_a, sent_b, parts, extra))
    _, *extra = lax.while_loop(
        lambda state: state[0] < number, more, (jnp.int32(most), *extra)
    )

    arrived_b = lax.ppermute(sent_b, "exp", across)
    picked_a = pick(index, spread_a, arrived_a, extra[0])
    landed_a = exchange(picked_a.reshape(packed_a.shape), devices)
    partial = add_up([flip(x, "exp", i) for i, x in zip(steps, parts)])
    arrived_b, partial = lax.optimization_barrier((arrived_b, partial))

    picked_b = pick(index, spread_b, arrived_b, extra[1])
    (new_moments_in,) = unpack(exchange(picked_b.reshape(packed_b.shape), devices), chunk_b)
    size = tokens.shape[0]
    pieces = [partial[n * size : (n + 1) * size] for n in range(len(outer))]
    outs_a, pieces[1] = lax.optimization_barrier((unpack(landed_a, chunk_a), pieces[1]))
    new_w_in, new_w_out, new_moments_out = outs_a
    mixed = add_up([flip(x, "exp", i) for i, x in zip(outer, pieces)])
    return mixed, new_w_in, new_w_out, new_moments_in, new_moments_out


def solution(mesh):
    return jax.shard_map(
        on_device,
        mesh=mesh,
        in_specs=(
            P(("grp", "exp"), None),
            P("exp", "grp", None),
            P("exp", "grp", None),
            P("exp", None, "grp", None),
            P("exp", None, "grp", None),
            P(("grp", "exp"), None),
            P(("grp", "exp"), None),
            P(),
            P(),
        ),
        out_specs=(
            P(("grp", "exp"), None),
            P("exp", "grp", None),
            P("exp", "grp", None),
            P("exp", None, "grp", None),
            P("exp", None, "grp", None),
        ),
        check_vma=False,
    )
```

```python
import jax
import jax.numpy as jnp
from jax import lax
from jax.experimental import pallas as pl
from jax.experimental.pallas import tpu as pltpu
from jax.sharding import PartitionSpec as P

SUB = 8
LANE = 128
FIXED = 8


def to_tiles(x):
    slots, columns = x.shape[0], x.shape[-1]
    x = x.reshape(slots, -1, SUB, columns // LANE, LANE)
    return x.swapaxes(2, 3).reshape(slots, -1, SUB, LANE)


def from_tiles(x, shape):
    columns = shape[-1]
    x = x.reshape(shape[0], -1, columns // LANE, SUB, LANE)
    return x.swapaxes(2, 3).reshape(shape)


def in_parts(tiles, parts):
    return tiles.reshape(tiles.shape[0], parts, -1, SUB, LANE).swapaxes(0, 1)


def pack(arrays, parts):
    tiles = [to_tiles(a) for a in arrays]
    if all(t.shape[1] % parts == 0 for t in tiles):
        return jnp.concatenate([in_parts(t, parts) for t in tiles], axis=2)
    slots = tiles[0].shape[0]
    extra = -sum(t.shape[1] for t in tiles) % parts
    tiles.append(jnp.zeros((slots, extra, SUB, LANE), tiles[0].dtype))
    return in_parts(jnp.concatenate(tiles, axis=1), parts)


def unpack(landed, arrays):
    parts, slots = landed.shape[:2]
    counts = [a.size // (slots * SUB * LANE) for a in arrays]
    whole = all(count % parts == 0 for count in counts)
    if not whole:
        landed = landed.swapaxes(0, 1).reshape(slots, -1, SUB, LANE)
    outs, at = [], 0
    for a, count in zip(arrays, counts):
        if whole:
            part = landed[:, :, at // parts : (at + count) // parts].swapaxes(0, 1)
            outs.append(from_tiles(part.reshape(slots, count, SUB, LANE), a.shape))
        else:
            outs.append(from_tiles(landed[:, at : at + count], a.shape))
        at += count
    return outs


def pick_kernel(index_ref, *refs):
    *tables, out_ref, sems = refs
    count = out_ref.shape[0]
    for d in range(count):
        i = index_ref[d]
        low = 0
        for table in tables:
            size = table.shape[0]

            @pl.when((i >= low) & (i < low + size))
            def _(table=table, low=low):
                pltpu.make_async_copy(table.at[i - low], out_ref.at[d], sems.at[d]).start()

            low += size
    for d in range(count):
        pltpu.make_async_copy(tables[0].at[0], out_ref.at[d], sems.at[d]).wait()


def pick(index, *tables):
    count = index.shape[0]
    shape = (count,) + tables[0].shape[1:]
    return pl.pallas_call(
        pick_kernel,
        in_specs=[pl.BlockSpec(memory_space=pltpu.SMEM)]
        + [pl.BlockSpec(memory_space=pl.ANY)] * len(tables),
        out_specs=pl.BlockSpec(memory_space=pltpu.VMEM),
        out_shape=jax.ShapeDtypeStruct(shape, tables[0].dtype),
        scratch_shapes=[pltpu.SemaphoreType.DMA((count,))],
        compiler_params=pltpu.CompilerParams(vmem_limit_bytes=16 * 1024 * 1024),
        cost_estimate=pl.CostEstimate(flops=0, bytes_accessed=0, transcendentals=0),
    )(index, *tables)


def lay(blocks):
    laid = pick(jnp.arange(len(blocks), dtype=jnp.int32), *(x[None] for x in blocks))
    return laid.reshape((-1,) + blocks[0].shape[1:])


def expert_kernel(first_ref, x_ref, share_ref, *refs):
    *weight_refs, out_ref = refs
    half = share_ref.shape[1] // 2
    x = x_ref[...]
    weights = share_ref[...].astype(jnp.float32)
    lane = lax.broadcasted_iota(jnp.int32, weights.shape, 1)
    total = jnp.zeros(out_ref.shape, jnp.float32)
    for n in range(len(weight_refs) // 2):
        w_in_ref, w_out_ref = weight_refs[2 * n : 2 * n + 2]
        hidden_size = w_out_ref.shape[1]
        for j in range(w_in_ref.shape[0]):
            both = jnp.dot(x, w_in_ref[j], preferred_element_type=jnp.float32)
            gate, up = both[:, :hidden_size], both[:, hidden_size:]
            hidden = (gate / (1.0 + jnp.exp(-gate)) * up).astype(jnp.bfloat16)
            result = jnp.dot(hidden, w_out_ref[j], preferred_element_type=jnp.float32)
            result = result.astype(jnp.bfloat16).astype(jnp.float32)
            at = first_ref[n] + j
            mine = (lane == at) | (lane == at + half)
            weight = jnp.sum(jnp.where(mine, weights, 0.0), axis=1, keepdims=True)
            total = total + weight * result
    out_ref[...] = total.astype(out_ref.dtype)


def experts(x, shares, first, weights):
    rows, width = x.shape
    block = 256 if rows % 256 == 0 else rows
    return pl.pallas_call(
        expert_kernel,
        grid=(rows // block,),
        in_specs=[
            pl.BlockSpec(memory_space=pltpu.SMEM),
            pl.BlockSpec((block, width), lambda i: (i, 0)),
            pl.BlockSpec((block, shares.shape[1]), lambda i: (i, 0)),
        ]
        + [pl.BlockSpec(w.shape, lambda i: (0, 0, 0)) for w in weights],
        out_specs=pl.BlockSpec((block, width), lambda i: (i, 0)),
        out_shape=jax.ShapeDtypeStruct((rows, width), jnp.bfloat16),
        compiler_params=pltpu.CompilerParams(vmem_limit_bytes=40 * 1024 * 1024),
        cost_estimate=pl.CostEstimate(flops=0, bytes_accessed=0, transcendentals=0),
    )(first, x, shares, *weights)


def plane_size(devices):
    size = 1
    while 4 * size * size <= devices:
        size *= 2
    return size


def swap(x, axis, groups=None):
    return lax.all_to_all(
        x, axis, split_axis=0, concat_axis=0, axis_index_groups=groups, tiled=True
    )


def flip(x, axis, bits):
    if bits == 0:
        return x
    return lax.ppermute(x, axis, [(d, d ^ bits) for d in range(lax.axis_size(axis))])


def add_up(blocks):
    return sum(x.astype(jnp.float32) for x in blocks).astype(jnp.bfloat16)


def slot_shares(expert_ids, route_weights, old_plan):
    slot_count = old_plan.shape[0]
    slot_index = jnp.arange(slot_count, dtype=jnp.int32)
    share = route_weights / jnp.sum(route_weights, axis=1, keepdims=True)
    earlier = (old_plan[None, :] == old_plan[:, None]) & (slot_index[None, :] < slot_index[:, None])
    is_first = ~jnp.any(earlier, axis=1)
    chosen = (expert_ids[:, :, None] == old_plan[None, None, :]) & is_first[None, None, :]
    weight = jnp.sum(jnp.where(chosen, share[:, :, None], 0.0), axis=1)
    high = lax.reduce_precision(weight, exponent_bits=8, mantissa_bits=7)
    half = -(-2 * slot_count // LANE) * LANE // 2
    pad = jnp.zeros((weight.shape[0], half - slot_count), jnp.bfloat16)
    return jnp.concatenate(
        [high.astype(jnp.bfloat16), pad, (weight - high).astype(jnp.bfloat16), pad], axis=1
    )


def crossing(old_plan, new_plan):
    slot_count = old_plan.shape[0]
    held = slot_count // 2
    slot_index = jnp.arange(slot_count, dtype=jnp.int32)
    same_expert = new_plan[:, None] == old_plan[None, :]
    source = jnp.min(jnp.where(same_expert, slot_index[None, :], slot_count), axis=1)
    apart = slot_index[:, None] // held != slot_index[None, :] // held
    cross = jnp.any((source[:, None] == slot_index[None, :]) & apart, axis=0)
    before = (~apart) & (slot_index[:, None] < slot_index[None, :])
    rank = jnp.sum((before & cross[:, None]).astype(jnp.int32), axis=0)
    number = jnp.max(jnp.where(cross, rank + 1, 0))
    return source, cross, rank, number


def exchange(x, devices):
    half = devices // 2
    return swap(x, "exp", [list(range(half)), list(range(half, devices))])


def places(plan, held, most):
    source, cross, rank = plan
    mine = lax.axis_index("exp") * 2 // lax.axis_size("exp")
    local = jnp.arange(held, dtype=jnp.int32)
    leaving = lax.dynamic_slice_in_dim(cross, mine * held, held)
    ranking = lax.dynamic_slice_in_dim(rank, mine * held, held)
    place = jnp.arange(most, dtype=jnp.int32)
    matches = leaving[None, :] & (ranking[None, :] == place[:, None])
    sent_index = jnp.sum(jnp.where(matches, local[None, :], 0), axis=1)
    wanted = lax.dynamic_slice_in_dim(source, mine * held, held)
    here = wanted // held == mine
    far = jnp.arange(source.shape[0], dtype=jnp.int32)[None, :] == wanted[:, None]
    far_rank = jnp.sum(jnp.where(far, rank[None, :], 0), axis=1)
    return sent_index, jnp.where(here, wanted - mine * held, held + far_rank)


def on_device(
    tokens, w_in, w_out, moments_in, moments_out, expert_ids, route_weights, old_plan, new_plan
):
    devices = lax.axis_size("exp")
    half = devices // 2
    slots = w_in.shape[0]
    held = half * slots
    chunk_a, chunk_b = (w_in, w_out, moments_out), (moments_in,)
    full_in = lax.all_gather(w_in, "grp", axis=1, tiled=True)
    full_out = lax.all_gather(w_out, "grp", axis=1, tiled=True)

    inner = plane_size(devices)
    outer = range(0, devices, inner)
    column = [flip(tokens, "exp", i) for i in outer]
    shares = {0: slot_shares(expert_ids, route_weights, old_plan)}
    bits = inner
    while bits < devices:
        got = flip(jnp.stack(list(shares.values())), "exp", bits)
        shares.update({at + bits: got[n] for n, at in enumerate(list(shares))})
        bits *= 2
    shares = [shares[i] for i in outer]
    packed_a, column, shares = lax.optimization_barrier((pack(chunk_a, half), column, shares))
    spread_a = exchange(packed_a, devices).reshape((held,) + packed_a.shape[2:])
    rows = [lay(column), lay(shares)]

    *plan, number = crossing(old_plan, new_plan)
    most = -(-held * FIXED // 16)
    sent_index, index = places(plan, held, held)
    across = [(d, (d + half) % devices) for d in range(devices)]

    sent_a = pick(sent_index[:most], spread_a)
    arrived_a = lax.ppermute(sent_a, "exp", across)
    packed_b = pack(chunk_b, half)
    spread_b = exchange(packed_b, devices).reshape((held,) + packed_b.shape[2:])
    sent_b = pick(sent_index[:most], spread_b)
    steps = range(0, inner, 2)
    blocks = [[flip(x, "exp", i) for x in rows] for i in steps]
    blocks[1:], full_out = lax.optimization_barrier((blocks[1:], full_out))
    weights = [full_in, full_out, flip(full_in, "exp", 1), flip(full_out, "exp", 1)]
    me = lax.axis_index("exp").astype(jnp.int32)
    first = jnp.stack([me, me ^ 1]) * slots
    blocks[1:], sent_b = lax.optimization_barrier((blocks[1:], sent_b))
    parts = [experts(*x, first, weights) for x in blocks]

    def more(state):
        place, *extra = state
        at = lax.dynamic_index_in_dim(sent_index, place, keepdims=False)
        out = []
        for spread, table in zip((spread_a, spread_b), extra):
            row = lax.dynamic_slice_in_dim(spread, at, 1, axis=0)
            row = lax.ppermute(row, "exp", across)
            out.append(lax.dynamic_update_slice_in_dim(table, row, place - most, axis=0))
        return place + 1, *out

    extra = [x[: max(held - most, 1)] for x in (spread_a, spread_b)]
    arrived_a, sent_b, parts, extra = lax.optimization_barrier((arrived_a, sent_b, parts, extra))
    _, *extra = lax.while_loop(
        lambda state: state[0] < number, more, (jnp.int32(most), *extra)
    )

    arrived_b = lax.ppermute(sent_b, "exp", across)
    picked_a = pick(index, spread_a, arrived_a, extra[0])
    landed_a = exchange(picked_a.reshape(packed_a.shape), devices)
    partial = add_up([flip(x, "exp", i) for i, x in zip(steps, parts)])
    arrived_b, partial = lax.optimization_barrier((arrived_b, partial))

    picked_b = pick(index, spread_b, arrived_b, extra[1])
    (new_moments_in,) = unpack(exchange(picked_b.reshape(packed_b.shape), devices), chunk_b)
    size = tokens.shape[0]
    pieces = [partial[n * size : (n + 1) * size] for n in range(len(outer))]
    outs_a, pieces[1] = lax.optimization_barrier((unpack(landed_a, chunk_a), pieces[1]))
    new_w_in, new_w_out, new_moments_out = outs_a
    mixed = add_up([flip(x, "exp", i) for i, x in zip(outer, pieces)])
    return mixed, new_w_in, new_w_out, new_moments_in, new_moments_out


def solution(mesh):
    return jax.shard_map(
        on_device,
        mesh=mesh,
        in_specs=(
            P(("grp", "exp"), None),
            P("exp", "grp", None),
            P("exp", "grp", None),
            P("exp", None, "grp", None),
            P("exp", None, "grp", None),
            P(("grp", "exp"), None),
            P(("grp", "exp"), None),
            P(),
            P(),
        ),
        out_specs=(
            P(("grp", "exp"), None),
            P("exp", "grp", None),
            P("exp", "grp", None),
            P("exp", None, "grp", None),
            P("exp", None, "grp", None),
        ),
        check_vma=False,
    )
```
